128 devices in a mesh: gx: 4 (over z), gy: 8 (over y, core), gz: 4 (over x).
Axes of the slice: x: 4, y: 4, z: 4, core: 2. Of those that a mesh axis runs over, the one named last changes fastest.
Arguments:
- atom_charge: float32 [4, 8, 4, 2048], P('gx', 'gy', 'gz'), may hold values from -6 to 6
- atom_fraction: float32 [3, 4, 8, 4, 2048], P(None, 'gx', 'gy', 'gz'), may hold values from 0 to 1
- atom_corner: int32 [3, 4, 8, 4, 2048], P(None, 'gx', 'gy', 'gz'), may hold values from 0 to 254, as said below
- block_count: int32 [4, 8, 4, 4], P('gx', 'gy', 'gz'), may hold values from 128 to 512, as said below
- permittivity: float32 [256, 512, 1024], P('gx', 'gy', 'gz'), may hold values from 0.1 to 2
- base_potential: float32 [256, 512, 1024], P('gx', 'gy', 'gz'), may hold values from -4 to 4
- ion_access: float32 [256, 512, 1024], P('gx', 'gy', 'gz'), may hold values from 0.05 to 0.5
Outputs:
- solution_field: float32 [256, 512, 1024], P('gx', 'gy', 'gz')
- atom_sensitivity: float32 [4, 8, 4, 2048], P('gx', 'gy', 'gz')
The draws below stay inside these ranges and needn't reach their ends.
Inputs may be any that keep to these rules, and one draw needn't show every extreme that they name: `atom_corner`: coordinate k of every corner is at most the slab's cell count along k minus 2, so that all eight B-spline cells lie in the destination slab. `block_count`: every block holds 128 or more live atoms; the devices with first and second index 0 send full blocks of 512 to the slab of third index 0 from every owner along the third axis.
All inputs are finite; a program needn't handle non-finite values.
Results may differ from the reference program's by a relative error of at most 0.00016.
Values sent between devices are 32-bit elements; how exact they have to be, the bound alone decides.
A program may use at most 192 MiB of HBM per device.

```python
import math
import jax
import jax.numpy as jnp

CX = 64
CY = 64
CZ = 256
CAP = 512
ITERS = 3
NX = 256
NY = 512
NZ = 1024
N_GX = 4
N_GY = 8
N_GZ = 4


def draw_atom_corner(key, part):
    key = jax.random.fold_in(key, 11)
    key_x, key_y, key_z = jax.random.split(key, 3)
    shape = (1, N_GX, N_GY, N_GZ, N_GZ * CAP)
    coord_x = jax.random.randint(key_x, shape, 0, CX - 1, dtype=jnp.int32)
    coord_y = jax.random.randint(key_y, shape, 0, CY - 1, dtype=jnp.int32)
    coord_z = jax.random.randint(key_z, shape, 0, CZ - 1, dtype=jnp.int32)
    return jnp.concatenate([coord_x, coord_y, coord_z], axis=0)


def draw_block_count(key, part):
    key = jax.random.fold_in(key, 23)
    counts = jax.random.randint(key, (N_GX, N_GY, N_GZ, N_GZ), CAP // 4, CAP + 1, dtype=jnp.int32)
    return counts.at[0, 0, :, 0].set(CAP)


def levels(key, dims, pieces, low, high):
    loudness, own = 1.0, jax.random.fold_in(key, 6)
    for dim, parts in pieces:
        steps = jnp.exp(jax.random.uniform(jax.random.fold_in(own, dim), (parts,), jnp.float32, low / len(pieces), high / len(pieces)))
        loudness = loudness * jnp.repeat(steps, dims[dim] // parts).reshape([-1 if axis == dim else 1 for axis in range(len(dims))])
    return loudness


def bell_draw(key, extent, width, reach, pieces=(), kind=jnp.bfloat16):
    array = jax.random.normal(key, extent, jnp.float32) * width
    if len(pieces) > 0:
        array = levels(key, extent, pieces, -0.22, 0.18) * array
    return jnp.clip(array, min=-reach, max=reach).astype(kind)


def setup_inputs(seed: int = 0) -> dict:
    key_list = jax.random.split(jax.random.key(seed), 8)
    atom_charge = bell_draw(key_list[0], (N_GX, N_GY, N_GZ, N_GZ * CAP), 1.0, 6.0, ((0, 4), (1, 8), (2, 4)), jnp.float32)
    atom_fraction = jnp.clip(1.0 * jax.random.uniform(key_list[1], (3, N_GX, N_GY, N_GZ, N_GZ * CAP), jnp.float32) ** levels(key_list[1], (3, N_GX, N_GY, N_GZ, N_GZ * CAP), ((1, 4), (2, 8), (3, 4)), -0.2, 0.2), 0.0, 1.0)
    atom_corner = draw_atom_corner(jax.random.fold_in(key_list[7], 71), 0)
    block_count = draw_block_count(jax.random.fold_in(key_list[7], 71), 0)
    permittivity = jnp.clip(jnp.exp(math.log(2.0) - 2.9957323 * jax.random.uniform(key_list[4], (NX, NY, NZ), jnp.float32) ** levels(key_list[4], (NX, NY, NZ), ((0, 4), (1, 8), (2, 4)), -0.2, 0.2)), 0.1, 2.0)
    base_potential = bell_draw(key_list[5], (NX, NY, NZ), 1.0, 4.0, ((0, 4), (1, 8), (2, 4)), jnp.float32)
    ion_access = jnp.clip(jnp.exp(math.log(0.5) - 2.3025851 * jax.random.uniform(key_list[6], (NX, NY, NZ), jnp.float32) ** levels(key_list[6], (NX, NY, NZ), ((0, 4), (1, 8), (2, 4)), -0.2, 0.2)), 0.05, 0.5)
    return {"atom_charge": atom_charge, "atom_fraction": atom_fraction, "atom_corner": atom_corner, "block_count": block_count, "permittivity": permittivity, "base_potential": base_potential, "ion_access": ion_access}


def harmonic(former, latter):
    return 2.0 * former * latter / (former + latter)


def neighbour_views(padded):
    return [padded[2:, 1:-1, 1:-1], padded[:-2, 1:-1, 1:-1], padded[1:-1, 2:, 1:-1],
            padded[1:-1, :-2, 1:-1], padded[1:-1, 1:-1, 2:], padded[1:-1, 1:-1, :-2]]


def ordered_total(items):
    result = items[0]
    for item in items[1:]:
        result = result + item
    return result


def face_terms(padded_eps):
    center = padded_eps[1:-1, 1:-1, 1:-1]
    return [harmonic(center, other) for other in neighbour_views(padded_eps)]


def operate(field, padded_eps, diagonal):
    faces = face_terms(padded_eps)
    views = neighbour_views(jnp.pad(field, 1))
    return diagonal * field - ordered_total([face * view for face, view in zip(faces, views)])


def atom_terms(atom_corner, atom_fraction, block_count):
    slots = N_GZ * CAP
    slot_ids = jnp.arange(slots, dtype=jnp.int32)
    within = (slot_ids % CAP).reshape(1, 1, 1, slots)
    target = (slot_ids // CAP).reshape(1, 1, 1, slots)
    live = within < jnp.repeat(block_count, CAP, axis=3)
    owner_x = jnp.arange(N_GX, dtype=jnp.int32).reshape(N_GX, 1, 1, 1)
    owner_y = jnp.arange(N_GY, dtype=jnp.int32).reshape(1, N_GY, 1, 1)
    coord_x = owner_x * CX + atom_corner[0]
    coord_y = owner_y * CY + atom_corner[1]
    coord_z = target * CZ + atom_corner[2]
    base_cell = ((coord_x * NY + coord_y) * NZ + coord_z).astype(jnp.int32)
    indices = []
    weights = []
    for shift_x in (0, 1):
        for shift_y in (0, 1):
            for shift_z in (0, 1):
                offset = shift_x * NY * NZ + shift_y * NZ + shift_z
                weight_x = atom_fraction[0] if shift_x else 1.0 - atom_fraction[0]
                weight_y = atom_fraction[1] if shift_y else 1.0 - atom_fraction[1]
                weight_z = atom_fraction[2] if shift_z else 1.0 - atom_fraction[2]
                indices.append((base_cell + offset).astype(jnp.int32))
                weights.append(weight_x * weight_y * weight_z)
    return jnp.stack(indices), jnp.stack(weights), live


def reference(atom_charge, atom_fraction, atom_corner, block_count, permittivity, base_potential, ion_access):
    cell_index, cell_weight, live = atom_terms(atom_corner, atom_fraction, block_count)
    charge = jnp.where(live, atom_charge, jnp.zeros_like(atom_charge))
    sources = jnp.zeros((NX * NY * NZ,), jnp.float32).astype(atom_charge.dtype)
    sources = sources.at[cell_index.reshape(-1)].add((cell_weight * charge[None]).reshape(-1))
    sources = sources.reshape(NX, NY, NZ)
    padded_eps = jnp.pad(permittivity, 1)
    diagonal = ordered_total(face_terms(padded_eps)) + ion_access * jnp.cosh(base_potential)
    solution_field = jnp.zeros_like(sources)
    residual = sources
    precond = residual / diagonal
    direction = precond
    product_now = jnp.sum(residual * precond)
    for iteration in range(ITERS):
        image = operate(direction, padded_eps, diagonal)
        alpha = product_now / jnp.sum(direction * image)
        solution_field = solution_field + alpha * direction
        residual = residual - alpha * image
        if iteration + 1 < ITERS:
            precond = residual / diagonal
            product_next = jnp.sum(residual * precond)
            direction = precond + (product_next / product_now) * direction
            product_now = product_next
    flat_field = solution_field.reshape(-1)
    sampled = jnp.sum(cell_weight * flat_field[cell_index], axis=0)
    atom_sensitivity = jnp.where(live, sampled, jnp.zeros_like(sampled))
    return solution_field, atom_sensitivity
```

```python
import functools

import jax
import jax.numpy as jnp
from jax import lax
from jax.experimental import pallas as pl
from jax.experimental.pallas import tpu as pltpu
from jax.sharding import PartitionSpec as P

F = jnp.float32
AXES = ("gx", "gy", "gz")
MESH = pl.DeviceIdType.MESH
LANES = 128
PAD = 8
CHUNK = 16
SLOTS_PER_STEP = 16
TABLES = 2


def patterns():
    row = lax.broadcasted_iota(jnp.int32, (8, LANES), 0)
    lane = lax.broadcasted_iota(jnp.int32, (8, LANES), 1)
    return row, ((row % 2) * LANES + lane).astype(F)


def z_hat(pos, cz, fz):
    return jnp.maximum(1.0 - jnp.abs((pos - cz) - fz), 0.0)


def spread_kernel(slots, span_y, q_ref, f_ref, c_ref, out_ref, *scratch):
    tables, sem = scratch[:TABLES], scratch[TABLES]
    rows = out_ref.shape[0]
    block = 64

    def clear(i, _):
        for table in tables:
            table[pl.ds(pl.multiple_of(i * block, block), block), :] = jnp.zeros((block, LANES), F)
        return 0

    lax.fori_loop(0, rows // block, clear, 0)
    for table in tables:
        table[pl.ds(rows, 8), :] = jnp.zeros((8, LANES), F)
    row, pos = patterns()
    ya = jnp.where(row < 2, 1.0, 0.0).astype(F)
    yb = jnp.where(row < 2, -1.0, jnp.where(row < 4, 1.0, 0.0)).astype(F)
    plane = 2 * span_y

    def body(i, _):
        for first in range(0, SLOTS_PER_STEP, TABLES):
            items = []
            for which, table in enumerate(tables):
                s = i * SLOTS_PER_STEP + first + which
                r = pl.multiple_of((c_ref[s] * span_y + c_ref[slots + s]) * 2, 2)
                cz = c_ref[2 * slots + s].astype(F)
                fx, fy, fz = f_ref[s], f_ref[slots + s], f_ref[2 * slots + s]
                q = q_ref[s]
                w = (ya + yb * fy) * z_hat(pos, cz, fz)
                near = table[pl.ds(r, 8), :] + w * (q * (1.0 - fx))
                far = table[pl.ds(r + plane, 8), :] + w * (q * fx)
                items.append((table, r, near, far))
            for table, r, near, far in items:
                table[pl.ds(r, 8), :] = near
                table[pl.ds(r + plane, 8), :] = far
        return 0

    lax.fori_loop(0, slots // SLOTS_PER_STEP, body, 0)

    def combine(i, _):
        part = pl.ds(pl.multiple_of(i * block, block), block)
        total = tables[0][part, :]
        for table in tables[1:]:
            total = total + table[part, :]
        tables[0][part, :] = total
        return 0

    lax.fori_loop(0, rows // block, combine, 0)
    copy = pltpu.make_async_copy(tables[0].at[pl.ds(0, rows), :], out_ref, sem)
    copy.start()
    copy.wait()


def spread(charge, fraction, corner, span):
    slots = charge.shape[0]
    rows = span[0] * span[1] * 2
    return pl.pallas_call(
        functools.partial(spread_kernel, slots, span[1]),
        out_shape=jax.ShapeDtypeStruct((rows, LANES), F),
        in_specs=[pl.BlockSpec(memory_space=pltpu.SMEM)] * 3,
        out_specs=pl.BlockSpec(memory_space=pl.ANY),
        scratch_shapes=[pltpu.VMEM((rows + 8, LANES), F)] * TABLES + [pltpu.SemaphoreType.DMA(())],
        compiler_params=pltpu.CompilerParams(vmem_limit_bytes=56 << 20),
        name="spread",
    )(charge, fraction, corner)


def sample_kernel(
    slots, span_y, f_ref, c_ref, rows_ref, grid_ref, field_ref, out_ref, table, grid, parts, sums, sems
):
    rows = rows_ref.shape[0]
    load = pltpu.make_async_copy(rows_ref, table.at[pl.ds(8, rows), :], sems.at[1])
    load.start()
    hold = pltpu.make_async_copy(grid_ref, grid, sems.at[0])
    hold.start()
    table[pl.ds(0, 8), :] = jnp.zeros((8, LANES), F)
    table[pl.ds(rows + 8, 8), :] = jnp.zeros((8, LANES), F)
    load.wait()
    hold.wait()
    keep = pltpu.make_async_copy(grid, field_ref, sems.at[2])
    keep.start()
    row, pos = patterns()
    first_row, second_row = row % 4 < 2, row < 4
    yb = jnp.where(first_row, -1.0, 1.0).astype(F)
    ya = jnp.where(first_row, 1.0, 0.0).astype(F)
    masks = [jnp.where(second_row, 1.0, 0.0).astype(F), jnp.where(second_row, 0.0, 1.0).astype(F)]
    plane = 2 * span_y

    def body(i, _):
        for pair in range(SLOTS_PER_STEP // 2):
            total = None
            for which in (0, 1):
                s = i * SLOTS_PER_STEP + 2 * pair + which
                r = pl.multiple_of((c_ref[s] * span_y + c_ref[slots + s]) * 2, 2)
                r = r + (8 - 4 * which)
                cz = c_ref[2 * slots + s].astype(F)
                fx, fy, fz = f_ref[s], f_ref[slots + s], f_ref[2 * slots + s]
                w = (ya * masks[which] + (yb * masks[which]) * fy) * z_hat(pos, cz, fz)
                near, far = table[pl.ds(r, 8), :], table[pl.ds(r + plane, 8), :]
                term = w * (near * (1.0 - fx) + far * fx)
                total = term if total is None else total + term
            start = pl.multiple_of((i * (SLOTS_PER_STEP // 2) + pair) * 8, 8)
            parts[pl.ds(start, 8), :] = total
        return 0

    lax.fori_loop(0, slots // SLOTS_PER_STEP, body, 0)

    def fold(i, _):
        start = pl.multiple_of(i * 256, 256)
        total = parts[pl.ds(start, 64, stride=4), :]
        for j in range(1, 4):
            total = total + parts[pl.ds(start + j, 64, stride=4), :]
        sums[pl.ds(pl.multiple_of(i * 64, 64), 64), :] = total
        return 0

    lax.fori_loop(0, slots // 64, fold, 0)
    out_ref[...] = lax.dot_general(
        jnp.ones((8, LANES), F),
        sums[...],
        (((1,), (1,)), ((), ())),
        precision=lax.Precision.HIGHEST,
        preferred_element_type=F,
    )
    keep.wait()


def sample(fraction, corner, rows_field, grid_field):
    slots = fraction.shape[0] // 3
    span_x, span_y, span_z = grid_field.shape
    rows = rows_field.shape[0]
    smem, anywhere = pl.BlockSpec(memory_space=pltpu.SMEM), pl.BlockSpec(memory_space=pl.ANY)
    return pl.pallas_call(
        functools.partial(sample_kernel, slots, span_y),
        out_shape=(
            jax.ShapeDtypeStruct(grid_field.shape, F),
            jax.ShapeDtypeStruct((8, slots), F),
        ),
        in_specs=[smem, smem, anywhere, anywhere],
        out_specs=(anywhere, pl.BlockSpec(memory_space=pltpu.VMEM)),
        scratch_shapes=[
            pltpu.VMEM((rows + 16, LANES), F),
            pltpu.VMEM(grid_field.shape, F),
            pltpu.VMEM((slots * 4, LANES), F),
            pltpu.VMEM((slots, LANES), F),
            pltpu.SemaphoreType.DMA((3,)),
        ],
        compiler_params=pltpu.CompilerParams(vmem_limit_bytes=56 << 20),
        name="sample",
    )(fraction, corner, rows_field, grid_field)


def harmonic(former, latter):
    return 2.0 * former * latter / (former + latter)


def krylov_kernel(
    sizes,
    b_ref, eps_ref, pot_ref, ion_ref,
    out_ref, rows_ref,
    e, fx, fy, fz, rd, v0, v1, v2, b, pot, ion,
    y_send, y_recv, z_send, z_recv, zf, red, sem_in, send_sem, recv_sem, red_send, red_recv, sem_out,
):
    span_x, span_y, _ = eps_ref.shape
    places = [lax.axis_index(axis) for axis in AXES]
    lane = lax.broadcasted_iota(jnp.int32, (CHUNK, LANES), 1)
    edge = (lane == 0) | (lane == LANES - 1)
    chunks = range(0, span_y, CHUNK)
    body_rows = pl.ds(PAD, span_y)
    vs = (v0, v1, v2)

    loads = []
    for half in (0, 1):
        lanes = pl.ds(half * LANES, LANES)
        for n, (src, dst) in enumerate(
            (
                (eps_ref.at[:, :, lanes], e.at[pl.ds(1, span_x), half, body_rows, :]),
                (pot_ref.at[:, :, lanes], pot.at[:, half]),
                (ion_ref.at[:, :, lanes], ion.at[:, half]),
            )
        ):
            loads.append(pltpu.make_async_copy(src, dst, sem_in.at[2 * n + half]))
    loads.append(pltpu.make_async_copy(b_ref, b, sem_in.at[6]))
    for load in loads:
        load.start()

    zero = jnp.zeros((span_y, LANES), F)
    for field in (e, v0, v1, v2):
        for half in (0, 1):
            for x in (0, span_x + 1):
                field[x, half, body_rows, :] = zero
    for k in range(4):
        for side in (0, 1):
            z_recv[k, side] = zero
            for half in (0, 1):
                y_recv[k, side, half] = jnp.zeros((span_x, LANES), F)

    barrier = pltpu.get_barrier_semaphore()
    for axis, place, size in zip(AXES, places, sizes):
        for step in range(1, size):
            pl.semaphore_signal(
                barrier, inc=1, device_id={axis: lax.rem(place + step, size)}, device_id_type=MESH
            )
    pl.semaphore_wait(barrier, sum(size - 1 for size in sizes))

    def halo_copies(k, field):
        pairs = []
        for n, (axis, place, size) in enumerate(zip(AXES, places, sizes)):
            if size == 1:
                continue
            for side in (0, 1):
                slot = 2 * n + side
                if n == 0:
                    src = field.at[span_x if side == 0 else 1, :, body_rows, :]
                    dst = field.at[0 if side == 0 else span_x + 1, :, body_rows, :]
                elif n == 1:
                    src, dst = y_send.at[k, side], y_recv.at[k, side]
                else:
                    src, dst = z_send.at[k], z_recv.at[k, side]
                copy = pltpu.make_async_remote_copy(
                    src_ref=src,
                    dst_ref=dst,
                    send_sem=send_sem.at[k, slot],
                    recv_sem=recv_sem.at[k, slot],
                    device_id={axis: place + 1 if side == 0 else place - 1},
                    device_id_type=MESH,
                )
                above, below = place < size - 1, place > 0
                pairs.append((above if side == 0 else below, below if side == 0 else above, copy))
        return pairs

    def send(k, field):
        for has_target, _, copy in halo_copies(k, field):
            pl.when(has_target)(copy.start)

    def receive(k, field):
        for _, has_source, copy in halo_copies(k, field):
            pl.when(has_source)(copy.wait_recv)

    def sent(k, field):
        for has_target, _, copy in halo_copies(k, field):
            pl.when(has_target)(copy.wait_send)

    def pack_y(k, field, x):
        for half in (0, 1):
            y_send[k, 1, half, pl.ds(x, 1), :] = field[x + 1, half, pl.ds(PAD, 1), :]
            y_send[k, 0, half, pl.ds(x, 1), :] = field[x + 1, half, pl.ds(PAD + span_y - 1, 1), :]

    def unpack_y(k, field, x):
        for half in (0, 1):
            field[x + 1, half, pl.ds(PAD - 1, 1), :] = y_recv[k, 0, half, pl.ds(x, 1), :]
            field[x + 1, half, pl.ds(PAD + span_y, 1), :] = y_recv[k, 1, half, pl.ds(x, 1), :]

    def pack_z(acc, low, high, x):
        both = pltpu.roll(jnp.where(lane == 0, low, high), 2 * x, 1)
        return jnp.where((lane == 2 * x) | (lane == lax.rem(2 * x + LANES - 1, LANES)), both, acc)

    def open_z(packed, x):
        return pltpu.roll(packed, LANES - 1 - 2 * x, 1)

    empty = tuple(jnp.zeros((CHUNK, LANES), F) for _ in chunks)

    loads[0].wait()
    loads[3].wait()

    def pack_e(x, accs):
        pack_y(0, e, x)
        out = []
        for t, acc in zip(chunks, accs):
            rows = pl.ds(PAD + t, CHUNK)
            out.append(pack_z(acc, e[x + 1, 0, rows, :], e[x + 1, 1, rows, :], x))
        return tuple(out)

    accs = lax.fori_loop(0, span_x, pack_e, empty)
    for t, acc in zip(chunks, accs):
        z_send[0, pl.ds(t, CHUNK), :] = acc
    send(0, e)

    for n in (1, 4, 2, 5):
        loads[n].wait()

    def screen(x, _):
        for half in (0, 1):
            for t in chunks:
                rows = pl.ds(t, CHUNK)
                up = jnp.exp(pot[x, half, rows, :])
                rd[x, half, rows, :] = ion[x, half, rows, :] * (0.5 * (up + 1.0 / up))
        return 0

    lax.fori_loop(0, span_x, screen, 0)
    receive(0, e)

    odd = lane % 2 == 1
    for t in chunks:
        rows = pl.ds(t, CHUNK)
        own = z_send[0, rows, :]
        low = harmonic(z_recv[0, 0, rows, :], pltpu.roll(own, LANES - 1, 1))
        high = harmonic(z_recv[0, 1, rows, :], pltpu.roll(own, 1, 1))
        zf[0, rows, :] = jnp.where(odd, low, 0.0)
        zf[1, rows, :] = jnp.where(odd, 0.0, high)
        zf[2, rows, :] = pltpu.roll(zf[0, rows, :], 2, 1) + zf[1, rows, :]

    for half in (0, 1):
        for t in chunks:
            rows = pl.ds(PAD + t, CHUNK)
            fx[0, half, pl.ds(t, CHUNK), :] = harmonic(e[0, half, rows, :], e[1, half, rows, :])

    loads[6].wait()

    def faces(x, carry):
        accs, total = carry
        unpack_y(0, e, x)
        for half in (0, 1):
            fy[x, half, pl.ds(PAD - 1, 1), :] = harmonic(
                e[x + 1, half, pl.ds(PAD - 1, 1), :], e[x + 1, half, pl.ds(PAD, 1), :]
            )
        out = []
        for t, acc in zip(chunks, accs):
            rows, wide = pl.ds(t, CHUNK), pl.ds(PAD + t, CHUNK)
            center = [e[x + 1, half, wide, :] for half in (0, 1)]
            turned = [pltpu.roll(c, LANES - 1, 1) for c in center]
            z_next = [jnp.where(lane == LANES - 1, turned[1], turned[0]), turned[1]]
            z_face = [harmonic(c, n) for c, n in zip(center, z_next)]
            z_face[1] = jnp.where(lane == LANES - 1, 0.0, z_face[1])
            back = [pltpu.roll(f, 1, 1) for f in z_face]
            outer = open_z(zf[2, rows, :], x)
            z_both = [
                z_face[0] + jnp.where(lane == 0, outer, back[0]),
                z_face[1] + jnp.where(lane == 0, back[0], back[1])
                + jnp.where(lane == LANES - 1, outer, 0.0),
            ]
            fields = []
            for half in (0, 1):
                c = center[half]
                x_face = harmonic(c, e[x + 2, half, wide, :])
                fx[x + 1, half, rows, :] = x_face
                y_face = harmonic(c, e[x + 1, half, pl.ds(PAD + t + 1, CHUNK), :])
                fy[x, half, wide, :] = y_face
                fz[x, half, rows, :] = z_face[half]
                diagonal = (
                    x_face + fx[x, half, rows, :]
                    + y_face + fy[x, half, pl.ds(PAD + t - 1, CHUNK), :]
                    + z_both[half] + rd[x, half, rows, :]
                )
                inverse = 1.0 / diagonal
                rd[x, half, rows, :] = inverse
                source = b[pl.ds(x * (2 * span_y) + 2 * t + half, CHUNK, stride=2), :]
                value = source * inverse
                v0[x + 1, half, wide, :] = value
                total = total + source * value
                fields.append(value)
            out.append(pack_z(acc, fields[0], fields[1], x))
        pack_y(1, v0, x)
        return tuple(out), total

    nothing = jnp.zeros((CHUNK, LANES), F)
    accs, total = lax.fori_loop(0, span_x, faces, (empty, nothing))
    moments = [total]

    for k in range(3):
        v = vs[k]
        last = k == 2
        for t, acc in zip(chunks, accs):
            z_send[k + 1, pl.ds(t, CHUNK), :] = acc
        send(k + 1, v)
        receive(k + 1, v)
        for t in chunks:
            rows = pl.ds(t, CHUNK)
            zf[2, rows, :] = (
                pltpu.roll(zf[0, rows, :] * z_recv[k + 1, 0, rows, :], 2, 1)
                + zf[1, rows, :] * z_recv[k + 1, 1, rows, :]
            )

        def apply(x, carry, v=v, k=k, last=last):
            accs, first, second = carry
            unpack_y(k + 1, v, x)
            out = []
            for t, acc in zip(chunks, accs):
                rows, wide = pl.ds(t, CHUNK), pl.ds(PAD + t, CHUNK)
                up, down = pl.ds(PAD + t + 1, CHUNK), pl.ds(PAD + t - 1, CHUNK)
                center = [v[x + 1, half, wide, :] for half in (0, 1)]
                turned = [pltpu.roll(c, LANES - 1, 1) for c in center]
                z_next = [jnp.where(lane == LANES - 1, turned[1], turned[0]), turned[1]]
                z_face = [fz[x, half, rows, :] for half in (0, 1)]
                back = [pltpu.roll(f * c, 1, 1) for f, c in zip(z_face, center)]
                outer = open_z(zf[2, rows, :], x)
                z_both = [
                    z_face[0] * z_next[0] + jnp.where(lane == 0, outer, back[0]),
                    z_face[1] * z_next[1] + jnp.where(lane == 0, back[0], back[1])
                    + jnp.where(lane == LANES - 1, outer, 0.0),
                ]
                fields = []
                for half in (0, 1):
                    image = (
                        fx[x + 1, half, rows, :] * v[x + 2, half, wide, :]
                        + fx[x, half, rows, :] * v[x, half, wide, :]
                        + fy[x, half, wide, :] * v[x + 1, half, up, :]
                        + fy[x, half, down, :] * v[x + 1, half, down, :]
                        + z_both[half]
                    )
                    first = first + center[half] * image
                    if not last:
                        value = image * rd[x, half, rows, :]
                        vs[k + 1][x + 1, half, wide, :] = value
                        second = second + image * value
                        fields.append(value)
                out.append(acc if last else pack_z(acc, fields[0], fields[1], x))
            if not last:
                pack_y(k + 2, vs[k + 1], x)
            return tuple(out), first, second

        accs, first, second = lax.fori_loop(0, span_x, apply, (empty, nothing, nothing))
        moments.append(first)
        if not last:
            moments.append(second)

    row = lax.broadcasted_iota(jnp.int32, (8, LANES), 0)
    mine = jnp.zeros((8, LANES), F)
    for n, moment in enumerate(moments):
        folded = jnp.sum(moment, axis=0, keepdims=True)
        mine = mine + jnp.where(row == n, folded, 0.0)
    for n, (axis, place, size) in enumerate(zip(AXES, places, sizes)):
        red[n, place] = mine
        copies = []
        for step in range(1, size):
            target = lax.rem(place + step, size)
            copy = pltpu.make_async_remote_copy(
                src_ref=red.at[n, place],
                dst_ref=red.at[n, place],
                send_sem=red_send.at[n, step],
                recv_sem=red_recv.at[n, step],
                device_id={axis: target},
                device_id_type=MESH,
            )
            copy.start()
            copies.append(copy)
        for step in range(1, size):
            source = lax.rem(place + size - step, size)
            pltpu.make_async_remote_copy(
                src_ref=red.at[n, place],
                dst_ref=red.at[n, source],
                send_sem=red_send.at[n, step],
                recv_sem=red_recv.at[n, step],
                device_id={axis: source},
                device_id_type=MESH,
            ).wait_recv()
        for copy in copies:
            copy.wait_send()
        mine = red[n, 0]
        for other in range(1, size):
            mine = mine + red[n, other]
    totals = jnp.sum(mine, axis=1, keepdims=True)
    m = [totals[n:n + 1] for n in range(6)]
    m = [value / m[0] for value in m]

    h = [m[n] - m[n + 1] for n in range(5)]
    l1, l2 = h[1] / h[0], h[2] / h[0]
    d1 = h[2] - l1 * h[1]
    o1 = h[3] - l1 * h[2]
    l3 = o1 / d1
    d2 = h[4] - l2 * h[2] - l3 * o1
    r1 = m[1] - l1 * m[0]
    r2 = m[2] - l2 * m[0] - l3 * r1
    c2 = r2 / d2
    c1 = r1 / d1 - l3 * c2
    c0 = m[0] / h[0] - l1 * c1 - l2 * c2

    weights = [jnp.broadcast_to(c, (CHUNK, LANES)) for c in (c0, c1, c2)]

    def finish(x, _):
        for half in (0, 1):
            for t in chunks:
                wide = pl.ds(PAD + t, CHUNK)
                value = weights[0] * v0[x + 1, half, wide, :]
                value = value + weights[1] * v1[x + 1, half, wide, :]
                value = value + weights[2] * v2[x + 1, half, wide, :]
                pot[x, half, pl.ds(t, CHUNK), :] = value
                b[pl.ds(x * (2 * span_y) + 2 * t + half, CHUNK, stride=2), :] = value
        return 0

    lax.fori_loop(0, span_x, finish, 0)
    stores = [
        pltpu.make_async_copy(
            pot.at[:, half], out_ref.at[:, :, pl.ds(half * LANES, LANES)], sem_out.at[half]
        )
        for half in (0, 1)
    ]
    stores.append(pltpu.make_async_copy(b, rows_ref, sem_out.at[2]))
    for store in stores:
        store.start()
    for k, field in enumerate((e, v0, v1, v2)):
        sent(k, field)
    for store in stores:
        store.wait()


def krylov(sizes, b, eps, pot, ion):
    span_x, span_y, span_z = eps.shape
    tall = span_y + 2 * PAD
    padded = pltpu.VMEM((span_x + 2, 2, tall, LANES), F)
    plain = pltpu.VMEM((span_x, 2, span_y, LANES), F)
    dma = pltpu.SemaphoreType.DMA
    anywhere = pl.BlockSpec(memory_space=pl.ANY)
    most = max(sizes)
    return pl.pallas_call(
        functools.partial(krylov_kernel, sizes),
        out_shape=(
            jax.ShapeDtypeStruct(eps.shape, F),
            jax.ShapeDtypeStruct(b.shape, F),
        ),
        in_specs=[anywhere] * 4,
        out_specs=(anywhere, anywhere),
        scratch_shapes=[
            padded,
            pltpu.VMEM((span_x + 1, 2, span_y, LANES), F),
            pltpu.VMEM((span_x, 2, tall, LANES), F),
            plain,
            plain,
            padded, padded, padded,
            pltpu.VMEM(b.shape, F),
            plain,
            plain,
            pltpu.VMEM((4, 2, 2, span_x, LANES), F),
            pltpu.VMEM((4, 2, 2, span_x, LANES), F),
            pltpu.VMEM((4, span_y, LANES), F),
            pltpu.VMEM((4, 2, span_y, LANES), F),
            pltpu.VMEM((3, span_y, LANES), F),
            pltpu.VMEM((3, most, 8, LANES), F),
            dma((7,)),
            dma((4, 6)),
            dma((4, 6)),
            dma((3, most)),
            dma((3, most)),
            dma((3,)),
        ],
        compiler_params=pltpu.CompilerParams(
            vmem_limit_bytes=60 << 20, collective_id=0, has_side_effects=True
        ),
        name="krylov",
    )(b, eps, pot, ion)


def per_device(
    atom_charge, atom_fraction, atom_corner, block_count, permittivity, base_potential, ion_access
):
    sizes = tuple(lax.axis_size(axis) for axis in AXES)
    groups = sizes[2]
    capacity = atom_charge.shape[3] // groups
    live = jnp.arange(capacity, dtype=jnp.int32)[None, :] < block_count.reshape(groups, 1)
    charge = jnp.where(live, atom_charge.reshape(groups, capacity), 0.0)
    fraction = atom_fraction.reshape(3, groups, capacity)
    corner = atom_corner.reshape(3, groups, capacity)
    record = jnp.concatenate([charge[None], fraction, corner.astype(F)], axis=0)
    arrived = lax.all_to_all(record, "gz", split_axis=1, concat_axis=1, tiled=True)
    there_charge = arrived[0].reshape(-1)
    there_fraction = arrived[1:4].reshape(-1)
    there_corner = arrived[4:7].astype(jnp.int32).reshape(-1)
    sources = spread(there_charge, there_fraction, there_corner, permittivity.shape)
    grid_field, rows_field = krylov(sizes, sources, permittivity, base_potential, ion_access)
    solution_field, sampled = sample(there_fraction, there_corner, rows_field, grid_field)
    returned = lax.all_to_all(
        sampled[0].reshape(groups, capacity), "gz", split_axis=0, concat_axis=0, tiled=True
    )
    atom_sensitivity = jnp.where(live, returned, 0.0).reshape(1, 1, 1, groups * capacity)
    return (solution_field, atom_sensitivity)


def solution(mesh):
    in_specs = (
        P("gx", "gy", "gz", None),
        P(None, "gx", "gy", "gz", None),
        P(None, "gx", "gy", "gz", None),
        P("gx", "gy", "gz", None),
        P("gx", "gy", "gz"),
        P("gx", "gy", "gz"),
        P("gx", "gy", "gz"),
    )
    out_specs = (P("gx", "gy", "gz"), P("gx", "gy", "gz", None))
    return jax.shard_map(
        per_device, mesh=mesh, in_specs=in_specs, out_specs=out_specs, check_vma=False
    )
```

```python
import functools

import jax
import jax.numpy as jnp
from jax import lax
from jax.experimental import pallas as pl
from jax.experimental.pallas import tpu as pltpu
from jax.sharding import PartitionSpec as P

F = jnp.float32
AXES = ("gx", "gy", "gz")
MESH = pl.DeviceIdType.MESH
LANES = 128
PAD = 8
CHUNK = 16
SLOTS_PER_STEP = 16
TABLES = 2
START = 8
UNROLL_FACES = 4
UNROLL_APPLY = 8


def patterns():
    row = lax.broadcasted_iota(jnp.int32, (8, LANES), 0)
    lane = lax.broadcasted_iota(jnp.int32, (8, LANES), 1)
    return row, ((row % 2) * LANES + lane).astype(F)


def z_hat(pos, cz, fz):
    return jnp.maximum(1.0 - jnp.abs((pos - cz) - fz), 0.0)


def spread_kernel(slots, span_y, q_ref, f_ref, c_ref, out_ref, *scratch):
    tables, sem = scratch[:TABLES], scratch[TABLES]
    rows = out_ref.shape[0]
    block = 64

    def clear(i, _):
        for table in tables:
            table[pl.ds(pl.multiple_of(i * block, block), block), :] = jnp.zeros((block, LANES), F)
        return 0

    lax.fori_loop(0, rows // block, clear, 0)
    for table in tables:
        table[pl.ds(rows, 8), :] = jnp.zeros((8, LANES), F)
    row, pos = patterns()
    ya = jnp.where(row < 2, 1.0, 0.0).astype(F)
    yb = jnp.where(row < 2, -1.0, jnp.where(row < 4, 1.0, 0.0)).astype(F)
    plane = 2 * span_y

    def body(i, _):
        for first in range(0, SLOTS_PER_STEP, TABLES):
            items = []
            for which, table in enumerate(tables):
                s = i * SLOTS_PER_STEP + first + which
                r = pl.multiple_of((c_ref[s] * span_y + c_ref[slots + s]) * 2, 2)
                cz = c_ref[2 * slots + s].astype(F)
                fx, fy, fz = f_ref[s], f_ref[slots + s], f_ref[2 * slots + s]
                q = q_ref[s]
                w = (ya + yb * fy) * z_hat(pos, cz, fz)
                near = table[pl.ds(r, 8), :] + w * (q * (1.0 - fx))
                far = table[pl.ds(r + plane, 8), :] + w * (q * fx)
                items.append((table, r, near, far))
            for table, r, near, far in items:
                table[pl.ds(r, 8), :] = near
                table[pl.ds(r + plane, 8), :] = far
        return 0

    lax.fori_loop(0, slots // SLOTS_PER_STEP, body, 0)

    def combine(i, _):
        part = pl.ds(pl.multiple_of(i * block, block), block)
        total = tables[0][part, :]
        for table in tables[1:]:
            total = total + table[part, :]
        tables[0][part, :] = total
        return 0

    lax.fori_loop(0, rows // block, combine, 0)
    copy = pltpu.make_async_copy(tables[0].at[pl.ds(0, rows), :], out_ref, sem)
    copy.start()
    copy.wait()


def spread(charge, fraction, corner, span):
    slots = charge.shape[0]
    rows = span[0] * span[1] * 2
    return pl.pallas_call(
        functools.partial(spread_kernel, slots, span[1]),
        out_shape=jax.ShapeDtypeStruct((rows, LANES), F),
        in_specs=[pl.BlockSpec(memory_space=pltpu.SMEM)] * 3,
        out_specs=pl.BlockSpec(memory_space=pl.ANY),
        scratch_shapes=[pltpu.VMEM((rows + 8, LANES), F)] * TABLES + [pltpu.SemaphoreType.DMA(())],
        compiler_params=pltpu.CompilerParams(vmem_limit_bytes=56 << 20),
        name="spread",
    )(charge, fraction, corner)


def sample_kernel(
    slots, span_y, f_ref, c_ref, rows_ref, grid_ref, field_ref, out_ref, table, grid, parts, sums, sems
):
    rows = rows_ref.shape[0]
    load = pltpu.make_async_copy(rows_ref, table.at[pl.ds(8, rows), :], sems.at[1])
    load.start()
    hold = pltpu.make_async_copy(grid_ref, grid, sems.at[0])
    hold.start()
    table[pl.ds(0, 8), :] = jnp.zeros((8, LANES), F)
    table[pl.ds(rows + 8, 8), :] = jnp.zeros((8, LANES), F)
    load.wait()
    hold.wait()
    keep = pltpu.make_async_copy(grid, field_ref, sems.at[2])
    keep.start()
    row, pos = patterns()
    first_row, second_row = row % 4 < 2, row < 4
    yb = jnp.where(first_row, -1.0, 1.0).astype(F)
    ya = jnp.where(first_row, 1.0, 0.0).astype(F)
    masks = [jnp.where(second_row, 1.0, 0.0).astype(F), jnp.where(second_row, 0.0, 1.0).astype(F)]
    plane = 2 * span_y

    def body(i, _):
        for pair in range(SLOTS_PER_STEP // 2):
            total = None
            for which in (0, 1):
                s = i * SLOTS_PER_STEP + 2 * pair + which
                r = pl.multiple_of((c_ref[s] * span_y + c_ref[slots + s]) * 2, 2)
                r = r + (8 - 4 * which)
                cz = c_ref[2 * slots + s].astype(F)
                fx, fy, fz = f_ref[s], f_ref[slots + s], f_ref[2 * slots + s]
                w = (ya * masks[which] + (yb * masks[which]) * fy) * z_hat(pos, cz, fz)
                near, far = table[pl.ds(r, 8), :], table[pl.ds(r + plane, 8), :]
                term = w * (near * (1.0 - fx) + far * fx)
                total = term if total is None else total + term
            start = pl.multiple_of((i * (SLOTS_PER_STEP // 2) + pair) * 8, 8)
            parts[pl.ds(start, 8), :] = total
        return 0

    lax.fori_loop(0, slots // SLOTS_PER_STEP, body, 0)

    def fold(i, _):
        start = pl.multiple_of(i * 256, 256)
        total = parts[pl.ds(start, 64, stride=4), :]
        for j in range(1, 4):
            total = total + parts[pl.ds(start + j, 64, stride=4), :]
        sums[pl.ds(pl.multiple_of(i * 64, 64), 64), :] = total
        return 0

    lax.fori_loop(0, slots // 64, fold, 0)
    out_ref[...] = lax.dot_general(
        jnp.ones((8, LANES), F),
        sums[...],
        (((1,), (1,)), ((), ())),
        precision=lax.Precision.HIGHEST,
        preferred_element_type=F,
    )
    keep.wait()


def sample(fraction, corner, rows_field, grid_field):
    slots = fraction.shape[0] // 3
    span_x, span_y, span_z = grid_field.shape
    rows = rows_field.shape[0]
    smem, anywhere = pl.BlockSpec(memory_space=pltpu.SMEM), pl.BlockSpec(memory_space=pl.ANY)
    return pl.pallas_call(
        functools.partial(sample_kernel, slots, span_y),
        out_shape=(
            jax.ShapeDtypeStruct(grid_field.shape, F),
            jax.ShapeDtypeStruct((8, slots), F),
        ),
        in_specs=[smem, smem, anywhere, anywhere],
        out_specs=(anywhere, pl.BlockSpec(memory_space=pltpu.VMEM)),
        scratch_shapes=[
            pltpu.VMEM((rows + 16, LANES), F),
            pltpu.VMEM(grid_field.shape, F),
            pltpu.VMEM((slots * 4, LANES), F),
            pltpu.VMEM((slots, LANES), F),
            pltpu.SemaphoreType.DMA((3,)),
        ],
        compiler_params=pltpu.CompilerParams(vmem_limit_bytes=56 << 20),
        name="sample",
    )(fraction, corner, rows_field, grid_field)


def inverse_of(value):
    guess = pl.reciprocal(value, approx=True)
    return guess * (2.0 - value * guess)


def harmonic(former, latter):
    return (2.0 * former * latter) * inverse_of(former + latter)


def krylov_kernel(
    sizes,
    b_ref, eps_ref, pot_ref, ion_ref,
    out_ref, rows_ref,
    e, fx, fy, fz, rd, v0, v1, v2, b, pot, ion,
    y_send, y_recv, z_send, z_recv, z_in, red,
    sem_in, send_sem, recv_sem, red_send, red_recv, sem_out,
):
    span_x, span_y, _ = eps_ref.shape
    places = [lax.axis_index(axis) for axis in AXES]
    lane = lax.broadcasted_iota(jnp.int32, (CHUNK, LANES), 1)
    at_first, at_last, odd = lane == 0, lane == LANES - 1, lane % 2 == 1
    chunks = range(0, span_y, CHUNK)
    body_rows = pl.ds(PAD, span_y)
    vs = (v0, v1, v2)
    part = span_x // 2
    fzm = ion

    def plane_of(i):
        return lax.rem(i + START, span_x)

    loads = []
    for n, (src, dst) in enumerate(((eps_ref, e), (pot_ref, pot), (ion_ref, ion))):
        for half in (0, 1):
            place = dst.at[pl.ds(1, span_x), half, body_rows, :] if n == 0 else dst.at[:, half]
            loads.append(
                pltpu.make_async_copy(
                    src.at[:, :, pl.ds(half * LANES, LANES)], place, sem_in.at[2 * n + half]
                )
            )
    loads.append(pltpu.make_async_copy(b_ref, b, sem_in.at[6]))
    loads[0].start()
    loads[1].start()

    zero = jnp.zeros((span_y, LANES), F)
    for field in (e, v0, v1, v2):
        for half in (0, 1):
            for x in (0, span_x + 1):
                field[x, half, body_rows, :] = zero
    for k in range(4):
        for side in (0, 1):
            for which in (0, 1):
                z_recv[k, side, which] = zero
                y_recv[k, side, which] = jnp.zeros((span_x, LANES), F)

    barrier = pltpu.get_barrier_semaphore()
    for axis, place, size in zip(AXES, places, sizes):
        for step in range(1, size):
            pl.semaphore_signal(
                barrier, inc=1, device_id={axis: lax.rem(place + step, size)}, device_id_type=MESH
            )
    pl.semaphore_wait(barrier, sum(size - 1 for size in sizes))

    def halo_copies(k, field, x_faces, parts):
        pairs = []
        for n, (axis, place, size) in enumerate(zip(AXES, places, sizes)):
            if size == 1:
                continue
            for side in ((1,) if k == 3 else (0, 1)):
                ends = []
                if n == 0 and x_faces:
                    src = field.at[span_x if side == 0 else 1, :, body_rows, :]
                    ends.append((0, src, field.at[0 if side == 0 else span_x + 1, :, body_rows, :]))
                if n == 1:
                    for which in parts:
                        rows = pl.ds(which * part, part)
                        src = y_send.at[k, side, :, rows, :]
                        ends.append((1 + which, src, y_recv.at[k, side, :, rows, :]))
                if n == 2:
                    for which in parts:
                        ends.append((3 + which, z_send.at[k, which], z_recv.at[k, side, which]))
                for kind, src, dst in ends:
                    copy = pltpu.make_async_remote_copy(
                        src_ref=src,
                        dst_ref=dst,
                        send_sem=send_sem.at[k, 2 * kind + side],
                        recv_sem=recv_sem.at[k, 2 * kind + side],
                        device_id={axis: place + 1 if side == 0 else place - 1},
                        device_id_type=MESH,
                    )
                    above, below = place < size - 1, place > 0
                    pairs.append((above if side == 0 else below, below if side == 0 else above, copy))
        return pairs

    def send(*exchange):
        for has_target, _, copy in halo_copies(*exchange):
            pl.when(has_target)(copy.start)

    def receive(*exchange):
        for _, has_source, copy in halo_copies(*exchange):
            pl.when(has_source)(copy.wait_recv)

    def sent(*exchange):
        for has_target, _, copy in halo_copies(*exchange):
            pl.when(has_target)(copy.wait_send)

    def pack(k, field, which):
        def rows_of(i, _):
            x = plane_of(i)
            for half in (0, 1):
                y_send[k, 1, half, pl.ds(i, 1), :] = field[x + 1, half, pl.ds(PAD, 1), :]
                if k < 3:
                    y_send[k, 0, half, pl.ds(i, 1), :] = field[
                        x + 1, half, pl.ds(PAD + span_y - 1, 1), :
                    ]
            return 0

        def columns_of(i, accs):
            x = plane_of(i)
            out = []
            for t, acc in zip(chunks, accs):
                rows = pl.ds(PAD + t, CHUNK)
                ends = jnp.where(
                    at_first,
                    field[x + 1, 0, rows, :],
                    jnp.where(at_last, field[x + 1, 1, rows, :], 0.0),
                )
                out.append(acc + pltpu.roll(ends, 2 * x, 1))
            return tuple(out)

        first = which * part
        lax.fori_loop(first, first + part, rows_of, 0, unroll=8)
        empty = tuple(jnp.zeros((CHUNK, LANES), F) for _ in chunks)
        accs = lax.fori_loop(first, first + part, columns_of, empty, unroll=8)
        for t, acc in zip(chunks, accs):
            z_send[k, which, pl.ds(t, CHUNK), :] = acc

    def unpack(k, field, which):
        def rows_of(i, _):
            x = plane_of(i)
            for half in (0, 1):
                if k < 3:
                    field[x + 1, half, pl.ds(PAD - 1, 1), :] = y_recv[k, 0, half, pl.ds(i, 1), :]
                field[x + 1, half, pl.ds(PAD + span_y, 1), :] = y_recv[k, 1, half, pl.ds(i, 1), :]
            return 0

        first = which * part
        lax.fori_loop(first, first + part, rows_of, 0, unroll=8)
        for t in chunks:
            rows = pl.ds(t, CHUNK)
            low = pltpu.roll(z_recv[k, 0, which, rows, :], 2, 1)
            z_in[which, rows, :] = jnp.where(odd, low, z_recv[k, 1, which, rows, :])

    def z_neighbours(center, outer):
        after = [pltpu.roll(c, LANES - 1, 1) for c in center]
        before = [pltpu.roll(c, 1, 1) for c in center]
        after = [jnp.where(at_last, after[1], after[0]), jnp.where(at_last, outer, after[1])]
        before = [jnp.where(at_first, outer, before[0]), jnp.where(at_first, before[0], before[1])]
        return after, before

    def outer_z(which, t, x):
        return pltpu.roll(z_in[which, pl.ds(t, CHUNK), :], LANES - 1 - 2 * x, 1)

    def both_parts(body, carry, before, after, unroll):
        for which in (0, 1):
            before(which)
            carry = lax.fori_loop(
                which * part,
                (which + 1) * part,
                functools.partial(body, which),
                carry,
                unroll=unroll,
            )
            after(which)
        return carry

    loads[0].wait()
    loads[1].wait()
    for load in loads[2:]:
        load.start()
    send(0, e, True, ())
    for which in (0, 1):
        pack(0, e, which)
        send(0, e, False, (which,))

    for load in loads[2:6]:
        load.wait()

    def screen(x, _):
        for half in (0, 1):
            for t in chunks:
                rows = pl.ds(t, CHUNK)
                up = jnp.exp(pot[x, half, rows, :])
                rd[x, half, rows, :] = ion[x, half, rows, :] * (0.5 * (up + inverse_of(up)))
        return 0

    lax.fori_loop(0, span_x, screen, 0, unroll=2)
    loads[6].wait()

    def x_face(x):
        for half in (0, 1):
            for t in chunks:
                rows = pl.ds(PAD + t, CHUNK)
                fx[x, half, pl.ds(t, CHUNK), :] = harmonic(e[x, half, rows, :], e[x + 1, half, rows, :])

    def faces(which, i, total):
        x = plane_of(i)
        for half in (0, 1):
            fy[x, half, pl.ds(PAD - 1, 1), :] = harmonic(
                e[x + 1, half, pl.ds(PAD - 1, 1), :], e[x + 1, half, pl.ds(PAD, 1), :]
            )
        for t in chunks:
            rows, wide = pl.ds(t, CHUNK), pl.ds(PAD + t, CHUNK)
            center = [e[x + 1, half, wide, :] for half in (0, 1)]
            after, before = z_neighbours(center, outer_z(which, t, x))
            for half in (0, 1):
                c = center[half]
                x_next = harmonic(c, e[x + 2, half, wide, :])
                fx[x + 1, half, rows, :] = x_next
                y_next = harmonic(c, e[x + 1, half, pl.ds(PAD + t + 1, CHUNK), :])
                fy[x, half, wide, :] = y_next
                z_next, z_last = harmonic(c, after[half]), harmonic(c, before[half])
                fz[x, half, rows, :] = z_next
                fzm[x, half, rows, :] = z_last
                diagonal = (
                    x_next + fx[x, half, rows, :]
                    + y_next + fy[x, half, pl.ds(PAD + t - 1, CHUNK), :]
                    + z_next + z_last + rd[x, half, rows, :]
                )
                inverse = inverse_of(diagonal)
                rd[x, half, rows, :] = inverse
                source = b[pl.ds(x * (2 * span_y) + 2 * t + half, CHUNK, stride=2), :]
                value = source * inverse
                v0[x + 1, half, wide, :] = value
                total = total + source * value
        return total

    def ready(k, field):
        def before(which):
            receive(k, field, which == 1, (which,))
            unpack(k, field, which)
            if k == 0:
                x_face(START if which == 0 else 0)

        return before

    def done(k, field):
        def after(which):
            if which == 1:
                send(k, field, True, ())
            pack(k, field, which)
            send(k, field, False, (which,))

        return after

    nothing = jnp.zeros((CHUNK, LANES), F)
    moments = [both_parts(faces, nothing, ready(0, e), done(1, v0), UNROLL_FACES)]

    for k in (0, 1):
        v, result = vs[k], vs[k + 1]

        def apply(which, i, carry, v=v, result=result):
            first, second = carry
            x = plane_of(i)
            for t in chunks:
                rows, wide = pl.ds(t, CHUNK), pl.ds(PAD + t, CHUNK)
                up, down = pl.ds(PAD + t + 1, CHUNK), pl.ds(PAD + t - 1, CHUNK)
                center = [v[x + 1, half, wide, :] for half in (0, 1)]
                after, before = z_neighbours(center, outer_z(which, t, x))
                for half in (0, 1):
                    image = (
                        fx[x + 1, half, rows, :] * v[x + 2, half, wide, :]
                        + fx[x, half, rows, :] * v[x, half, wide, :]
                        + fy[x, half, wide, :] * v[x + 1, half, up, :]
                        + fy[x, half, down, :] * v[x + 1, half, down, :]
                        + fz[x, half, rows, :] * after[half]
                        + fzm[x, half, rows, :] * before[half]
                    )
                    value = image * rd[x, half, rows, :]
                    result[x + 1, half, wide, :] = value
                    first = first + center[half] * image
                    second = second + image * value
            return first, second

        moments.extend(
            both_parts(
                apply, (nothing, nothing), ready(k + 1, v), done(k + 2, result), UNROLL_APPLY
            )
        )

    def product(which, i, total):
        x = plane_of(i)
        for t in chunks:
            rows, wide = pl.ds(t, CHUNK), pl.ds(PAD + t, CHUNK)
            center = [v2[x + 1, half, wide, :] for half in (0, 1)]
            after = [pltpu.roll(c, LANES - 1, 1) for c in center]
            after = [
                jnp.where(at_last, after[1], after[0]),
                jnp.where(at_last, outer_z(which, t, x), after[1]),
            ]
            for half in (0, 1):
                image = (
                    fx[x + 1, half, rows, :] * v2[x + 2, half, wide, :]
                    + fy[x, half, wide, :] * v2[x + 1, half, pl.ds(PAD + t + 1, CHUNK), :]
                    + fz[x, half, rows, :] * after[half]
                )
                total = total + center[half] * image
        return total

    total = both_parts(product, nothing, ready(3, v2), lambda which: None, UNROLL_APPLY)
    moments.append(2.0 * total)

    row = lax.broadcasted_iota(jnp.int32, (8, LANES), 0)
    mine = jnp.zeros((8, LANES), F)
    for n, moment in enumerate(moments):
        folded = jnp.sum(moment, axis=0, keepdims=True)
        mine = mine + jnp.where(row == n, folded, 0.0)
    for n, (axis, place, size) in enumerate(zip(AXES, places, sizes)):
        red[n, place] = mine
        copies = []
        for step in range(1, size):
            target = lax.rem(place + step, size)
            copy = pltpu.make_async_remote_copy(
                src_ref=red.at[n, place],
                dst_ref=red.at[n, place],
                send_sem=red_send.at[n, step],
                recv_sem=red_recv.at[n, step],
                device_id={axis: target},
                device_id_type=MESH,
            )
            copy.start()
            copies.append(copy)
        for step in range(1, size):
            source = lax.rem(place + size - step, size)
            pltpu.make_async_remote_copy(
                src_ref=red.at[n, place],
                dst_ref=red.at[n, source],
                send_sem=red_send.at[n, step],
                recv_sem=red_recv.at[n, step],
                device_id={axis: source},
                device_id_type=MESH,
            ).wait_recv()
        for copy in copies:
            copy.wait_send()
        mine = red[n, 0]
        for other in range(1, size):
            mine = mine + red[n, other]
    totals = jnp.sum(mine, axis=1, keepdims=True)
    m = [totals[n:n + 1] for n in range(6)]
    m = [value / m[0] for value in m]

    h = [m[n] - m[n + 1] for n in range(5)]
    l1, l2 = h[1] / h[0], h[2] / h[0]
    d1 = h[2] - l1 * h[1]
    o1 = h[3] - l1 * h[2]
    l3 = o1 / d1
    d2 = h[4] - l2 * h[2] - l3 * o1
    r1 = m[1] - l1 * m[0]
    r2 = m[2] - l2 * m[0] - l3 * r1
    c2 = r2 / d2
    c1 = r1 / d1 - l3 * c2
    c0 = m[0] / h[0] - l1 * c1 - l2 * c2

    weights = [jnp.broadcast_to(c, (CHUNK, LANES)) for c in (c0, c1, c2)]

    def finish(x, _):
        for half in (0, 1):
            for t in chunks:
                wide = pl.ds(PAD + t, CHUNK)
                value = weights[0] * v0[x + 1, half, wide, :]
                value = value + weights[1] * v1[x + 1, half, wide, :]
                value = value + weights[2] * v2[x + 1, half, wide, :]
                pot[x, half, pl.ds(t, CHUNK), :] = value
                b[pl.ds(x * (2 * span_y) + 2 * t + half, CHUNK, stride=2), :] = value
        return 0

    lax.fori_loop(0, span_x, finish, 0, unroll=2)
    stores = [
        pltpu.make_async_copy(
            pot.at[:, half], out_ref.at[:, :, pl.ds(half * LANES, LANES)], sem_out.at[half]
        )
        for half in (0, 1)
    ]
    stores.append(pltpu.make_async_copy(b, rows_ref, sem_out.at[2]))
    for store in stores:
        store.start()
    for k, field in enumerate((e, v0, v1, v2)):
        sent(k, field, True, (0, 1))
    for store in stores:
        store.wait()


def krylov(sizes, b, eps, pot, ion):
    span_x, span_y, span_z = eps.shape
    tall = span_y + 2 * PAD
    padded = pltpu.VMEM((span_x + 2, 2, tall, LANES), F)
    plain = pltpu.VMEM((span_x, 2, span_y, LANES), F)
    dma = pltpu.SemaphoreType.DMA
    anywhere = pl.BlockSpec(memory_space=pl.ANY)
    most = max(sizes)
    return pl.pallas_call(
        functools.partial(krylov_kernel, sizes),
        out_shape=(
            jax.ShapeDtypeStruct(eps.shape, F),
            jax.ShapeDtypeStruct(b.shape, F),
        ),
        in_specs=[anywhere] * 4,
        out_specs=(anywhere, anywhere),
        scratch_shapes=[
            padded,
            pltpu.VMEM((span_x + 1, 2, span_y, LANES), F),
            pltpu.VMEM((span_x, 2, tall, LANES), F),
            plain,
            plain,
            padded, padded, padded,
            pltpu.VMEM(b.shape, F),
            plain,
            plain,
            pltpu.VMEM((4, 2, 2, span_x, LANES), F),
            pltpu.VMEM((4, 2, 2, span_x, LANES), F),
            pltpu.VMEM((4, 2, span_y, LANES), F),
            pltpu.VMEM((4, 2, 2, span_y, LANES), F),
            pltpu.VMEM((2, span_y, LANES), F),
            pltpu.VMEM((3, most, 8, LANES), F),
            dma((7,)),
            dma((4, 10)),
            dma((4, 10)),
            dma((3, most)),
            dma((3, most)),
            dma((3,)),
        ],
        compiler_params=pltpu.CompilerParams(
            vmem_limit_bytes=60 << 20, collective_id=0, has_side_effects=True
        ),
        name="krylov",
    )(b, eps, pot, ion)


def per_device(
    atom_charge, atom_fraction, atom_corner, block_count, permittivity, base_potential, ion_access
):
    sizes = tuple(lax.axis_size(axis) for axis in AXES)
    groups = sizes[2]
    capacity = atom_charge.shape[3] // groups
    live = jnp.arange(capacity, dtype=jnp.int32)[None, :] < block_count.reshape(groups, 1)
    charge = jnp.where(live, atom_charge.reshape(groups, capacity), 0.0)
    fraction = atom_fraction.reshape(3, groups, capacity)
    corner = atom_corner.reshape(3, groups, capacity)
    record = jnp.concatenate([charge[None], fraction, corner.astype(F)], axis=0)
    arrived = lax.all_to_all(record, "gz", split_axis=1, concat_axis=1, tiled=True)
    there_charge = arrived[0].reshape(-1)
    there_fraction = arrived[1:4].reshape(-1)
    there_corner = arrived[4:7].astype(jnp.int32).reshape(-1)
    sources = spread(there_charge, there_fraction, there_corner, permittivity.shape)
    grid_field, rows_field = krylov(sizes, sources, permittivity, base_potential, ion_access)
    solution_field, sampled = sample(there_fraction, there_corner, rows_field, grid_field)
    returned = lax.all_to_all(
        sampled[0].reshape(groups, capacity), "gz", split_axis=0, concat_axis=0, tiled=True
    )
    atom_sensitivity = jnp.where(live, returned, 0.0).reshape(1, 1, 1, groups * capacity)
    return (solution_field, atom_sensitivity)


def solution(mesh):
    in_specs = (
        P("gx", "gy", "gz", None),
        P(None, "gx", "gy", "gz", None),
        P(None, "gx", "gy", "gz", None),
        P("gx", "gy", "gz", None),
        P("gx", "gy", "gz"),
        P("gx", "gy", "gz"),
        P("gx", "gy", "gz"),
    )
    out_specs = (P("gx", "gy", "gz"), P("gx", "gy", "gz", None))
    return jax.shard_map(
        per_device, mesh=mesh, in_specs=in_specs, out_specs=out_specs, check_vma=False
    )
```

```python
import functools

import jax
import jax.numpy as jnp
from jax import lax
from jax.experimental import pallas as pl
from jax.experimental.pallas import tpu as pltpu
from jax.sharding import PartitionSpec as P

F = jnp.float32
AXES = ("gx", "gy", "gz")
MESH = pl.DeviceIdType.MESH
LANES = 128
PAD = 8
CHUNK = 16
SLOTS_PER_STEP = 16
TABLES = 2
START = 8
UNROLL_FACES = 4
UNROLL_APPLY = 8


def patterns():
    row = lax.broadcasted_iota(jnp.int32, (8, LANES), 0)
    lane = lax.broadcasted_iota(jnp.int32, (8, LANES), 1)
    return row, ((row % 2) * LANES + lane).astype(F)


def z_hat(pos, z):
    return jnp.maximum(1.0 - jnp.abs(pos - z), 0.0)


def greet(axis, size):
    barrier, place = pltpu.get_barrier_semaphore(), lax.axis_index(axis)
    for step in range(1, size):
        pl.semaphore_signal(
            barrier, inc=1, device_id={axis: lax.rem(place + step, size)}, device_id_type=MESH
        )
    pl.semaphore_wait(barrier, size - 1)


def deliver_kernel(
    size, span_y, q_ref, f_ref, c_ref, count_ref, index_ref, value_ref, q_out, q_in, f_in, c_in, send_sem, recv_sem
):
    place = lax.axis_index("gz")
    capacity = q_out.shape[2]
    slot = lax.broadcasted_iota(jnp.int32, (1, capacity), 1)
    for g in range(size):
        block = pl.ds(g * capacity, capacity)
        q_out[g] = jnp.where(slot < count_ref[0, 0, 0, g], q_ref[0, 0, :, block], 0.0)
    greet("gz", size)

    def copies(step, to, source):
        block = pl.ds(pl.multiple_of(to * capacity, capacity), capacity)
        parts = (
            (q_out.at[to], q_in.at[source]),
            (f_ref.at[:, 0, 0, :, block], f_in.at[source]),
            (c_ref.at[:, 0, 0, :, block], c_in.at[source]),
        )
        return [
            pltpu.make_async_remote_copy(
                src_ref=src,
                dst_ref=dst,
                send_sem=send_sem.at[step, n],
                recv_sem=recv_sem.at[step, n],
                device_id={"gz": to},
                device_id_type=MESH,
            )
            for n, (src, dst) in enumerate(parts)
        ]

    out = []
    for step in range(1, size):
        out.extend(copies(step, lax.rem(place + step, size), place))
    for copy in out:
        copy.start()

    def work_out(source, q, f, c):
        index_ref[source] = (c[0] * span_y + c[1]) * 2
        value_ref[source, 0] = c[2].astype(F) + f[2]
        value_ref[source, 1] = f[1]
        value_ref[source, 2] = f[0]
        value_ref[source, 3] = q * (1.0 - f[0])
        value_ref[source, 4] = q * f[0]

    own = pl.ds(pl.multiple_of(place * capacity, capacity), capacity)
    work_out(
        place,
        q_out[place],
        [f_ref[k, 0, 0, :, own] for k in range(3)],
        [c_ref[k, 0, 0, :, own] for k in range(3)],
    )
    for step in range(1, size):
        source = lax.rem(place + size - step, size)
        for copy in copies(step, lax.rem(place + step, size), source):
            copy.wait_recv()
        work_out(
            source,
            q_in[source],
            [f_in[source, k] for k in range(3)],
            [c_in[source, k] for k in range(3)],
        )
    for copy in out:
        copy.wait_send()


def deliver(size, span_y, charge, fraction, corner, count):
    capacity = charge.shape[3] // size
    vmem = pl.BlockSpec(memory_space=pltpu.VMEM)
    dma = pltpu.SemaphoreType.DMA
    return pl.pallas_call(
        functools.partial(deliver_kernel, size, span_y),
        out_shape=(
            jax.ShapeDtypeStruct((size, 1, capacity), jnp.int32),
            jax.ShapeDtypeStruct((size, 5, 1, capacity), F),
        ),
        in_specs=[vmem, vmem, vmem, pl.BlockSpec(memory_space=pltpu.SMEM)],
        out_specs=(vmem, vmem),
        scratch_shapes=[
            pltpu.VMEM((size, 1, capacity), F),
            pltpu.VMEM((size, 1, capacity), F),
            pltpu.VMEM((size, 3, 1, capacity), F),
            pltpu.VMEM((size, 3, 1, capacity), jnp.int32),
            dma((size, 3)),
            dma((size, 3)),
        ],
        compiler_params=pltpu.CompilerParams(collective_id=1, has_side_effects=True),
        name="deliver",
    )(charge, fraction, corner, count)


def give_back_kernel(size, sampled_ref, count_ref, out_ref, came, send_sem, recv_sem):
    place = lax.axis_index("gz")
    capacity = came.shape[2]
    slot = lax.broadcasted_iota(jnp.int32, (1, capacity), 1)
    greet("gz", size)

    def copy_of(step, to, source):
        block = pl.ds(pl.multiple_of(to * capacity, capacity), capacity)
        return pltpu.make_async_remote_copy(
            src_ref=sampled_ref.at[:, block],
            dst_ref=came.at[source],
            send_sem=send_sem.at[step],
            recv_sem=recv_sem.at[step],
            device_id={"gz": to},
            device_id_type=MESH,
        )

    out = [copy_of(step, lax.rem(place + step, size), place) for step in range(1, size)]
    for copy in out:
        copy.start()

    def put(source, values):
        block = pl.ds(pl.multiple_of(source * capacity, capacity), capacity)
        out_ref[0, 0, :, block] = jnp.where(slot < count_ref[0, 0, 0, source], values, 0.0)

    put(place, sampled_ref[:, pl.ds(pl.multiple_of(place * capacity, capacity), capacity)])
    for step in range(1, size):
        source = lax.rem(place + size - step, size)
        copy_of(step, lax.rem(place + step, size), source).wait_recv()
        put(source, came[source])
    for copy in out:
        copy.wait_send()


def give_back(size, sampled, count):
    slots = sampled.shape[1]
    vmem = pl.BlockSpec(memory_space=pltpu.VMEM)
    dma = pltpu.SemaphoreType.DMA
    return pl.pallas_call(
        functools.partial(give_back_kernel, size),
        out_shape=jax.ShapeDtypeStruct((1, 1, 1, slots), F),
        in_specs=[vmem, pl.BlockSpec(memory_space=pltpu.SMEM)],
        out_specs=vmem,
        scratch_shapes=[pltpu.VMEM((size, 1, slots // size), F), dma((size,)), dma((size,))],
        compiler_params=pltpu.CompilerParams(collective_id=2, has_side_effects=True),
        name="give_back",
    )(sampled, count)


def spread_kernel(span_y, index_ref, value_ref, out_ref, *scratch):
    tables, sem = scratch[:TABLES], scratch[TABLES]
    rows = out_ref.shape[0]
    block = 128

    def clear(i, _):
        for table in tables:
            table[pl.ds(pl.multiple_of(i * block, block), block), :] = jnp.zeros((block, LANES), F)
        return 0

    lax.fori_loop(0, rows // block, clear, 0)
    for table in tables:
        table[pl.ds(rows, 8), :] = jnp.zeros((8, LANES), F)
    row, pos = patterns()
    ya = jnp.where(row < 2, 1.0, 0.0).astype(F)
    yb = jnp.where(row < 2, -1.0, jnp.where(row < 4, 1.0, 0.0)).astype(F)
    plane = 2 * span_y
    groups, _, capacity = index_ref.shape

    for g in range(groups):

        def body(i, _, g=g):
            for first in range(0, SLOTS_PER_STEP, TABLES):
                items = []
                for which, table in enumerate(tables):
                    s = i * SLOTS_PER_STEP + first + which
                    r = pl.multiple_of(index_ref[g, 0, s], 2)
                    w = (ya + yb * value_ref[g, 1, 0, s]) * z_hat(pos, value_ref[g, 0, 0, s])
                    near = table[pl.ds(r, 8), :] + w * value_ref[g, 3, 0, s]
                    far = table[pl.ds(r + plane, 8), :] + w * value_ref[g, 4, 0, s]
                    items.append((table, r, near, far))
                for table, r, near, far in items:
                    table[pl.ds(r, 8), :] = near
                    table[pl.ds(r + plane, 8), :] = far
            return 0

        lax.fori_loop(0, capacity // SLOTS_PER_STEP, body, 0)

    def combine(i, _):
        part = pl.ds(pl.multiple_of(i * block, block), block)
        total = tables[0][part, :]
        for table in tables[1:]:
            total = total + table[part, :]
        tables[0][part, :] = total
        return 0

    lax.fori_loop(0, rows // block, combine, 0)
    copy = pltpu.make_async_copy(tables[0].at[pl.ds(0, rows), :], out_ref, sem)
    copy.start()
    copy.wait()


def spread(index, value, span):
    rows = span[0] * span[1] * 2
    return pl.pallas_call(
        functools.partial(spread_kernel, span[1]),
        out_shape=jax.ShapeDtypeStruct((rows, LANES), F),
        in_specs=[pl.BlockSpec(memory_space=pltpu.SMEM)] * 2,
        out_specs=pl.BlockSpec(memory_space=pl.ANY),
        scratch_shapes=[pltpu.VMEM((rows + 8, LANES), F)] * TABLES + [pltpu.SemaphoreType.DMA(())],
        compiler_params=pltpu.CompilerParams(vmem_limit_bytes=56 << 20),
        name="spread",
    )(index, value)


def sample_kernel(
    span_y, index_ref, value_ref, rows_ref, grid_ref, field_ref, out_ref, table, grid, parts, sums, sems
):
    rows = rows_ref.shape[0]
    load = pltpu.make_async_copy(rows_ref, table.at[pl.ds(8, rows), :], sems.at[1])
    load.start()
    table[pl.ds(0, 8), :] = jnp.zeros((8, LANES), F)
    table[pl.ds(rows + 8, 8), :] = jnp.zeros((8, LANES), F)
    load.wait()
    hold = pltpu.make_async_copy(grid_ref, grid, sems.at[0])
    hold.start()
    row, pos = patterns()
    first_row, second_row = row % 4 < 2, row < 4
    yb = jnp.where(first_row, -1.0, 1.0).astype(F)
    ya = jnp.where(first_row, 1.0, 0.0).astype(F)
    masks = [jnp.where(second_row, 1.0, 0.0).astype(F), jnp.where(second_row, 0.0, 1.0).astype(F)]
    weights = [(ya * mask, yb * mask) for mask in masks]
    plane = 2 * span_y
    groups, _, capacity = index_ref.shape
    keep = pltpu.make_async_copy(grid, field_ref, sems.at[2])

    for g in range(groups):

        def body(i, _, g=g):
            for pair in range(SLOTS_PER_STEP // 2):
                total = None
                for which in (0, 1):
                    s = i * SLOTS_PER_STEP + 2 * pair + which
                    r = pl.multiple_of(index_ref[g, 0, s], 2) + (8 - 4 * which)
                    wa, wb = weights[which]
                    w = (wa + wb * value_ref[g, 1, 0, s]) * z_hat(pos, value_ref[g, 0, 0, s])
                    near, far = table[pl.ds(r, 8), :], table[pl.ds(r + plane, 8), :]
                    term = w * (near + value_ref[g, 2, 0, s] * (far - near))
                    total = term if total is None else total + term
                start = i * (SLOTS_PER_STEP // 2) + (g * (capacity // 2) + pair)
                parts[pl.ds(pl.multiple_of(start * 8, 8), 8), :] = total
            return 0

        lax.fori_loop(0, capacity // SLOTS_PER_STEP, body, 0)
        if g == 0:
            hold.wait()
            keep.start()

    def fold(i, _):
        start = pl.multiple_of(i * 256, 256)
        total = parts[pl.ds(start, 64, stride=4), :]
        for j in range(1, 4):
            total = total + parts[pl.ds(start + j, 64, stride=4), :]
        sums[pl.ds(pl.multiple_of(i * 64, 64), 64), :] = total
        return 0

    lax.fori_loop(0, groups * capacity // 64, fold, 0)
    out_ref[...] = lax.dot_general(
        jnp.ones((8, LANES), F),
        sums[...],
        (((1,), (1,)), ((), ())),
        precision=lax.Precision.HIGHEST,
        preferred_element_type=F,
    )[0:1]
    keep.wait()


def sample(index, value, rows_field, grid_field):
    span_y, rows = grid_field.shape[1], rows_field.shape[0]
    slots = index.shape[0] * index.shape[2]
    smem, anywhere = pl.BlockSpec(memory_space=pltpu.SMEM), pl.BlockSpec(memory_space=pl.ANY)
    return pl.pallas_call(
        functools.partial(sample_kernel, span_y),
        out_shape=(
            jax.ShapeDtypeStruct(grid_field.shape, F),
            jax.ShapeDtypeStruct((1, slots), F),
        ),
        in_specs=[smem, smem, anywhere, anywhere],
        out_specs=(anywhere, pl.BlockSpec(memory_space=pltpu.VMEM)),
        scratch_shapes=[
            pltpu.VMEM((rows + 16, LANES), F),
            pltpu.VMEM(grid_field.shape, F),
            pltpu.VMEM((slots * 4, LANES), F),
            pltpu.VMEM((slots, LANES), F),
            pltpu.SemaphoreType.DMA((3,)),
        ],
        compiler_params=pltpu.CompilerParams(vmem_limit_bytes=56 << 20),
        name="sample",
    )(index, value, rows_field, grid_field)


def inverse_of(value):
    guess = pl.reciprocal(value, approx=True)
    return guess * (2.0 - value * guess)


def harmonic(former, latter):
    return (2.0 * former * latter) * inverse_of(former + latter)


def krylov_kernel(
    sizes,
    b_ref, eps_ref, pot_ref, ion_ref,
    out_ref, rows_ref,
    e, fx, fy, fz, rd, v0, v1, v2, b, pot, ion,
    y_send, y_recv, z_send, z_recv, z_in, red,
    sem_in, send_sem, recv_sem, red_send, red_recv, sem_out,
):
    span_x, span_y, _ = eps_ref.shape
    places = [lax.axis_index(axis) for axis in AXES]
    lane = lax.broadcasted_iota(jnp.int32, (CHUNK, LANES), 1)
    at_first, at_last, odd = lane == 0, lane == LANES - 1, lane % 2 == 1
    chunks = range(0, span_y, CHUNK)
    body_rows = pl.ds(PAD, span_y)
    vs = (v0, v1, v2)
    part = span_x // 2
    fzm = ion

    def plane_of(i):
        return lax.rem(i + START, span_x)

    loads = []
    for n, (src, dst) in enumerate(((eps_ref, e), (pot_ref, pot), (ion_ref, ion))):
        for half in (0, 1):
            place = dst.at[pl.ds(1, span_x), half, body_rows, :] if n == 0 else dst.at[:, half]
            loads.append(
                pltpu.make_async_copy(
                    src.at[:, :, pl.ds(half * LANES, LANES)], place, sem_in.at[2 * n + half]
                )
            )
    loads.append(pltpu.make_async_copy(b_ref, b, sem_in.at[6]))
    loads[0].start()
    loads[1].start()

    zero = jnp.zeros((span_y, LANES), F)
    for field in (e, v0, v1, v2):
        for half in (0, 1):
            for x in (0, span_x + 1):
                field[x, half, body_rows, :] = zero
    for k in range(4):
        for side in (0, 1):
            for which in (0, 1):
                z_recv[k, side, which] = zero
                y_recv[k, side, which] = jnp.zeros((span_x, LANES), F)

    barrier = pltpu.get_barrier_semaphore()
    for axis, place, size in zip(AXES, places, sizes):
        for step in range(1, size):
            pl.semaphore_signal(
                barrier, inc=1, device_id={axis: lax.rem(place + step, size)}, device_id_type=MESH
            )
    pl.semaphore_wait(barrier, sum(size - 1 for size in sizes))

    def halo_copies(k, field, x_faces, parts):
        pairs = []
        for n, (axis, place, size) in enumerate(zip(AXES, places, sizes)):
            if size == 1:
                continue
            for side in ((1,) if k == 3 else (0, 1)):
                ends = []
                if n == 0 and x_faces:
                    src = field.at[span_x if side == 0 else 1, :, body_rows, :]
                    ends.append((0, src, field.at[0 if side == 0 else span_x + 1, :, body_rows, :]))
                if n == 1:
                    for which in parts:
                        rows = pl.ds(which * part, part)
                        src = y_send.at[k, side, :, rows, :]
                        ends.append((1 + which, src, y_recv.at[k, side, :, rows, :]))
                if n == 2:
                    for which in parts:
                        ends.append((3 + which, z_send.at[k, which], z_recv.at[k, side, which]))
                for kind, src, dst in ends:
                    copy = pltpu.make_async_remote_copy(
                        src_ref=src,
                        dst_ref=dst,
                        send_sem=send_sem.at[k, 2 * kind + side],
                        recv_sem=recv_sem.at[k, 2 * kind + side],
                        device_id={axis: place + 1 if side == 0 else place - 1},
                        device_id_type=MESH,
                    )
                    above, below = place < size - 1, place > 0
                    pairs.append((above if side == 0 else below, below if side == 0 else above, copy))
        return pairs

    def send(*exchange):
        for has_target, _, copy in halo_copies(*exchange):
            pl.when(has_target)(copy.start)

    def receive(*exchange):
        for _, has_source, copy in halo_copies(*exchange):
            pl.when(has_source)(copy.wait_recv)

    def sent(*exchange):
        for has_target, _, copy in halo_copies(*exchange):
            pl.when(has_target)(copy.wait_send)

    def pack(k, field, which):
        def rows_of(i, _):
            x = plane_of(i)
            for half in (0, 1):
                y_send[k, 1, half, pl.ds(i, 1), :] = field[x + 1, half, pl.ds(PAD, 1), :]
                if k < 3:
                    y_send[k, 0, half, pl.ds(i, 1), :] = field[
                        x + 1, half, pl.ds(PAD + span_y - 1, 1), :
                    ]
            return 0

        def columns_of(i, accs):
            x = plane_of(i)
            out = []
            for t, acc in zip(chunks, accs):
                rows = pl.ds(PAD + t, CHUNK)
                ends = jnp.where(
                    at_first,
                    field[x + 1, 0, rows, :],
                    jnp.where(at_last, field[x + 1, 1, rows, :], 0.0),
                )
                out.append(acc + pltpu.roll(ends, 2 * x, 1))
            return tuple(out)

        first = which * part
        lax.fori_loop(first, first + part, rows_of, 0, unroll=8)
        empty = tuple(jnp.zeros((CHUNK, LANES), F) for _ in chunks)
        accs = lax.fori_loop(first, first + part, columns_of, empty, unroll=8)
        for t, acc in zip(chunks, accs):
            z_send[k, which, pl.ds(t, CHUNK), :] = acc

    def unpack(k, field, which):
        def rows_of(i, _):
            x = plane_of(i)
            for half in (0, 1):
                if k < 3:
                    field[x + 1, half, pl.ds(PAD - 1, 1), :] = y_recv[k, 0, half, pl.ds(i, 1), :]
                field[x + 1, half, pl.ds(PAD + span_y, 1), :] = y_recv[k, 1, half, pl.ds(i, 1), :]
            return 0

        first = which * part
        lax.fori_loop(first, first + part, rows_of, 0, unroll=8)
        for t in chunks:
            rows = pl.ds(t, CHUNK)
            low = pltpu.roll(z_recv[k, 0, which, rows, :], 2, 1)
            z_in[which, rows, :] = jnp.where(odd, low, z_recv[k, 1, which, rows, :])

    def z_neighbours(center, outer):
        after = [pltpu.roll(c, LANES - 1, 1) for c in center]
        before = [pltpu.roll(c, 1, 1) for c in center]
        after = [jnp.where(at_last, after[1], after[0]), jnp.where(at_last, outer, after[1])]
        before = [jnp.where(at_first, outer, before[0]), jnp.where(at_first, before[0], before[1])]
        return after, before

    def outer_z(which, t, x):
        return pltpu.roll(z_in[which, pl.ds(t, CHUNK), :], LANES - 1 - 2 * x, 1)

    def both_parts(body, carry, before, after, unroll):
        for which in (0, 1):
            before(which)
            carry = lax.fori_loop(
                which * part,
                (which + 1) * part,
                functools.partial(body, which),
                carry,
                unroll=unroll,
            )
            after(which)
        return carry

    loads[0].wait()
    loads[1].wait()
    for load in loads[2:]:
        load.start()
    send(0, e, True, ())
    for which in (0, 1):
        pack(0, e, which)
        send(0, e, False, (which,))

    for load in loads[2:6]:
        load.wait()

    def screen(x, _):
        for half in (0, 1):
            for t in chunks:
                rows = pl.ds(t, CHUNK)
                up = jnp.exp(pot[x, half, rows, :])
                rd[x, half, rows, :] = ion[x, half, rows, :] * (0.5 * (up + inverse_of(up)))
        return 0

    lax.fori_loop(0, span_x, screen, 0, unroll=2)
    loads[6].wait()

    def x_face(x):
        for half in (0, 1):
            for t in chunks:
                rows = pl.ds(PAD + t, CHUNK)
                fx[x, half, pl.ds(t, CHUNK), :] = harmonic(e[x, half, rows, :], e[x + 1, half, rows, :])

    def faces(which, i, total):
        x = plane_of(i)
        for half in (0, 1):
            fy[x, half, pl.ds(PAD - 1, 1), :] = harmonic(
                e[x + 1, half, pl.ds(PAD - 1, 1), :], e[x + 1, half, pl.ds(PAD, 1), :]
            )
        for t in chunks:
            rows, wide = pl.ds(t, CHUNK), pl.ds(PAD + t, CHUNK)
            center = [e[x + 1, half, wide, :] for half in (0, 1)]
            after, before = z_neighbours(center, outer_z(which, t, x))
            for half in (0, 1):
                c = center[half]
                x_next = harmonic(c, e[x + 2, half, wide, :])
                fx[x + 1, half, rows, :] = x_next
                y_next = harmonic(c, e[x + 1, half, pl.ds(PAD + t + 1, CHUNK), :])
                fy[x, half, wide, :] = y_next
                z_next, z_last = harmonic(c, after[half]), harmonic(c, before[half])
                fz[x, half, rows, :] = z_next
                fzm[x, half, rows, :] = z_last
                diagonal = (
                    x_next + fx[x, half, rows, :]
                    + y_next + fy[x, half, pl.ds(PAD + t - 1, CHUNK), :]
                    + z_next + z_last + rd[x, half, rows, :]
                )
                inverse = inverse_of(diagonal)
                rd[x, half, rows, :] = inverse
                source = b[pl.ds(x * (2 * span_y) + 2 * t + half, CHUNK, stride=2), :]
                value = source * inverse
                v0[x + 1, half, wide, :] = value
                total = total + source * value
        return total

    def ready(k, field):
        def before(which):
            receive(k, field, which == 1, (which,))
            unpack(k, field, which)
            if k == 0:
                x_face(START if which == 0 else 0)

        return before

    def done(k, field):
        def after(which):
            if which == 1:
                send(k, field, True, ())
            pack(k, field, which)
            send(k, field, False, (which,))

        return after

    nothing = jnp.zeros((CHUNK, LANES), F)
    moments = [both_parts(faces, nothing, ready(0, e), done(1, v0), UNROLL_FACES)]

    for k in (0, 1):
        v, result = vs[k], vs[k + 1]

        def apply(which, i, carry, v=v, result=result):
            first, second = carry
            x = plane_of(i)
            for t in chunks:
                rows, wide = pl.ds(t, CHUNK), pl.ds(PAD + t, CHUNK)
                up, down = pl.ds(PAD + t + 1, CHUNK), pl.ds(PAD + t - 1, CHUNK)
                center = [v[x + 1, half, wide, :] for half in (0, 1)]
                after, before = z_neighbours(center, outer_z(which, t, x))
                for half in (0, 1):
                    image = (
                        fx[x + 1, half, rows, :] * v[x + 2, half, wide, :]
                        + fx[x, half, rows, :] * v[x, half, wide, :]
                        + fy[x, half, wide, :] * v[x + 1, half, up, :]
                        + fy[x, half, down, :] * v[x + 1, half, down, :]
                        + fz[x, half, rows, :] * after[half]
                        + fzm[x, half, rows, :] * before[half]
                    )
                    value = image * rd[x, half, rows, :]
                    result[x + 1, half, wide, :] = value
                    first = first + center[half] * image
                    second = second + image * value
            return first, second

        moments.extend(
            both_parts(
                apply, (nothing, nothing), ready(k + 1, v), done(k + 2, result), UNROLL_APPLY
            )
        )

    def product(which, i, total):
        x = plane_of(i)
        for t in chunks:
            rows, wide = pl.ds(t, CHUNK), pl.ds(PAD + t, CHUNK)
            center = [v2[x + 1, half, wide, :] for half in (0, 1)]
            after = [pltpu.roll(c, LANES - 1, 1) for c in center]
            after = [
                jnp.where(at_last, after[1], after[0]),
                jnp.where(at_last, outer_z(which, t, x), after[1]),
            ]
            for half in (0, 1):
                image = (
                    fx[x + 1, half, rows, :] * v2[x + 2, half, wide, :]
                    + fy[x, half, wide, :] * v2[x + 1, half, pl.ds(PAD + t + 1, CHUNK), :]
                    + fz[x, half, rows, :] * after[half]
                )
                total = total + center[half] * image
        return total

    total = both_parts(product, nothing, ready(3, v2), lambda which: None, UNROLL_APPLY)
    moments.append(2.0 * total)

    row = lax.broadcasted_iota(jnp.int32, (8, LANES), 0)
    mine = jnp.zeros((8, LANES), F)
    for n, moment in enumerate(moments):
        folded = jnp.sum(moment, axis=0, keepdims=True)
        mine = mine + jnp.where(row == n, folded, 0.0)
    for n, (axis, place, size) in enumerate(zip(AXES, places, sizes)):
        red[n, place] = mine
        copies = []
        for step in range(1, size):
            target = lax.rem(place + step, size)
            copy = pltpu.make_async_remote_copy(
                src_ref=red.at[n, place],
                dst_ref=red.at[n, place],
                send_sem=red_send.at[n, step],
                recv_sem=red_recv.at[n, step],
                device_id={axis: target},
                device_id_type=MESH,
            )
            copy.start()
            copies.append(copy)
        for step in range(1, size):
            source = lax.rem(place + size - step, size)
            pltpu.make_async_remote_copy(
                src_ref=red.at[n, place],
                dst_ref=red.at[n, source],
                send_sem=red_send.at[n, step],
                recv_sem=red_recv.at[n, step],
                device_id={axis: source},
                device_id_type=MESH,
            ).wait_recv()
        for copy in copies:
            copy.wait_send()
        mine = red[n, 0]
        for other in range(1, size):
            mine = mine + red[n, other]
    totals = jnp.sum(mine, axis=1, keepdims=True)
    m = [totals[n:n + 1] for n in range(6)]
    m = [value / m[0] for value in m]

    h = [m[n] - m[n + 1] for n in range(5)]
    l1, l2 = h[1] / h[0], h[2] / h[0]
    d1 = h[2] - l1 * h[1]
    o1 = h[3] - l1 * h[2]
    l3 = o1 / d1
    d2 = h[4] - l2 * h[2] - l3 * o1
    r1 = m[1] - l1 * m[0]
    r2 = m[2] - l2 * m[0] - l3 * r1
    c2 = r2 / d2
    c1 = r1 / d1 - l3 * c2
    c0 = m[0] / h[0] - l1 * c1 - l2 * c2

    weights = [jnp.broadcast_to(c, (CHUNK, LANES)) for c in (c0, c1, c2)]

    def finish(x, _):
        for half in (0, 1):
            for t in chunks:
                wide = pl.ds(PAD + t, CHUNK)
                value = weights[0] * v0[x + 1, half, wide, :]
                value = value + weights[1] * v1[x + 1, half, wide, :]
                value = value + weights[2] * v2[x + 1, half, wide, :]
                pot[x, half, pl.ds(t, CHUNK), :] = value
                b[pl.ds(x * (2 * span_y) + 2 * t + half, CHUNK, stride=2), :] = value
        return 0

    lax.fori_loop(0, span_x, finish, 0, unroll=2)
    stores = [
        pltpu.make_async_copy(
            pot.at[:, half], out_ref.at[:, :, pl.ds(half * LANES, LANES)], sem_out.at[half]
        )
        for half in (0, 1)
    ]
    stores.append(pltpu.make_async_copy(b, rows_ref, sem_out.at[2]))
    for store in stores:
        store.start()
    for k, field in enumerate((e, v0, v1, v2)):
        sent(k, field, True, (0, 1))
    for store in stores:
        store.wait()


def krylov(sizes, b, eps, pot, ion):
    span_x, span_y, span_z = eps.shape
    tall = span_y + 2 * PAD
    padded = pltpu.VMEM((span_x + 2, 2, tall, LANES), F)
    plain = pltpu.VMEM((span_x, 2, span_y, LANES), F)
    dma = pltpu.SemaphoreType.DMA
    anywhere = pl.BlockSpec(memory_space=pl.ANY)
    most = max(sizes)
    return pl.pallas_call(
        functools.partial(krylov_kernel, sizes),
        out_shape=(
            jax.ShapeDtypeStruct(eps.shape, F),
            jax.ShapeDtypeStruct(b.shape, F),
        ),
        in_specs=[anywhere] * 4,
        out_specs=(anywhere, anywhere),
        scratch_shapes=[
            padded,
            pltpu.VMEM((span_x + 1, 2, span_y, LANES), F),
            pltpu.VMEM((span_x, 2, tall, LANES), F),
            plain,
            plain,
            padded, padded, padded,
            pltpu.VMEM(b.shape, F),
            plain,
            plain,
            pltpu.VMEM((4, 2, 2, span_x, LANES), F),
            pltpu.VMEM((4, 2, 2, span_x, LANES), F),
            pltpu.VMEM((4, 2, span_y, LANES), F),
            pltpu.VMEM((4, 2, 2, span_y, LANES), F),
            pltpu.VMEM((2, span_y, LANES), F),
            pltpu.VMEM((3, most, 8, LANES), F),
            dma((7,)),
            dma((4, 10)),
            dma((4, 10)),
            dma((3, most)),
            dma((3, most)),
            dma((3,)),
        ],
        compiler_params=pltpu.CompilerParams(
            vmem_limit_bytes=60 << 20, collective_id=0, has_side_effects=True
        ),
        name="krylov",
    )(b, eps, pot, ion)


def per_device(
    atom_charge, atom_fraction, atom_corner, block_count, permittivity, base_potential, ion_access
):
    sizes = tuple(lax.axis_size(axis) for axis in AXES)
    index, value = deliver(
        sizes[2], permittivity.shape[1], atom_charge, atom_fraction, atom_corner, block_count
    )
    sources = spread(index, value, permittivity.shape)
    grid_field, rows_field = krylov(sizes, sources, permittivity, base_potential, ion_access)
    solution_field, sampled = sample(index, value, rows_field, grid_field)
    return solution_field, give_back(sizes[2], sampled, block_count)


def solution(mesh):
    in_specs = (
        P("gx", "gy", "gz", None),
        P(None, "gx", "gy", "gz", None),
        P(None, "gx", "gy", "gz", None),
        P("gx", "gy", "gz", None),
        P("gx", "gy", "gz"),
        P("gx", "gy", "gz"),
        P("gx", "gy", "gz"),
    )
    out_specs = (P("gx", "gy", "gz"), P("gx", "gy", "gz", None))
    return jax.shard_map(
        per_device, mesh=mesh, in_specs=in_specs, out_specs=out_specs, check_vma=False
    )
```

```python
import functools

import jax
import jax.numpy as jnp
from jax import lax
from jax.experimental import pallas as pl
from jax.experimental.pallas import tpu as pltpu
from jax.sharding import PartitionSpec as P

F = jnp.float32
AXES = ("gx", "gy", "gz")
STAGES = (("gy",), ("gx", "gz"))
MESH = pl.DeviceIdType.MESH
LANES = 128
PAD = 8
CHUNK = 16
SLOTS_PER_STEP = 32
TABLES = 2
START = 8
UNROLL_FACES = 4
UNROLL_APPLY = 8


def patterns():
    row = lax.broadcasted_iota(jnp.int32, (8, LANES), 0)
    lane = lax.broadcasted_iota(jnp.int32, (8, LANES), 1)
    return row, ((row % 2) * LANES + lane).astype(F)


def z_hat(pos, z):
    return jnp.maximum(1.0 - jnp.abs(pos - z), 0.0)


def greet(axis, size):
    barrier, place = pltpu.get_barrier_semaphore(), lax.axis_index(axis)
    for step in range(1, size):
        pl.semaphore_signal(
            barrier, inc=1, device_id={axis: lax.rem(place + step, size)}, device_id_type=MESH
        )
    pl.semaphore_wait(barrier, size - 1)


def deliver_kernel(
    size, span_y, q_ref, f_ref, c_ref, count_ref, index_ref, value_ref, q_out, q_in, f_in, c_in, send_sem, recv_sem
):
    place = lax.axis_index("gz")
    capacity = q_out.shape[2]
    slot = lax.broadcasted_iota(jnp.int32, (1, capacity), 1)
    for g in range(size):
        block = pl.ds(g * capacity, capacity)
        q_out[g] = jnp.where(slot < count_ref[0, 0, 0, g], q_ref[0, 0, :, block], 0.0)
    greet("gz", size)

    def copies(step, to, source):
        block = pl.ds(pl.multiple_of(to * capacity, capacity), capacity)
        parts = (
            (q_out.at[to], q_in.at[source]),
            (f_ref.at[:, 0, 0, :, block], f_in.at[source]),
            (c_ref.at[:, 0, 0, :, block], c_in.at[source]),
        )
        return [
            pltpu.make_async_remote_copy(
                src_ref=src,
                dst_ref=dst,
                send_sem=send_sem.at[step, n],
                recv_sem=recv_sem.at[step, n],
                device_id={"gz": to},
                device_id_type=MESH,
            )
            for n, (src, dst) in enumerate(parts)
        ]

    out = []
    for step in range(1, size):
        out.extend(copies(step, lax.rem(place + step, size), place))
    for copy in out:
        copy.start()

    def work_out(source, q, f, c):
        block = pl.ds(pl.multiple_of(source * capacity, capacity), capacity)
        index_ref[:, block] = (c[0] * span_y + c[1]) * 2
        value_ref[0, :, block] = c[2].astype(F) + f[2]
        value_ref[1, :, block] = f[1]
        value_ref[2, :, block] = f[0]
        value_ref[3, :, block] = q * (1.0 - f[0])
        value_ref[4, :, block] = q * f[0]

    own = pl.ds(pl.multiple_of(place * capacity, capacity), capacity)
    work_out(
        place,
        q_out[place],
        [f_ref[k, 0, 0, :, own] for k in range(3)],
        [c_ref[k, 0, 0, :, own] for k in range(3)],
    )
    for step in range(1, size):
        source = lax.rem(place + size - step, size)
        for copy in copies(step, lax.rem(place + step, size), source):
            copy.wait_recv()
        work_out(
            source,
            q_in[source],
            [f_in[source, k] for k in range(3)],
            [c_in[source, k] for k in range(3)],
        )
    for copy in out:
        copy.wait_send()


def deliver(size, span_y, charge, fraction, corner, count):
    capacity = charge.shape[3] // size
    vmem = pl.BlockSpec(memory_space=pltpu.VMEM)
    dma = pltpu.SemaphoreType.DMA
    return pl.pallas_call(
        functools.partial(deliver_kernel, size, span_y),
        out_shape=(
            jax.ShapeDtypeStruct((1, size * capacity), jnp.int32),
            jax.ShapeDtypeStruct((5, 1, size * capacity), F),
        ),
        in_specs=[vmem, vmem, vmem, pl.BlockSpec(memory_space=pltpu.SMEM)],
        out_specs=(vmem, vmem),
        scratch_shapes=[
            pltpu.VMEM((size, 1, capacity), F),
            pltpu.VMEM((size, 1, capacity), F),
            pltpu.VMEM((size, 3, 1, capacity), F),
            pltpu.VMEM((size, 3, 1, capacity), jnp.int32),
            dma((size, 3)),
            dma((size, 3)),
        ],
        compiler_params=pltpu.CompilerParams(collective_id=1, has_side_effects=True),
        name="deliver",
    )(charge, fraction, corner, count)


def give_back_kernel(size, sampled_ref, count_ref, out_ref, came, send_sem, recv_sem):
    place = lax.axis_index("gz")
    capacity = came.shape[2]
    slot = lax.broadcasted_iota(jnp.int32, (1, capacity), 1)
    greet("gz", size)

    def copy_of(step, to, source):
        block = pl.ds(pl.multiple_of(to * capacity, capacity), capacity)
        return pltpu.make_async_remote_copy(
            src_ref=sampled_ref.at[:, block],
            dst_ref=came.at[source],
            send_sem=send_sem.at[step],
            recv_sem=recv_sem.at[step],
            device_id={"gz": to},
            device_id_type=MESH,
        )

    out = [copy_of(step, lax.rem(place + step, size), place) for step in range(1, size)]
    for copy in out:
        copy.start()

    def put(source, values):
        block = pl.ds(pl.multiple_of(source * capacity, capacity), capacity)
        out_ref[0, 0, :, block] = jnp.where(slot < count_ref[0, 0, 0, source], values, 0.0)

    put(place, sampled_ref[:, pl.ds(pl.multiple_of(place * capacity, capacity), capacity)])
    for step in range(1, size):
        source = lax.rem(place + size - step, size)
        copy_of(step, lax.rem(place + step, size), source).wait_recv()
        put(source, came[source])
    for copy in out:
        copy.wait_send()


def give_back(size, sampled, count):
    slots = sampled.shape[1]
    vmem = pl.BlockSpec(memory_space=pltpu.VMEM)
    dma = pltpu.SemaphoreType.DMA
    return pl.pallas_call(
        functools.partial(give_back_kernel, size),
        out_shape=jax.ShapeDtypeStruct((1, 1, 1, slots), F),
        in_specs=[vmem, pl.BlockSpec(memory_space=pltpu.SMEM)],
        out_specs=vmem,
        scratch_shapes=[pltpu.VMEM((size, 1, slots // size), F), dma((size,)), dma((size,))],
        compiler_params=pltpu.CompilerParams(collective_id=2, has_side_effects=True),
        name="give_back",
    )(sampled, count)


def spread_kernel(span_y, index_ref, value_ref, out_ref, *scratch):
    tables, sem = scratch[:TABLES], scratch[TABLES]
    rows = out_ref.shape[0]
    block = 128

    def clear(i, _):
        for table in tables:
            table[pl.ds(pl.multiple_of(i * block, block), block), :] = jnp.zeros((block, LANES), F)
        return 0

    lax.fori_loop(0, rows // block, clear, 0)
    for table in tables:
        table[pl.ds(rows, 8), :] = jnp.zeros((8, LANES), F)
    row, pos = patterns()
    ya = jnp.where(row < 2, 1.0, 0.0).astype(F)
    yb = jnp.where(row < 2, -1.0, jnp.where(row < 4, 1.0, 0.0)).astype(F)
    plane = 2 * span_y

    steps = index_ref.shape[1] // SLOTS_PER_STEP

    def body(i, _):
        for first in range(0, SLOTS_PER_STEP, TABLES):
            items = []
            for which, table in enumerate(tables):
                s = i * SLOTS_PER_STEP + (first + which)
                r = pl.multiple_of(index_ref[0, s], 2)
                w = (ya + yb * value_ref[1, 0, s]) * z_hat(pos, value_ref[0, 0, s])
                near = table[pl.ds(r, 8), :] + w * value_ref[3, 0, s]
                far = table[pl.ds(r + plane, 8), :] + w * value_ref[4, 0, s]
                items.append((table, r, near, far))
            for table, r, near, far in items:
                table[pl.ds(r, 8), :] = near
                table[pl.ds(r + plane, 8), :] = far
        return 0

    lax.fori_loop(0, steps, body, 0)

    def combine(i, _):
        part = pl.ds(pl.multiple_of(i * block, block), block)
        total = tables[0][part, :]
        for table in tables[1:]:
            total = total + table[part, :]
        tables[0][part, :] = total
        return 0

    lax.fori_loop(0, rows // block, combine, 0)
    copy = pltpu.make_async_copy(tables[0].at[pl.ds(0, rows), :], out_ref, sem)
    copy.start()
    copy.wait()


def spread(index, value, span):
    rows = span[0] * span[1] * 2
    return pl.pallas_call(
        functools.partial(spread_kernel, span[1]),
        out_shape=jax.ShapeDtypeStruct((rows, LANES), F),
        in_specs=[pl.BlockSpec(memory_space=pltpu.SMEM)] * 2,
        out_specs=pl.BlockSpec(memory_space=pl.ANY),
        scratch_shapes=[pltpu.VMEM((rows + 8, LANES), F)] * TABLES + [pltpu.SemaphoreType.DMA(())],
        compiler_params=pltpu.CompilerParams(vmem_limit_bytes=56 << 20),
        name="spread",
    )(index, value)


def sample_kernel(
    span_y, index_ref, value_ref, rows_ref, grid_ref, field_ref, out_ref, table, grid, parts, sums, sems
):
    rows = rows_ref.shape[0]
    load = pltpu.make_async_copy(rows_ref, table.at[pl.ds(8, rows), :], sems.at[1])
    load.start()
    table[pl.ds(0, 8), :] = jnp.zeros((8, LANES), F)
    table[pl.ds(rows + 8, 8), :] = jnp.zeros((8, LANES), F)
    load.wait()
    hold = pltpu.make_async_copy(grid_ref, grid, sems.at[0])
    hold.start()
    row, pos = patterns()
    first_row, second_row = row % 4 < 2, row < 4
    yb = jnp.where(first_row, -1.0, 1.0).astype(F)
    ya = jnp.where(first_row, 1.0, 0.0).astype(F)
    masks = [jnp.where(second_row, 1.0, 0.0).astype(F), jnp.where(second_row, 0.0, 1.0).astype(F)]
    weights = [(ya * mask, yb * mask) for mask in masks]
    plane = 2 * span_y
    keep = pltpu.make_async_copy(grid, field_ref, sems.at[2])

    steps = index_ref.shape[1] // SLOTS_PER_STEP

    def body(i, _):
        for pair in range(SLOTS_PER_STEP // 2):
            total = None
            for which in (0, 1):
                s = i * SLOTS_PER_STEP + (2 * pair + which)
                r = pl.multiple_of(index_ref[0, s], 2) + (8 - 4 * which)
                wa, wb = weights[which]
                w = (wa + wb * value_ref[1, 0, s]) * z_hat(pos, value_ref[0, 0, s])
                near, far = table[pl.ds(r, 8), :], table[pl.ds(r + plane, 8), :]
                term = w * (near + value_ref[2, 0, s] * (far - near))
                total = term if total is None else total + term
            start = i * (SLOTS_PER_STEP // 2) + pair
            parts[pl.ds(pl.multiple_of(start * 8, 8), 8), :] = total

        @pl.when(i == steps // 4)
        def _():
            hold.wait()
            keep.start()

        return 0

    lax.fori_loop(0, steps, body, 0)

    def fold(i, _):
        start = pl.multiple_of(i * 256, 256)
        total = parts[pl.ds(start, 64, stride=4), :]
        for j in range(1, 4):
            total = total + parts[pl.ds(start + j, 64, stride=4), :]
        sums[pl.ds(pl.multiple_of(i * 64, 64), 64), :] = total
        return 0

    lax.fori_loop(0, sums.shape[0] // 64, fold, 0)
    out_ref[...] = lax.dot_general(
        jnp.ones((8, LANES), F),
        sums[...],
        (((1,), (1,)), ((), ())),
        precision=lax.Precision.HIGHEST,
        preferred_element_type=F,
    )[0:1]
    keep.wait()


def sample(index, value, rows_field, grid_field):
    span_y, rows = grid_field.shape[1], rows_field.shape[0]
    slots = index.shape[1]
    smem, anywhere = pl.BlockSpec(memory_space=pltpu.SMEM), pl.BlockSpec(memory_space=pl.ANY)
    return pl.pallas_call(
        functools.partial(sample_kernel, span_y),
        out_shape=(
            jax.ShapeDtypeStruct(grid_field.shape, F),
            jax.ShapeDtypeStruct((1, slots), F),
        ),
        in_specs=[smem, smem, anywhere, anywhere],
        out_specs=(anywhere, pl.BlockSpec(memory_space=pltpu.VMEM)),
        scratch_shapes=[
            pltpu.VMEM((rows + 16, LANES), F),
            pltpu.VMEM(grid_field.shape, F),
            pltpu.VMEM((slots * 4, LANES), F),
            pltpu.VMEM((slots, LANES), F),
            pltpu.SemaphoreType.DMA((3,)),
        ],
        compiler_params=pltpu.CompilerParams(vmem_limit_bytes=56 << 20),
        name="sample",
    )(index, value, rows_field, grid_field)


def inverse_of(value):
    guess = pl.reciprocal(value, approx=True)
    return guess * (2.0 - value * guess)


def harmonic(former, latter):
    return (2.0 * former * latter) * inverse_of(former + latter)


def stage_of(axes, sizes, places):
    number, count = 0, 1
    for axis in axes:
        number = number * sizes[axis] + places[axis]
        count *= sizes[axis]
    others = []
    for step in range(1, count):
        target, source, source_number, rest = {}, {}, 0, step
        moves = {}
        for axis in reversed(axes):
            moves[axis], rest = rest % sizes[axis], rest // sizes[axis]
        for axis in axes:
            size, move = sizes[axis], moves[axis]
            if move:
                target[axis] = lax.rem(places[axis] + move, size)
                source[axis] = lax.rem(places[axis] + size - move, size)
            source_number = source_number * size + source.get(axis, places[axis])
        others.append((target, source, source_number))
    return number, others


def krylov_kernel(
    sizes,
    b_ref, eps_ref, pot_ref, ion_ref,
    out_ref, rows_ref,
    e, fx, fy, fz, rd, v0, v1, v2, b, pot, ion, sums,
    y_send, y_recv, z_send, z_recv, z_in, red,
    sem_in, send_sem, recv_sem, red_send, red_recv, sem_out,
):
    span_x, span_y, _ = eps_ref.shape
    places = [lax.axis_index(axis) for axis in AXES]
    lane = lax.broadcasted_iota(jnp.int32, (CHUNK, LANES), 1)
    at_first, at_last, odd = lane == 0, lane == LANES - 1, lane % 2 == 1
    chunks = range(0, span_y, CHUNK)
    body_rows = pl.ds(PAD, span_y)
    fields = (e, v0, v1, v2)
    part = span_x // 2
    fzm = ion

    def plane_of(i):
        return lax.rem(i + START, span_x)

    loads = []
    for n, (src, dst) in enumerate(((eps_ref, e), (pot_ref, pot), (ion_ref, ion))):
        for half in (0, 1):
            place = dst.at[pl.ds(1, span_x), half, body_rows, :] if n == 0 else dst.at[:, half]
            loads.append(
                pltpu.make_async_copy(
                    src.at[:, :, pl.ds(half * LANES, LANES)], place, sem_in.at[2 * n + half]
                )
            )
    loads.append(pltpu.make_async_copy(b_ref, b, sem_in.at[6]))
    loads[0].start()
    loads[1].start()

    zero = jnp.zeros((span_y, LANES), F)
    for field in (e, v0, v1, v2):
        for half in (0, 1):
            for x in (0, span_x + 1):
                field[x, half, body_rows, :] = zero
    for k in range(4):
        for side in (0, 1):
            for which in (0, 1):
                z_recv[k, side, which] = zero
                y_recv[k, side, which] = jnp.zeros((span_x, LANES), F)

    barrier = pltpu.get_barrier_semaphore()
    stages = [stage_of(axes, dict(zip(AXES, sizes)), dict(zip(AXES, places))) for axes in STAGES]
    for _, others in stages:
        for target, _, _ in others:
            pl.semaphore_signal(barrier, inc=1, device_id=target, device_id_type=MESH)

    def halo_copies(k, x_faces, parts):
        pairs, field = [], fields[k]
        for n, (axis, place, size) in enumerate(zip(AXES, places, sizes)):
            if size == 1:
                continue
            for side in ((1,) if k == 3 else (0, 1)):
                ends = []
                if n == 0 and x_faces:
                    src = field.at[span_x if side == 0 else 1, :, body_rows, :]
                    ends.append((0, src, field.at[0 if side == 0 else span_x + 1, :, body_rows, :]))
                if n == 1:
                    for which in parts:
                        rows = pl.ds(pl.multiple_of(which * part, 8), part)
                        src = y_send.at[k, side, :, rows, :]
                        ends.append((1 + which, src, y_recv.at[k, side, :, rows, :]))
                if n == 2:
                    for which in parts:
                        ends.append((3 + which, z_send.at[k, which], z_recv.at[k, side, which]))
                for kind, src, dst in ends:
                    copy = pltpu.make_async_remote_copy(
                        src_ref=src,
                        dst_ref=dst,
                        send_sem=send_sem.at[k, 2 * kind + side],
                        recv_sem=recv_sem.at[k, 2 * kind + side],
                        device_id={axis: place + 1 if side == 0 else place - 1},
                        device_id_type=MESH,
                    )
                    above, below = place < size - 1, place > 0
                    pairs.append((above if side == 0 else below, below if side == 0 else above, copy))
        return pairs

    def send(*exchange):
        for has_target, _, copy in halo_copies(*exchange):
            pl.when(has_target)(copy.start)

    def receive(*exchange):
        for _, has_source, copy in halo_copies(*exchange):
            pl.when(has_source)(copy.wait_recv)

    def sent(*exchange):
        for has_target, _, copy in halo_copies(*exchange):
            pl.when(has_target)(copy.wait_send)

    def eight(body, first):
        for n in range(8):
            body(first + n, 0)
        return 0

    def pack(k, which):
        field = fields[k]

        def rows_of(i, _):
            x = plane_of(i)
            for half in (0, 1):
                y_send[k, 1, half, pl.ds(i, 1), :] = field[x + 1, half, pl.ds(PAD, 1), :]
                y_send[k, 0, half, pl.ds(i, 1), :] = field[
                    x + 1, half, pl.ds(PAD + span_y - 1, 1), :
                ]
            return 0

        def columns_of(i, accs):
            x = plane_of(i)
            out = []
            for t, acc in zip(chunks, accs):
                rows = pl.ds(PAD + t, CHUNK)
                ends = jnp.where(
                    at_first,
                    field[x + 1, 0, rows, :],
                    jnp.where(at_last, field[x + 1, 1, rows, :], 0.0),
                )
                out.append(acc + pltpu.roll(ends, 2 * x, 1))
            return tuple(out)

        first = which * part
        lax.fori_loop(0, part // 8, lambda n, c: eight(rows_of, first + 8 * n), 0)
        empty = tuple(jnp.zeros((CHUNK, LANES), F) for _ in chunks)
        accs = lax.fori_loop(0, part, lambda n, c: columns_of(first + n, c), empty, unroll=8)
        for t, acc in zip(chunks, accs):
            z_send[k, which, pl.ds(t, CHUNK), :] = acc

    def unpack(k, which):
        field = fields[k]

        def rows_of(i, _):
            x = plane_of(i)
            for half in (0, 1):
                field[x + 1, half, pl.ds(PAD - 1, 1), :] = y_recv[k, 0, half, pl.ds(i, 1), :]
                field[x + 1, half, pl.ds(PAD + span_y, 1), :] = y_recv[k, 1, half, pl.ds(i, 1), :]
            return 0

        first = which * part
        lax.fori_loop(0, part // 8, lambda n, c: eight(rows_of, first + 8 * n), 0)
        for t in chunks:
            rows = pl.ds(t, CHUNK)
            low = pltpu.roll(z_recv[k, 0, which, rows, :], 2, 1)
            z_in[which, rows, :] = jnp.where(odd, low, z_recv[k, 1, which, rows, :])

    def z_neighbours(center, outer):
        after = [pltpu.roll(c, LANES - 1, 1) for c in center]
        before = [pltpu.roll(c, 1, 1) for c in center]
        after = [jnp.where(at_last, after[1], after[0]), jnp.where(at_last, outer, after[1])]
        before = [jnp.where(at_first, outer, before[0]), jnp.where(at_first, before[0], before[1])]
        return after, before

    def outer_z(which, t, x):
        return pltpu.roll(z_in[which, pl.ds(t, CHUNK), :], LANES - 1 - 2 * x, 1)

    def both_parts(body, carry, before, after, unroll):
        def one(which, carry):
            before(which)
            carry = lax.fori_loop(
                0, part, lambda n, c: body(which, which * part + n, c), carry, unroll=unroll
            )
            after(which)
            return carry

        return lax.fori_loop(0, 2, one, carry)

    loads[0].wait()
    loads[1].wait()
    for load in loads[2:]:
        load.start()
    pl.semaphore_wait(barrier, sum(len(others) for _, others in stages))
    send(0, True, ())

    def pack_and_send(which, _):
        pack(0, which)
        send(0, False, (which,))
        return 0

    lax.fori_loop(0, 2, pack_and_send, 0)

    for load in loads[2:6]:
        load.wait()

    def screen(x, _):
        for half in (0, 1):
            for t in chunks:
                rows = pl.ds(t, CHUNK)
                up = jnp.exp(pot[x, half, rows, :])
                rd[x, half, rows, :] = ion[x, half, rows, :] * (0.5 * (up + inverse_of(up)))
        return 0

    lax.fori_loop(0, span_x, screen, 0, unroll=2)
    loads[6].wait()

    def x_face(x):
        for half in (0, 1):
            for t in chunks:
                rows = pl.ds(PAD + t, CHUNK)
                fx[x, half, pl.ds(t, CHUNK), :] = harmonic(e[x, half, rows, :], e[x + 1, half, rows, :])

    def faces(which, i, total):
        x = plane_of(i)
        for half in (0, 1):
            fy[x, half, pl.ds(PAD - 1, 1), :] = harmonic(
                e[x + 1, half, pl.ds(PAD - 1, 1), :], e[x + 1, half, pl.ds(PAD, 1), :]
            )
        for t in chunks:
            rows, wide = pl.ds(t, CHUNK), pl.ds(PAD + t, CHUNK)
            center = [e[x + 1, half, wide, :] for half in (0, 1)]
            after, before = z_neighbours(center, outer_z(which, t, x))
            for half in (0, 1):
                c = center[half]
                x_next = harmonic(c, e[x + 2, half, wide, :])
                fx[x + 1, half, rows, :] = x_next
                y_next = harmonic(c, e[x + 1, half, pl.ds(PAD + t + 1, CHUNK), :])
                fy[x, half, wide, :] = y_next
                z_next, z_last = harmonic(c, after[half]), harmonic(c, before[half])
                fz[x, half, rows, :] = z_next
                fzm[x, half, rows, :] = z_last
                diagonal = (
                    x_next + fx[x, half, rows, :]
                    + y_next + fy[x, half, pl.ds(PAD + t - 1, CHUNK), :]
                    + z_next + z_last + rd[x, half, rows, :]
                )
                inverse = inverse_of(diagonal)
                rd[x, half, rows, :] = inverse
                source = b[pl.ds(x * (2 * span_y) + 2 * t + half, CHUNK, stride=2), :]
                value = source * inverse
                v0[x + 1, half, wide, :] = value
                total = total + source * value
        return total

    def ready(k):
        def before(which):
            @pl.when(which == 1)
            def _():
                receive(k, True, ())

            receive(k, False, (which,))
            unpack(k, which)

        return before

    def ready_faces(which):
        ready(0)(which)
        x_face(START * (1 - which))

    def done(k):
        def after(which):
            @pl.when(which == 1)
            def _():
                send(k, True, ())

            pack(k, which)
            send(k, False, (which,))

        return after

    nothing = jnp.zeros((CHUNK, LANES), F)
    sums[0] = both_parts(faces, nothing, ready_faces, done(1), UNROLL_FACES)

    def stencil(k):
        v, result = fields[k], fields[k + 1]

        def apply(which, i, carry):
            first, second = carry
            x = plane_of(i)
            for t in chunks:
                rows, wide = pl.ds(t, CHUNK), pl.ds(PAD + t, CHUNK)
                up, down = pl.ds(PAD + t + 1, CHUNK), pl.ds(PAD + t - 1, CHUNK)
                center = [v[x + 1, half, wide, :] for half in (0, 1)]
                after, before = z_neighbours(center, outer_z(which, t, x))
                for half in (0, 1):
                    image = (
                        fx[x + 1, half, rows, :] * v[x + 2, half, wide, :]
                        + fx[x, half, rows, :] * v[x, half, wide, :]
                        + fy[x, half, wide, :] * v[x + 1, half, up, :]
                        + fy[x, half, down, :] * v[x + 1, half, down, :]
                        + fz[x, half, rows, :] * after[half]
                        + fzm[x, half, rows, :] * before[half]
                    )
                    value = image * rd[x, half, rows, :]
                    result[x + 1, half, wide, :] = value
                    first = first + center[half] * image
                    second = second + image * value
            return first, second

        first, second = both_parts(apply, (nothing, nothing), ready(k), done(k + 1), UNROLL_APPLY)
        sums[2 * k - 1] = first
        sums[2 * k] = second

    stencil(1)
    stencil(2)

    def product(which, i, total):
        x = plane_of(i)
        for t in chunks:
            rows, wide = pl.ds(t, CHUNK), pl.ds(PAD + t, CHUNK)
            center = [v2[x + 1, half, wide, :] for half in (0, 1)]
            after = [pltpu.roll(c, LANES - 1, 1) for c in center]
            after = [
                jnp.where(at_last, after[1], after[0]),
                jnp.where(at_last, outer_z(which, t, x), after[1]),
            ]
            for half in (0, 1):
                image = (
                    fx[x + 1, half, rows, :] * v2[x + 2, half, wide, :]
                    + fy[x, half, wide, :] * v2[x + 1, half, pl.ds(PAD + t + 1, CHUNK), :]
                    + fz[x, half, rows, :] * after[half]
                )
                total = total + center[half] * image
        return total

    sums[5] = 2.0 * both_parts(product, nothing, ready(3), lambda which: None, UNROLL_APPLY)

    row = lax.broadcasted_iota(jnp.int32, (8, LANES), 0)
    mine = jnp.zeros((8, LANES), F)
    for n in range(6):
        folded = jnp.sum(sums[n], axis=0, keepdims=True)
        mine = mine + jnp.where(row == n, folded, 0.0)
    for n, (number, others) in enumerate(stages):
        red[n, number] = mine

        def copy_of(step, device, slot, n=n, number=number):
            return pltpu.make_async_remote_copy(
                src_ref=red.at[n, number],
                dst_ref=red.at[n, slot],
                send_sem=red_send.at[n, step],
                recv_sem=red_recv.at[n, step],
                device_id=device,
                device_id_type=MESH,
            )

        copies = [copy_of(step, target, number) for step, (target, _, _) in enumerate(others)]
        for copy in copies:
            copy.start()
        for step, (_, source, slot) in enumerate(others):
            copy_of(step, source, slot).wait_recv()
        for copy in copies:
            copy.wait_send()
        mine = red[n, 0]
        for other in range(1, len(others) + 1):
            mine = mine + red[n, other]
    totals = jnp.sum(mine, axis=1, keepdims=True)
    m = [totals[n:n + 1] for n in range(6)]
    m = [value / m[0] for value in m]

    h = [m[n] - m[n + 1] for n in range(5)]
    l1, l2 = h[1] / h[0], h[2] / h[0]
    d1 = h[2] - l1 * h[1]
    o1 = h[3] - l1 * h[2]
    l3 = o1 / d1
    d2 = h[4] - l2 * h[2] - l3 * o1
    r1 = m[1] - l1 * m[0]
    r2 = m[2] - l2 * m[0] - l3 * r1
    c2 = r2 / d2
    c1 = r1 / d1 - l3 * c2
    c0 = m[0] / h[0] - l1 * c1 - l2 * c2

    weights = [jnp.broadcast_to(c, (CHUNK, LANES)) for c in (c0, c1, c2)]

    def finish(x, _):
        for half in (0, 1):
            for t in chunks:
                wide = pl.ds(PAD + t, CHUNK)
                value = weights[0] * v0[x + 1, half, wide, :]
                value = value + weights[1] * v1[x + 1, half, wide, :]
                value = value + weights[2] * v2[x + 1, half, wide, :]
                pot[x, half, pl.ds(t, CHUNK), :] = value
                b[pl.ds(x * (2 * span_y) + 2 * t + half, CHUNK, stride=2), :] = value
        return 0

    lax.fori_loop(0, span_x, finish, 0, unroll=2)
    stores = [
        pltpu.make_async_copy(
            pot.at[:, half], out_ref.at[:, :, pl.ds(half * LANES, LANES)], sem_out.at[half]
        )
        for half in (0, 1)
    ]
    stores.append(pltpu.make_async_copy(b, rows_ref, sem_out.at[2]))
    for store in stores:
        store.start()
    for k in range(4):
        sent(k, True, (0, 1))
    for store in stores:
        store.wait()


def krylov(sizes, b, eps, pot, ion):
    span_x, span_y, span_z = eps.shape
    tall = span_y + 2 * PAD
    padded = pltpu.VMEM((span_x + 2, 2, tall, LANES), F)
    plain = pltpu.VMEM((span_x, 2, span_y, LANES), F)
    dma = pltpu.SemaphoreType.DMA
    anywhere = pl.BlockSpec(memory_space=pl.ANY)
    most = max(sizes[1], sizes[0] * sizes[2])
    return pl.pallas_call(
        functools.partial(krylov_kernel, sizes),
        out_shape=(
            jax.ShapeDtypeStruct(eps.shape, F),
            jax.ShapeDtypeStruct(b.shape, F),
        ),
        in_specs=[anywhere] * 4,
        out_specs=(anywhere, anywhere),
        scratch_shapes=[
            padded,
            pltpu.VMEM((span_x + 1, 2, span_y, LANES), F),
            pltpu.VMEM((span_x, 2, tall, LANES), F),
            plain,
            plain,
            padded, padded, padded,
            pltpu.VMEM(b.shape, F),
            plain,
            plain,
            pltpu.VMEM((6, CHUNK, LANES), F),
            pltpu.VMEM((4, 2, 2, span_x, LANES), F),
            pltpu.VMEM((4, 2, 2, span_x, LANES), F),
            pltpu.VMEM((4, 2, span_y, LANES), F),
            pltpu.VMEM((4, 2, 2, span_y, LANES), F),
            pltpu.VMEM((2, span_y, LANES), F),
            pltpu.VMEM((2, most, 8, LANES), F),
            dma((7,)),
            dma((4, 10)),
            dma((4, 10)),
            dma((2, most)),
            dma((2, most)),
            dma((3,)),
        ],
        compiler_params=pltpu.CompilerParams(
            vmem_limit_bytes=60 << 20, collective_id=0, has_side_effects=True
        ),
        name="krylov",
    )(b, eps, pot, ion)


def per_device(
    atom_charge, atom_fraction, atom_corner, block_count, permittivity, base_potential, ion_access
):
    sizes = tuple(lax.axis_size(axis) for axis in AXES)
    index, value = deliver(
        sizes[2], permittivity.shape[1], atom_charge, atom_fraction, atom_corner, block_count
    )
    sources = spread(index, value, permittivity.shape)
    grid_field, rows_field = krylov(sizes, sources, permittivity, base_potential, ion_access)
    solution_field, sampled = sample(index, value, rows_field, grid_field)
    return solution_field, give_back(sizes[2], sampled, block_count)


def solution(mesh):
    in_specs = (
        P("gx", "gy", "gz", None),
        P(None, "gx", "gy", "gz", None),
        P(None, "gx", "gy", "gz", None),
        P("gx", "gy", "gz", None),
        P("gx", "gy", "gz"),
        P("gx", "gy", "gz"),
        P("gx", "gy", "gz"),
    )
    out_specs = (P("gx", "gy", "gz"), P("gx", "gy", "gz", None))
    return jax.shard_map(
        per_device, mesh=mesh, in_specs=in_specs, out_specs=out_specs, check_vma=False
    )
```

```python
import functools

import jax
import jax.numpy as jnp
from jax import lax
from jax.experimental import pallas as pl
from jax.experimental.pallas import tpu as pltpu
from jax.sharding import PartitionSpec as P

F = jnp.float32
AXES = ("gx", "gy", "gz")
STAGES = (("gy",), ("gx", "gz"))
MESH = pl.DeviceIdType.MESH
LANES = 128
PAD = 8
CHUNK = 16
SLOTS_PER_STEP = 32
TABLES = 2
START = 8
UNROLL_FACES = 4
UNROLL_APPLY = 8


def patterns():
    row = lax.broadcasted_iota(jnp.int32, (8, LANES), 0)
    lane = lax.broadcasted_iota(jnp.int32, (8, LANES), 1)
    return row, ((row % 2) * LANES + lane).astype(F)


def z_hat(pos, z):
    return jnp.maximum(1.0 - jnp.abs(pos - z), 0.0)


def greet(axis, size):
    barrier, place = pltpu.get_barrier_semaphore(), lax.axis_index(axis)
    for step in range(1, size):
        pl.semaphore_signal(
            barrier, inc=1, device_id={axis: lax.rem(place + step, size)}, device_id_type=MESH
        )
    pl.semaphore_wait(barrier, size - 1)


def inverse_of(value):
    guess = pl.reciprocal(value, approx=True)
    return guess * (2.0 - value * guess)


def plane_of(i, span_x):
    return lax.rem(i + START, span_x)


def pack_columns(first, count, read, lane, chunks, span_x):
    def columns_of(n, accs):
        x = plane_of(first + n, span_x)
        out = []
        for t, acc in zip(chunks, accs):
            low, high = read(x, t)
            ends = jnp.where(lane == 0, low, jnp.where(lane == LANES - 1, high, 0.0))
            out.append(acc + pltpu.roll(ends, 2 * x, 1))
        return tuple(out)

    empty = tuple(jnp.zeros((CHUNK, LANES), F) for _ in chunks)
    return lax.fori_loop(0, count, columns_of, empty, unroll=8)


def deliver_kernel(
    sizes,
    q_ref, f_ref, c_ref, count_ref, eps_ref, pot_ref, ion_ref,
    index_ref, value_ref, screen_ref, xh_ref, yh_ref, zh_ref,
    q_out, q_in, f_in, c_in, e, pot, ion, y_send, z_send, zeros,
    sem_in, sem_out, sem_zero, send_sem, recv_sem, halo_send, halo_recv,
):
    span_x, span_y, _ = eps_ref.shape
    size = sizes[2]
    places = [lax.axis_index(axis) for axis in AXES]
    place = places[2]
    capacity = q_out.shape[2]
    lane = lax.broadcasted_iota(jnp.int32, (CHUNK, LANES), 1)
    chunks = range(0, span_y, CHUNK)

    loads, pieces = [], [pl.ds(n * (span_x // 4), span_x // 4) for n in range(4)]
    for half in (0, 1):
        lanes = pl.ds(half * LANES, LANES)
        loads.append(pltpu.make_async_copy(eps_ref.at[:, :, lanes], e.at[:, half], sem_in.at[half]))
    for n, piece in enumerate(pieces):
        for m, (src, dst) in enumerate(((pot_ref, pot), (ion_ref, ion))):
            for half in (0, 1):
                lanes = pl.ds(half * LANES, LANES)
                sem = sem_in.at[2 + 4 * n + 2 * m + half]
                loads.append(pltpu.make_async_copy(src.at[piece, :, lanes], dst.at[piece, half], sem))
    for load in loads:
        load.start()

    barrier = pltpu.get_barrier_semaphore()
    greeted = 0
    for axis, own, count in zip(AXES, places, sizes):
        steps = range(1, count) if axis == "gz" else ((1, count - 1) if count > 1 else ())
        for step in steps:
            pl.semaphore_signal(
                barrier, inc=1, device_id={axis: lax.rem(own + step, count)}, device_id_type=MESH
            )
            greeted += 1

    slot = lax.broadcasted_iota(jnp.int32, (1, capacity), 1)
    for g in range(size):
        block = pl.ds(g * capacity, capacity)
        q_out[g] = jnp.where(slot < count_ref[0, 0, 0, g], q_ref[0, 0, :, block], 0.0)
    for half in (0, 1):
        zeros[half] = jnp.zeros((span_y, LANES), F)
    pl.semaphore_wait(barrier, greeted)

    def copies(step, to, source):
        block = pl.ds(pl.multiple_of(to * capacity, capacity), capacity)
        parts = (
            (q_out.at[to], q_in.at[source]),
            (f_ref.at[:, 0, 0, :, block], f_in.at[source]),
            (c_ref.at[:, 0, 0, :, block], c_in.at[source]),
        )
        return [
            pltpu.make_async_remote_copy(
                src_ref=src,
                dst_ref=dst,
                send_sem=send_sem.at[step, n],
                recv_sem=recv_sem.at[step, n],
                device_id={"gz": to},
                device_id_type=MESH,
            )
            for n, (src, dst) in enumerate(parts)
        ]

    out = []
    for step in range(1, size):
        out.extend(copies(step, lax.rem(place + step, size), place))
    for copy in out:
        copy.start()

    loads[0].wait()
    loads[1].wait()
    halos = []
    for n, (axis, own, count) in enumerate(zip(AXES, places, sizes)):
        for side in (0, 1):
            src = (e.at[span_x - 1 if side == 0 else 0], y_send.at[side], z_send)[n]
            dst = (xh_ref, yh_ref, zh_ref)[n].at[side]
            copy = fill = None
            if count > 1:
                copy = pltpu.make_async_remote_copy(
                    src_ref=src,
                    dst_ref=dst,
                    send_sem=halo_send.at[n, side],
                    recv_sem=halo_recv.at[n, side],
                    device_id={axis: own + 1 if side == 0 else own - 1},
                    device_id_type=MESH,
                )
            above, below = own < count - 1, own > 0
            fill = pltpu.make_async_copy(zeros.at[0] if n == 2 else zeros, dst, sem_zero.at[n, side])
            halos.append((n, above if side == 0 else below, below if side == 0 else above, copy, fill))

    def send(axis):
        for n, has_target, has_source, copy, fill in halos:
            if n == axis:
                if copy is not None:
                    pl.when(has_target)(copy.start)
                pl.when(jnp.logical_not(has_source))(fill.start)

    send(0)

    def rows_of(n, _):
        for m in range(8):
            i = 8 * n + m
            x = plane_of(i, span_x)
            for half in (0, 1):
                y_send[1, half, pl.ds(i, 1), :] = e[x, half, pl.ds(0, 1), :]
                y_send[0, half, pl.ds(i, 1), :] = e[x, half, pl.ds(span_y - 1, 1), :]
        return 0

    lax.fori_loop(0, span_x // 8, rows_of, 0)
    send(1)
    accs = pack_columns(
        0, span_x, lambda x, t: [e[x, half, pl.ds(t, CHUNK), :] for half in (0, 1)], lane, chunks, span_x
    )
    for t, acc in zip(chunks, accs):
        z_send[pl.ds(t, CHUNK), :] = acc
    send(2)

    def screen(x, _):
        for half in (0, 1):
            for t in chunks:
                rows = pl.ds(t, CHUNK)
                up = jnp.exp(pot[x, half, rows, :])
                pot[x, half, rows, :] = ion[x, half, rows, :] * (0.5 * (up + inverse_of(up)))
        return 0

    stores = []
    for n, piece in enumerate(pieces):
        for load in loads[2 + 4 * n:6 + 4 * n]:
            load.wait()
        lax.fori_loop(n * (span_x // 4), (n + 1) * (span_x // 4), screen, 0, unroll=4)
        stores.append(pltpu.make_async_copy(pot.at[piece], screen_ref.at[piece], sem_out.at[n]))
        stores[-1].start()

    def work_out(source, q, f, c):
        block = pl.ds(pl.multiple_of(source * capacity, capacity), capacity)
        index_ref[:, block] = (c[0] * span_y + c[1]) * 2
        value_ref[0, :, block] = c[2].astype(F) + f[2]
        value_ref[1, :, block] = f[1]
        value_ref[2, :, block] = f[0]
        value_ref[3, :, block] = q * (1.0 - f[0])
        value_ref[4, :, block] = q * f[0]

    own_block = pl.ds(pl.multiple_of(place * capacity, capacity), capacity)
    work_out(
        place,
        q_out[place],
        [f_ref[k, 0, 0, :, own_block] for k in range(3)],
        [c_ref[k, 0, 0, :, own_block] for k in range(3)],
    )
    for step in range(1, size):
        source = lax.rem(place + size - step, size)
        for copy in copies(step, lax.rem(place + step, size), source):
            copy.wait_recv()
        work_out(
            source,
            q_in[source],
            [f_in[source, k] for k in range(3)],
            [c_in[source, k] for k in range(3)],
        )
    for _, has_target, has_source, copy, fill in halos:
        if copy is not None:
            pl.when(has_source)(copy.wait_recv)
            pl.when(has_target)(copy.wait_send)
        pl.when(jnp.logical_not(has_source))(fill.wait)
    for copy in out:
        copy.wait_send()
    for store in stores:
        store.wait()


def deliver(sizes, charge, fraction, corner, count, eps, pot, ion):
    size = sizes[2]
    capacity = charge.shape[3] // size
    span_x, span_y, _ = eps.shape
    vmem, anywhere = pl.BlockSpec(memory_space=pltpu.VMEM), pl.BlockSpec(memory_space=pl.ANY)
    dma = pltpu.SemaphoreType.DMA
    plain = (span_x, 2, span_y, LANES)
    return pl.pallas_call(
        functools.partial(deliver_kernel, sizes),
        out_shape=(
            jax.ShapeDtypeStruct((1, size * capacity), jnp.int32),
            jax.ShapeDtypeStruct((5, 1, size * capacity), F),
            jax.ShapeDtypeStruct(plain, F),
            jax.ShapeDtypeStruct((2, 2, span_y, LANES), F),
            jax.ShapeDtypeStruct((2, 2, span_x, LANES), F),
            jax.ShapeDtypeStruct((2, span_y, LANES), F),
        ),
        in_specs=[vmem, vmem, vmem, pl.BlockSpec(memory_space=pltpu.SMEM)] + [anywhere] * 3,
        out_specs=(vmem, vmem) + (anywhere,) * 4,
        scratch_shapes=[
            pltpu.VMEM((size, 1, capacity), F),
            pltpu.VMEM((size, 1, capacity), F),
            pltpu.VMEM((size, 3, 1, capacity), F),
            pltpu.VMEM((size, 3, 1, capacity), jnp.int32),
            pltpu.VMEM(plain, F),
            pltpu.VMEM(plain, F),
            pltpu.VMEM(plain, F),
            pltpu.VMEM((2, 2, span_x, LANES), F),
            pltpu.VMEM((span_y, LANES), F),
            pltpu.VMEM((2, span_y, LANES), F),
            dma((18,)),
            dma((4,)),
            dma((3, 2)),
            dma((size, 3)),
            dma((size, 3)),
            dma((3, 2)),
            dma((3, 2)),
        ],
        compiler_params=pltpu.CompilerParams(
            vmem_limit_bytes=60 << 20, collective_id=1, has_side_effects=True
        ),
        name="deliver",
    )(charge, fraction, corner, count, eps, pot, ion)


def give_back_kernel(size, sampled_ref, out_ref, came, send_sem, recv_sem):
    place = lax.axis_index("gz")
    capacity = came.shape[2]
    greet("gz", size)

    def copy_of(step, to, source):
        block = pl.ds(pl.multiple_of(to * capacity, capacity), capacity)
        return pltpu.make_async_remote_copy(
            src_ref=sampled_ref.at[:, block],
            dst_ref=came.at[source],
            send_sem=send_sem.at[step],
            recv_sem=recv_sem.at[step],
            device_id={"gz": to},
            device_id_type=MESH,
        )

    out = [copy_of(step, lax.rem(place + step, size), place) for step in range(1, size)]
    for copy in out:
        copy.start()

    def put(source, values):
        block = pl.ds(pl.multiple_of(source * capacity, capacity), capacity)
        out_ref[:, block] = values

    put(place, sampled_ref[:, pl.ds(pl.multiple_of(place * capacity, capacity), capacity)])
    for step in range(1, size):
        source = lax.rem(place + size - step, size)
        copy_of(step, lax.rem(place + step, size), source).wait_recv()
        put(source, came[source])
    for copy in out:
        copy.wait_send()


def give_back(size, sampled):
    slots = sampled.shape[1]
    vmem = pl.BlockSpec(memory_space=pltpu.VMEM)
    dma = pltpu.SemaphoreType.DMA
    return pl.pallas_call(
        functools.partial(give_back_kernel, size),
        out_shape=jax.ShapeDtypeStruct((1, slots), F),
        in_specs=[vmem],
        out_specs=vmem,
        scratch_shapes=[pltpu.VMEM((size, 1, slots // size), F), dma((size,)), dma((size,))],
        compiler_params=pltpu.CompilerParams(collective_id=2, has_side_effects=True),
        name="give_back",
    )(sampled)


def spread_kernel(span_y, index_ref, value_ref, out_ref, *scratch):
    tables, sem = scratch[:TABLES], scratch[TABLES]
    rows = out_ref.shape[0]
    block = 128

    def clear(i, _):
        for table in tables:
            table[pl.ds(pl.multiple_of(i * block, block), block), :] = jnp.zeros((block, LANES), F)
        return 0

    lax.fori_loop(0, rows // block, clear, 0)
    for table in tables:
        table[pl.ds(rows, 8), :] = jnp.zeros((8, LANES), F)
    row, pos = patterns()
    ya = jnp.where(row < 2, 1.0, 0.0).astype(F)
    yb = jnp.where(row < 2, -1.0, jnp.where(row < 4, 1.0, 0.0)).astype(F)
    plane = 2 * span_y

    steps = index_ref.shape[1] // SLOTS_PER_STEP

    def body(i, _):
        for first in range(0, SLOTS_PER_STEP, TABLES):
            items = []
            for which, table in enumerate(tables):
                s = i * SLOTS_PER_STEP + (first + which)
                r = pl.multiple_of(index_ref[0, s], 2)
                w = (ya + yb * value_ref[1, 0, s]) * z_hat(pos, value_ref[0, 0, s])
                near = table[pl.ds(r, 8), :] + w * value_ref[3, 0, s]
                far = table[pl.ds(r + plane, 8), :] + w * value_ref[4, 0, s]
                items.append((table, r, near, far))
            for table, r, near, far in items:
                table[pl.ds(r, 8), :] = near
                table[pl.ds(r + plane, 8), :] = far
        return 0

    lax.fori_loop(0, steps, body, 0)

    def combine(i, _):
        part = pl.ds(pl.multiple_of(i * block, block), block)
        total = tables[0][part, :]
        for table in tables[1:]:
            total = total + table[part, :]
        tables[0][part, :] = total
        return 0

    pieces, copies = rows // block // 4, []
    for n in range(4):
        lax.fori_loop(n * pieces, (n + 1) * pieces, combine, 0, unroll=2)
        part = pl.ds(n * pieces * block, pieces * block)
        copies.append(pltpu.make_async_copy(tables[0].at[part, :], out_ref.at[part, :], sem.at[n]))
        copies[-1].start()
    for copy in copies:
        copy.wait()


def spread(index, value, span):
    rows = span[0] * span[1] * 2
    return pl.pallas_call(
        functools.partial(spread_kernel, span[1]),
        out_shape=jax.ShapeDtypeStruct((rows, LANES), F),
        in_specs=[pl.BlockSpec(memory_space=pltpu.SMEM)] * 2,
        out_specs=pl.BlockSpec(memory_space=pl.ANY),
        scratch_shapes=[pltpu.VMEM((rows + 8, LANES), F)] * TABLES + [pltpu.SemaphoreType.DMA((4,))],
        compiler_params=pltpu.CompilerParams(vmem_limit_bytes=60 << 20),
        name="spread",
    )(index, value)


def sample_kernel(
    span_y, index_ref, value_ref, rows_ref, field_ref, out_ref, table, grid, parts, sums, sems
):
    rows = rows_ref.shape[0]
    load = pltpu.make_async_copy(rows_ref, table.at[pl.ds(8, rows), :], sems.at[1])
    load.start()
    table[pl.ds(0, 8), :] = jnp.zeros((8, LANES), F)
    table[pl.ds(rows + 8, 8), :] = jnp.zeros((8, LANES), F)
    load.wait()
    row, pos = patterns()
    first_row, second_row = row % 4 < 2, row < 4
    yb = jnp.where(first_row, -1.0, 1.0).astype(F)
    ya = jnp.where(first_row, 1.0, 0.0).astype(F)
    masks = [jnp.where(second_row, 1.0, 0.0).astype(F), jnp.where(second_row, 0.0, 1.0).astype(F)]
    weights = [(ya * mask, yb * mask) for mask in masks]
    plane = 2 * span_y
    span_x = grid.shape[0]
    turn = span_x // (index_ref.shape[1] // SLOTS_PER_STEP)
    halves = [pl.ds(n * (span_x // 2), span_x // 2) for n in (0, 1)]
    keeps = [pltpu.make_async_copy(grid.at[h], field_ref.at[h], sems.at[2 * n]) for n, h in enumerate(halves)]

    steps = index_ref.shape[1] // SLOTS_PER_STEP

    def body(i, _):
        for pair in range(SLOTS_PER_STEP // 2):
            total = None
            for which in (0, 1):
                s = i * SLOTS_PER_STEP + (2 * pair + which)
                r = pl.multiple_of(index_ref[0, s], 2) + (8 - 4 * which)
                wa, wb = weights[which]
                w = (wa + wb * value_ref[1, 0, s]) * z_hat(pos, value_ref[0, 0, s])
                near, far = table[pl.ds(r, 8), :], table[pl.ds(r + plane, 8), :]
                term = w * (near + value_ref[2, 0, s] * (far - near))
                total = term if total is None else total + term
            start = i * (SLOTS_PER_STEP // 2) + pair
            parts[pl.ds(pl.multiple_of(start * 8, 8), 8), :] = total

        for n in range(turn):
            x = i * turn + n
            for half in (0, 1):
                for t in range(0, span_y, CHUNK):
                    place = pl.ds(8 + x * plane + 2 * t + half, CHUNK, stride=2)
                    grid[x, pl.ds(t, CHUNK), half * LANES:(half + 1) * LANES] = table[place, :]

        @pl.when(i == steps // 2)
        def _():
            keeps[0].start()

        return 0

    lax.fori_loop(0, steps, body, 0)
    keeps[1].start()

    def fold(i, _):
        start = pl.multiple_of(i * 256, 256)
        total = parts[pl.ds(start, 64, stride=4), :]
        for j in range(1, 4):
            total = total + parts[pl.ds(start + j, 64, stride=4), :]
        sums[pl.ds(pl.multiple_of(i * 64, 64), 64), :] = total
        return 0

    lax.fori_loop(0, sums.shape[0] // 64, fold, 0)
    out_ref[...] = lax.dot_general(
        jnp.ones((8, LANES), F),
        sums[...],
        (((1,), (1,)), ((), ())),
        precision=lax.Precision.HIGHEST,
        preferred_element_type=F,
    )[0:1]
    for keep in keeps:
        keep.wait()


def sample(index, value, rows_field, span):
    span_y, rows = span[1], rows_field.shape[0]
    slots = index.shape[1]
    smem, anywhere = pl.BlockSpec(memory_space=pltpu.SMEM), pl.BlockSpec(memory_space=pl.ANY)
    return pl.pallas_call(
        functools.partial(sample_kernel, span_y),
        out_shape=(
            jax.ShapeDtypeStruct(span, F),
            jax.ShapeDtypeStruct((1, slots), F),
        ),
        in_specs=[smem, smem, anywhere],
        out_specs=(anywhere, pl.BlockSpec(memory_space=pltpu.VMEM)),
        scratch_shapes=[
            pltpu.VMEM((rows + 16, LANES), F),
            pltpu.VMEM(span, F),
            pltpu.VMEM((slots * 4, LANES), F),
            pltpu.VMEM((slots, LANES), F),
            pltpu.SemaphoreType.DMA((3,)),
        ],
        compiler_params=pltpu.CompilerParams(vmem_limit_bytes=60 << 20),
        name="sample",
    )(index, value, rows_field)


def harmonic(former, latter):
    return (2.0 * former * latter) * inverse_of(former + latter)


def stage_of(axes, sizes, places):
    number, count = 0, 1
    for axis in axes:
        number = number * sizes[axis] + places[axis]
        count *= sizes[axis]
    others = []
    for step in range(1, count):
        target, source, source_number, rest = {}, {}, 0, step
        moves = {}
        for axis in reversed(axes):
            moves[axis], rest = rest % sizes[axis], rest // sizes[axis]
        for axis in axes:
            size, move = sizes[axis], moves[axis]
            if move:
                target[axis] = lax.rem(places[axis] + move, size)
                source[axis] = lax.rem(places[axis] + size - move, size)
            source_number = source_number * size + source.get(axis, places[axis])
        others.append((target, source, source_number))
    return number, others


def krylov_kernel(
    sizes,
    b_ref, eps_ref, screen_ref, xh_ref, yh_ref, zh_ref,
    rows_ref,
    e, fx, fy, fz, fzm, rd, v0, v1, v2, b, sums,
    y_send, y_recv, z_send, z_recv, z_in, red,
    sem_in, send_sem, recv_sem, red_send, red_recv, sem_out,
):
    span_x, span_y, _ = eps_ref.shape
    places = [lax.axis_index(axis) for axis in AXES]
    lane = lax.broadcasted_iota(jnp.int32, (CHUNK, LANES), 1)
    at_first, at_last, odd = lane == 0, lane == LANES - 1, lane % 2 == 1
    chunks = range(0, span_y, CHUNK)
    body_rows = pl.ds(PAD, span_y)
    fields = (e, v0, v1, v2)
    part = span_x // 2

    def load_planes(src, dst, number, first, count, shift):
        out = []
        for start, many in ((first, min(count, span_x - first)), (0, count - min(count, span_x - first))):
            if many:
                out.append((src(start, many), dst(start + shift, many)))
        return [pltpu.make_async_copy(a, b, sem_in.at[number + n]) for n, (a, b) in enumerate(out)]

    tall = 2 * span_y
    loads = []
    for which in (0, 1):
        group = []
        for half in (0, 1):
            group += load_planes(
                lambda a, m: eps_ref.at[pl.ds(a, m), :, pl.ds(half * LANES, LANES)],
                lambda a, m: e.at[pl.ds(a, m), half, body_rows, :],
                12 * which + 2 * half,
                START - 1 if which == 0 else START + part + 1,
                part + 2 if which == 0 else part - 2,
                1,
            )
        group += load_planes(
            lambda a, m: screen_ref.at[pl.ds(a, m)],
            lambda a, m: rd.at[pl.ds(a, m)],
            12 * which + 4,
            START + part * which,
            part,
            0,
        )
        group += load_planes(
            lambda a, m: b_ref.at[pl.ds(a * tall, m * tall), :],
            lambda a, m: b.at[pl.ds(a * tall, m * tall), :],
            12 * which + 6,
            START + part * which,
            part,
            0,
        )
        if which == 0:
            group.append(pltpu.make_async_copy(yh_ref, y_recv.at[0], sem_in.at[8]))
            group.append(pltpu.make_async_copy(zh_ref, z_recv.at[0, :, 0], sem_in.at[9]))
            for side in (0, 1):
                x = span_x + 1 if side else 0
                group.append(
                    pltpu.make_async_copy(xh_ref.at[side], e.at[x, :, body_rows, :], sem_in.at[10 + side])
                )
        loads.append(group)
    for group in loads:
        for load in group:
            load.start()

    zero = jnp.zeros((span_y, LANES), F)
    for field in (v0, v1, v2):
        for half in (0, 1):
            for x in (0, span_x + 1):
                field[x, half, body_rows, :] = zero
    for k in range(1, 4):
        for side in (0, 1):
            for which in (0, 1):
                z_recv[k, side, which] = zero
                y_recv[k, side, which] = jnp.zeros((span_x, LANES), F)

    barrier = pltpu.get_barrier_semaphore()
    stages = [stage_of(axes, dict(zip(AXES, sizes)), dict(zip(AXES, places))) for axes in STAGES]
    for _, others in stages:
        for target, _, _ in others:
            pl.semaphore_signal(barrier, inc=1, device_id=target, device_id_type=MESH)

    def halo_copies(k, x_faces, parts):
        pairs, field = [], fields[k]
        for n, (axis, place, size) in enumerate(zip(AXES, places, sizes)):
            if size == 1:
                continue
            for side in ((1,) if k == 3 else (0, 1)):
                ends = []
                if n == 0 and x_faces:
                    src = field.at[span_x if side == 0 else 1, :, body_rows, :]
                    ends.append((0, src, field.at[0 if side == 0 else span_x + 1, :, body_rows, :]))
                if n == 1:
                    for which in parts:
                        rows = pl.ds(pl.multiple_of(which * part, 8), part)
                        src = y_send.at[k, side, :, rows, :]
                        ends.append((1 + which, src, y_recv.at[k, side, :, rows, :]))
                if n == 2:
                    for which in parts:
                        ends.append((3 + which, z_send.at[k, which], z_recv.at[k, side, which]))
                for kind, src, dst in ends:
                    copy = pltpu.make_async_remote_copy(
                        src_ref=src,
                        dst_ref=dst,
                        send_sem=send_sem.at[k, 2 * kind + side],
                        recv_sem=recv_sem.at[k, 2 * kind + side],
                        device_id={axis: place + 1 if side == 0 else place - 1},
                        device_id_type=MESH,
                    )
                    above, below = place < size - 1, place > 0
                    pairs.append((above if side == 0 else below, below if side == 0 else above, copy))
        return pairs

    def send(*exchange):
        for has_target, _, copy in halo_copies(*exchange):
            pl.when(has_target)(copy.start)

    def receive(*exchange):
        for _, has_source, copy in halo_copies(*exchange):
            pl.when(has_source)(copy.wait_recv)

    def sent(*exchange):
        for has_target, _, copy in halo_copies(*exchange):
            pl.when(has_target)(copy.wait_send)

    def eight(body, first):
        for n in range(8):
            body(first + n, 0)
        return 0

    def pack(k, which):
        field = fields[k]

        def rows_of(i, _):
            x = plane_of(i, span_x)
            for half in (0, 1):
                y_send[k, 1, half, pl.ds(i, 1), :] = field[x + 1, half, pl.ds(PAD, 1), :]
                y_send[k, 0, half, pl.ds(i, 1), :] = field[
                    x + 1, half, pl.ds(PAD + span_y - 1, 1), :
                ]
            return 0

        first = which * part
        lax.fori_loop(0, part // 8, lambda n, c: eight(rows_of, first + 8 * n), 0)
        accs = pack_columns(
            first,
            part,
            lambda x, t: [field[x + 1, half, pl.ds(PAD + t, CHUNK), :] for half in (0, 1)],
            lane,
            chunks,
            span_x,
        )
        for t, acc in zip(chunks, accs):
            z_send[k, which, pl.ds(t, CHUNK), :] = acc

    def unpack(k, which):
        field = fields[k]

        def rows_of(i, _):
            x = plane_of(i, span_x)
            for half in (0, 1):
                field[x + 1, half, pl.ds(PAD - 1, 1), :] = y_recv[k, 0, half, pl.ds(i, 1), :]
                field[x + 1, half, pl.ds(PAD + span_y, 1), :] = y_recv[k, 1, half, pl.ds(i, 1), :]
            return 0

        first = which * part
        lax.fori_loop(0, part // 8, lambda n, c: eight(rows_of, first + 8 * n), 0)
        for t in chunks:
            rows = pl.ds(t, CHUNK)
            held = which if k > 0 else 0
            low = pltpu.roll(z_recv[k, 0, held, rows, :], 2, 1)
            z_in[which, rows, :] = jnp.where(odd, low, z_recv[k, 1, held, rows, :])

    def z_neighbours(center, outer):
        after = [pltpu.roll(c, LANES - 1, 1) for c in center]
        before = [pltpu.roll(c, 1, 1) for c in center]
        after = [jnp.where(at_last, after[1], after[0]), jnp.where(at_last, outer, after[1])]
        before = [jnp.where(at_first, outer, before[0]), jnp.where(at_first, before[0], before[1])]
        return after, before

    def outer_z(which, t, x):
        return pltpu.roll(z_in[which, pl.ds(t, CHUNK), :], LANES - 1 - 2 * x, 1)

    def both_parts(body, carry, before, after, unroll):
        def one(which, carry):
            before(which)
            carry = lax.fori_loop(
                0, part, lambda n, c: body(which, which * part + n, c), carry, unroll=unroll
            )
            after(which)
            return carry

        return lax.fori_loop(0, 2, one, carry)

    def x_face(x):
        for half in (0, 1):
            for t in chunks:
                rows = pl.ds(PAD + t, CHUNK)
                fx[x, half, pl.ds(t, CHUNK), :] = harmonic(e[x, half, rows, :], e[x + 1, half, rows, :])

    def faces(which, i, total):
        x = plane_of(i, span_x)
        for half in (0, 1):
            fy[x, half, pl.ds(PAD - 1, 1), :] = harmonic(
                e[x + 1, half, pl.ds(PAD - 1, 1), :], e[x + 1, half, pl.ds(PAD, 1), :]
            )
        for t in chunks:
            rows, wide = pl.ds(t, CHUNK), pl.ds(PAD + t, CHUNK)
            center = [e[x + 1, half, wide, :] for half in (0, 1)]
            after, before = z_neighbours(center, outer_z(which, t, x))
            for half in (0, 1):
                c = center[half]
                x_next = harmonic(c, e[x + 2, half, wide, :])
                fx[x + 1, half, rows, :] = x_next
                y_next = harmonic(c, e[x + 1, half, pl.ds(PAD + t + 1, CHUNK), :])
                fy[x, half, wide, :] = y_next
                z_next, z_last = harmonic(c, after[half]), harmonic(c, before[half])
                fz[x, half, rows, :] = z_next
                fzm[x, half, rows, :] = z_last
                diagonal = (
                    x_next + fx[x, half, rows, :]
                    + y_next + fy[x, half, pl.ds(PAD + t - 1, CHUNK), :]
                    + z_next + z_last + rd[x, half, rows, :]
                )
                inverse = inverse_of(diagonal)
                rd[x, half, rows, :] = inverse
                source = b[pl.ds(x * (2 * span_y) + 2 * t + half, CHUNK, stride=2), :]
                value = source * inverse
                v0[x + 1, half, wide, :] = value
                total = total + source * value
        return total

    def ready(k):
        def before(which):
            @pl.when(which == 1)
            def _():
                receive(k, True, ())

            receive(k, False, (which,))
            unpack(k, which)

        return before

    def ready_faces(which):
        for n in (0, 1):

            @pl.when(which == n)
            def _():
                for load in loads[n]:
                    load.wait()

        unpack(0, which)
        x_face(START * (1 - which))

    def done(k):
        def after(which):
            if k == 1:

                @pl.when(which == 0)
                def _():
                    pl.semaphore_wait(barrier, sum(len(others) for _, others in stages))

            @pl.when(which == 1)
            def _():
                send(k, True, ())

            pack(k, which)
            send(k, False, (which,))

        return after

    nothing = jnp.zeros((CHUNK, LANES), F)
    sums[0] = both_parts(faces, nothing, ready_faces, done(1), UNROLL_FACES)

    def stencil(k):
        v, result = fields[k], fields[k + 1]

        def apply(which, i, carry):
            first, second = carry
            x = plane_of(i, span_x)
            for t in chunks:
                rows, wide = pl.ds(t, CHUNK), pl.ds(PAD + t, CHUNK)
                up, down = pl.ds(PAD + t + 1, CHUNK), pl.ds(PAD + t - 1, CHUNK)
                center = [v[x + 1, half, wide, :] for half in (0, 1)]
                after, before = z_neighbours(center, outer_z(which, t, x))
                for half in (0, 1):
                    image = (
                        fx[x + 1, half, rows, :] * v[x + 2, half, wide, :]
                        + fx[x, half, rows, :] * v[x, half, wide, :]
                        + fy[x, half, wide, :] * v[x + 1, half, up, :]
                        + fy[x, half, down, :] * v[x + 1, half, down, :]
                        + fz[x, half, rows, :] * after[half]
                        + fzm[x, half, rows, :] * before[half]
                    )
                    value = image * rd[x, half, rows, :]
                    result[x + 1, half, wide, :] = value
                    first = first + center[half] * image
                    second = second + image * value
            return first, second

        first, second = both_parts(apply, (nothing, nothing), ready(k), done(k + 1), UNROLL_APPLY)
        sums[2 * k - 1] = first
        sums[2 * k] = second

    stencil(1)
    stencil(2)

    def product(which, i, total):
        x = plane_of(i, span_x)
        for t in chunks:
            rows, wide = pl.ds(t, CHUNK), pl.ds(PAD + t, CHUNK)
            center = [v2[x + 1, half, wide, :] for half in (0, 1)]
            after = [pltpu.roll(c, LANES - 1, 1) for c in center]
            after = [
                jnp.where(at_last, after[1], after[0]),
                jnp.where(at_last, outer_z(which, t, x), after[1]),
            ]
            for half in (0, 1):
                image = (
                    fx[x + 1, half, rows, :] * v2[x + 2, half, wide, :]
                    + fy[x, half, wide, :] * v2[x + 1, half, pl.ds(PAD + t + 1, CHUNK), :]
                    + fz[x, half, rows, :] * after[half]
                )
                total = total + center[half] * image
        return total

    sums[5] = 2.0 * both_parts(product, nothing, ready(3), lambda which: None, UNROLL_APPLY)

    row = lax.broadcasted_iota(jnp.int32, (8, LANES), 0)
    mine = jnp.zeros((8, LANES), F)
    for n in range(6):
        folded = jnp.sum(sums[n], axis=0, keepdims=True)
        mine = mine + jnp.where(row == n, folded, 0.0)
    for n, (number, others) in enumerate(stages):
        red[n, number] = mine

        def copy_of(step, device, slot, n=n, number=number):
            return pltpu.make_async_remote_copy(
                src_ref=red.at[n, number],
                dst_ref=red.at[n, slot],
                send_sem=red_send.at[n, step],
                recv_sem=red_recv.at[n, step],
                device_id=device,
                device_id_type=MESH,
            )

        copies = [copy_of(step, target, number) for step, (target, _, _) in enumerate(others)]
        for copy in copies:
            copy.start()
        for step, (_, source, slot) in enumerate(others):
            copy_of(step, source, slot).wait_recv()
        for copy in copies:
            copy.wait_send()
        mine = red[n, 0]
        for other in range(1, len(others) + 1):
            mine = mine + red[n, other]
    totals = jnp.sum(mine, axis=1, keepdims=True)
    m = [totals[n:n + 1] for n in range(6)]
    m = [value / m[0] for value in m]

    h = [m[n] - m[n + 1] for n in range(5)]
    l1, l2 = h[1] / h[0], h[2] / h[0]
    d1 = h[2] - l1 * h[1]
    o1 = h[3] - l1 * h[2]
    l3 = o1 / d1
    d2 = h[4] - l2 * h[2] - l3 * o1
    r1 = m[1] - l1 * m[0]
    r2 = m[2] - l2 * m[0] - l3 * r1
    c2 = r2 / d2
    c1 = r1 / d1 - l3 * c2
    c0 = m[0] / h[0] - l1 * c1 - l2 * c2

    weights = [jnp.broadcast_to(c, (CHUNK, LANES)) for c in (c0, c1, c2)]

    def finish(x, _):
        for half in (0, 1):
            for t in chunks:
                wide = pl.ds(PAD + t, CHUNK)
                value = weights[0] * v0[x + 1, half, wide, :]
                value = value + weights[1] * v1[x + 1, half, wide, :]
                value = value + weights[2] * v2[x + 1, half, wide, :]
                b[pl.ds(x * (2 * span_y) + 2 * t + half, CHUNK, stride=2), :] = value
        return 0

    stores, some = [], span_x // 4
    for n in range(4):
        lax.fori_loop(n * some, (n + 1) * some, finish, 0, unroll=2)
        rows = pl.ds(n * some * tall, some * tall)
        stores.append(pltpu.make_async_copy(b.at[rows, :], rows_ref.at[rows, :], sem_out.at[n]))
        stores[-1].start()
    for k in range(1, 4):
        sent(k, True, (0, 1))
    for store in stores:
        store.wait()


def krylov(sizes, b, eps, screen, x_halo, y_halo, z_halo):
    span_x, span_y, span_z = eps.shape
    tall = span_y + 2 * PAD
    padded = pltpu.VMEM((span_x + 2, 2, tall, LANES), F)
    plain = pltpu.VMEM((span_x, 2, span_y, LANES), F)
    dma = pltpu.SemaphoreType.DMA
    anywhere = pl.BlockSpec(memory_space=pl.ANY)
    most = max(sizes[1], sizes[0] * sizes[2])
    return pl.pallas_call(
        functools.partial(krylov_kernel, sizes),
        out_shape=jax.ShapeDtypeStruct(b.shape, F),
        in_specs=[anywhere] * 6,
        out_specs=anywhere,
        scratch_shapes=[
            padded,
            pltpu.VMEM((span_x + 1, 2, span_y, LANES), F),
            pltpu.VMEM((span_x, 2, tall, LANES), F),
            plain,
            plain,
            plain,
            padded, padded, padded,
            pltpu.VMEM(b.shape, F),
            pltpu.VMEM((6, CHUNK, LANES), F),
            pltpu.VMEM((4, 2, 2, span_x, LANES), F),
            pltpu.VMEM((4, 2, 2, span_x, LANES), F),
            pltpu.VMEM((4, 2, span_y, LANES), F),
            pltpu.VMEM((4, 2, 2, span_y, LANES), F),
            pltpu.VMEM((2, span_y, LANES), F),
            pltpu.VMEM((2, most, 8, LANES), F),
            dma((24,)),
            dma((4, 10)),
            dma((4, 10)),
            dma((2, most)),
            dma((2, most)),
            dma((4,)),
        ],
        compiler_params=pltpu.CompilerParams(
            vmem_limit_bytes=60 << 20, collective_id=0, has_side_effects=True
        ),
        name="krylov",
    )(b, eps, screen, x_halo, y_halo, z_halo)


def per_device(
    atom_charge, atom_fraction, atom_corner, block_count, permittivity, base_potential, ion_access
):
    sizes = tuple(lax.axis_size(axis) for axis in AXES)
    slots = atom_charge.shape[3]
    index, value, screen, *halos = deliver(
        sizes,
        atom_charge, atom_fraction, atom_corner, block_count,
        permittivity, base_potential, ion_access,
    )
    sources = spread(index, value, permittivity.shape)
    rows_field = krylov(sizes, sources, permittivity, screen, *halos)
    solution_field, sampled = sample(index, value, rows_field, permittivity.shape)
    returned = give_back(sizes[2], sampled).reshape(sizes[2], -1)
    slot = lax.broadcasted_iota(jnp.int32, returned.shape, 1)
    live = slot < block_count.reshape(sizes[2], 1)
    return solution_field, jnp.where(live, returned, 0.0).reshape(1, 1, 1, slots)


def solution(mesh):
    in_specs = (
        P("gx", "gy", "gz", None),
        P(None, "gx", "gy", "gz", None),
        P(None, "gx", "gy", "gz", None),
        P("gx", "gy", "gz", None),
        P("gx", "gy", "gz"),
        P("gx", "gy", "gz"),
        P("gx", "gy", "gz"),
    )
    out_specs = (P("gx", "gy", "gz"), P("gx", "gy", "gz", None))
    return jax.shard_map(
        per_device, mesh=mesh, in_specs=in_specs, out_specs=out_specs, check_vma=False
    )
```

```python
import functools

import jax
import jax.numpy as jnp
from jax import lax
from jax.experimental import pallas as pl
from jax.experimental.pallas import tpu as pltpu
from jax.sharding import PartitionSpec as P

F = jnp.float32
AXES = ("gx", "gy", "gz")
STAGES = (("gy",), ("gx", "gz"))
MESH = pl.DeviceIdType.MESH
LANES = 128
PAD = 8
CHUNK = 16
SLOTS_PER_STEP = 64
TABLES = 2
START = 8
PARTS = 4
UNROLL_FACES = 8
UNROLL_APPLY = 16


def patterns():
    row = lax.broadcasted_iota(jnp.int32, (8, LANES), 0)
    lane = lax.broadcasted_iota(jnp.int32, (8, LANES), 1)
    return row, ((row % 2) * LANES + lane).astype(F)


def z_hat(pos, z):
    return jnp.maximum(1.0 - jnp.abs(pos - z), 0.0)


def greet(axis, size):
    barrier, place = pltpu.get_barrier_semaphore(), lax.axis_index(axis)
    for step in range(1, size):
        pl.semaphore_signal(
            barrier, inc=1, device_id={axis: lax.rem(place + step, size)}, device_id_type=MESH
        )
    pl.semaphore_wait(barrier, size - 1)


def inverse_of(value):
    guess = pl.reciprocal(value, approx=True)
    return guess * (2.0 - value * guess)


def plane_of(i, span_x):
    return lax.rem(i + START, span_x)


def pack_columns(first, count, read, lane, chunks, span_x):
    def columns_of(n, accs):
        x = plane_of(first + n, span_x)
        out = []
        for t, acc in zip(chunks, accs):
            low, high = read(x, t)
            ends = jnp.where(lane == 0, low, jnp.where(lane == LANES - 1, high, 0.0))
            out.append(acc + pltpu.roll(ends, 2 * x, 1))
        return tuple(out)

    empty = tuple(jnp.zeros((CHUNK, LANES), F) for _ in chunks)
    return lax.fori_loop(0, count, columns_of, empty, unroll=8)


def deliver_kernel(
    sizes,
    q_ref, f_ref, c_ref, count_ref, eps_ref, pot_ref, ion_ref,
    index_ref, value_ref, live_ref, screen_ref, xh_ref, yh_ref, zh_ref,
    q_out, q_in, f_in, c_in, e, pot, ion, y_send, z_send, zeros,
    sem_in, sem_out, sem_zero, send_sem, recv_sem, halo_send, halo_recv,
):
    span_x, span_y, _ = eps_ref.shape
    size = sizes[2]
    places = [lax.axis_index(axis) for axis in AXES]
    place = places[2]
    capacity = q_out.shape[2]
    lane = lax.broadcasted_iota(jnp.int32, (CHUNK, LANES), 1)
    chunks = range(0, span_y, CHUNK)

    loads, pieces = [], [pl.ds(n * (span_x // 4), span_x // 4) for n in range(4)]
    for half in (0, 1):
        lanes = pl.ds(half * LANES, LANES)
        loads.append(pltpu.make_async_copy(eps_ref.at[:, :, lanes], e.at[:, half], sem_in.at[half]))
    for n, piece in enumerate(pieces):
        for m, (src, dst) in enumerate(((pot_ref, pot), (ion_ref, ion))):
            for half in (0, 1):
                lanes = pl.ds(half * LANES, LANES)
                sem = sem_in.at[2 + 4 * n + 2 * m + half]
                loads.append(pltpu.make_async_copy(src.at[piece, :, lanes], dst.at[piece, half], sem))
    for load in loads:
        load.start()

    barrier = pltpu.get_barrier_semaphore()
    greeted = 0
    for axis, own, count in zip(AXES, places, sizes):
        steps = range(1, count) if axis == "gz" else ((1, count - 1) if count > 1 else ())
        for step in steps:
            pl.semaphore_signal(
                barrier, inc=1, device_id={axis: lax.rem(own + step, count)}, device_id_type=MESH
            )
            greeted += 1

    slot = lax.broadcasted_iota(jnp.int32, (1, capacity), 1)
    for g in range(size):
        block = pl.ds(g * capacity, capacity)
        live = slot < count_ref[0, 0, 0, g]
        live_ref[:, block] = jnp.where(live, 1.0, 0.0)
        q_out[g] = jnp.where(live, q_ref[0, 0, :, block], 0.0)
    for half in (0, 1):
        zeros[half] = jnp.zeros((span_y, LANES), F)
    pl.semaphore_wait(barrier, greeted)

    def copies(step, to, source):
        block = pl.ds(pl.multiple_of(to * capacity, capacity), capacity)
        parts = (
            (q_out.at[to], q_in.at[source]),
            (f_ref.at[:, 0, 0, :, block], f_in.at[source]),
            (c_ref.at[:, 0, 0, :, block], c_in.at[source]),
        )
        return [
            pltpu.make_async_remote_copy(
                src_ref=src,
                dst_ref=dst,
                send_sem=send_sem.at[step, n],
                recv_sem=recv_sem.at[step, n],
                device_id={"gz": to},
                device_id_type=MESH,
            )
            for n, (src, dst) in enumerate(parts)
        ]

    out = []
    for step in range(1, size):
        out.extend(copies(step, lax.rem(place + step, size), place))
    for copy in out:
        copy.start()

    loads[0].wait()
    loads[1].wait()
    halos = []
    for n, (axis, own, count) in enumerate(zip(AXES, places, sizes)):
        for side in (0, 1):
            src = (e.at[span_x - 1 if side == 0 else 0], y_send.at[side], z_send)[n]
            dst = (xh_ref, yh_ref, zh_ref)[n].at[side]
            copy = fill = None
            if count > 1:
                copy = pltpu.make_async_remote_copy(
                    src_ref=src,
                    dst_ref=dst,
                    send_sem=halo_send.at[n, side],
                    recv_sem=halo_recv.at[n, side],
                    device_id={axis: own + 1 if side == 0 else own - 1},
                    device_id_type=MESH,
                )
            above, below = own < count - 1, own > 0
            fill = pltpu.make_async_copy(zeros.at[0] if n == 2 else zeros, dst, sem_zero.at[n, side])
            halos.append((n, above if side == 0 else below, below if side == 0 else above, copy, fill))

    def send(axis):
        for n, has_target, has_source, copy, fill in halos:
            if n == axis:
                if copy is not None:
                    pl.when(has_target)(copy.start)
                pl.when(jnp.logical_not(has_source))(fill.start)

    send(0)

    def rows_of(n, _):
        for m in range(8):
            i = 8 * n + m
            x = plane_of(i, span_x)
            for half in (0, 1):
                y_send[1, half, pl.ds(i, 1), :] = e[x, half, pl.ds(0, 1), :]
                y_send[0, half, pl.ds(i, 1), :] = e[x, half, pl.ds(span_y - 1, 1), :]
        return 0

    lax.fori_loop(0, span_x // 8, rows_of, 0)
    send(1)
    accs = pack_columns(
        0, span_x, lambda x, t: [e[x, half, pl.ds(t, CHUNK), :] for half in (0, 1)], lane, chunks, span_x
    )
    for t, acc in zip(chunks, accs):
        z_send[pl.ds(t, CHUNK), :] = acc
    send(2)

    def screen(x, _):
        for half in (0, 1):
            for t in chunks:
                rows = pl.ds(t, CHUNK)
                up = jnp.exp(pot[x, half, rows, :])
                pot[x, half, rows, :] = ion[x, half, rows, :] * (0.5 * (up + inverse_of(up)))
        return 0

    stores = []
    for n, piece in enumerate(pieces):
        for load in loads[2 + 4 * n:6 + 4 * n]:
            load.wait()
        lax.fori_loop(n * (span_x // 4), (n + 1) * (span_x // 4), screen, 0, unroll=4)
        stores.append(pltpu.make_async_copy(pot.at[piece], screen_ref.at[piece], sem_out.at[n]))
        stores[-1].start()

    def work_out(source, q, f, c):
        block = pl.ds(pl.multiple_of(source * capacity, capacity), capacity)
        index_ref[:, block] = (c[0] * span_y + c[1]) * 2
        value_ref[0, :, block] = c[2].astype(F) + f[2]
        value_ref[1, :, block] = f[1]
        value_ref[2, :, block] = f[0]
        value_ref[3, :, block] = q * (1.0 - f[0])
        value_ref[4, :, block] = q * f[0]

    own_block = pl.ds(pl.multiple_of(place * capacity, capacity), capacity)
    work_out(
        place,
        q_out[place],
        [f_ref[k, 0, 0, :, own_block] for k in range(3)],
        [c_ref[k, 0, 0, :, own_block] for k in range(3)],
    )
    for step in range(1, size):
        source = lax.rem(place + size - step, size)
        for copy in copies(step, lax.rem(place + step, size), source):
            copy.wait_recv()
        work_out(
            source,
            q_in[source],
            [f_in[source, k] for k in range(3)],
            [c_in[source, k] for k in range(3)],
        )
    for _, has_target, has_source, copy, fill in halos:
        if copy is not None:
            pl.when(has_source)(copy.wait_recv)
            pl.when(has_target)(copy.wait_send)
        pl.when(jnp.logical_not(has_source))(fill.wait)
    for copy in out:
        copy.wait_send()
    for store in stores:
        store.wait()


def deliver(sizes, charge, fraction, corner, count, eps, pot, ion):
    size = sizes[2]
    capacity = charge.shape[3] // size
    span_x, span_y, _ = eps.shape
    vmem, anywhere = pl.BlockSpec(memory_space=pltpu.VMEM), pl.BlockSpec(memory_space=pl.ANY)
    dma = pltpu.SemaphoreType.DMA
    plain = (span_x, 2, span_y, LANES)
    return pl.pallas_call(
        functools.partial(deliver_kernel, sizes),
        out_shape=(
            jax.ShapeDtypeStruct((1, size * capacity), jnp.int32),
            jax.ShapeDtypeStruct((5, 1, size * capacity), F),
            jax.ShapeDtypeStruct((1, size * capacity), F),
            jax.ShapeDtypeStruct(plain, F),
            jax.ShapeDtypeStruct((2, 2, span_y, LANES), F),
            jax.ShapeDtypeStruct((2, 2, span_x, LANES), F),
            jax.ShapeDtypeStruct((2, span_y, LANES), F),
        ),
        in_specs=[vmem, vmem, vmem, pl.BlockSpec(memory_space=pltpu.SMEM)] + [anywhere] * 3,
        out_specs=(vmem,) * 3 + (anywhere,) * 4,
        scratch_shapes=[
            pltpu.VMEM((size, 1, capacity), F),
            pltpu.VMEM((size, 1, capacity), F),
            pltpu.VMEM((size, 3, 1, capacity), F),
            pltpu.VMEM((size, 3, 1, capacity), jnp.int32),
            pltpu.VMEM(plain, F),
            pltpu.VMEM(plain, F),
            pltpu.VMEM(plain, F),
            pltpu.VMEM((2, 2, span_x, LANES), F),
            pltpu.VMEM((span_y, LANES), F),
            pltpu.VMEM((2, span_y, LANES), F),
            dma((18,)),
            dma((4,)),
            dma((3, 2)),
            dma((size, 3)),
            dma((size, 3)),
            dma((3, 2)),
            dma((3, 2)),
        ],
        compiler_params=pltpu.CompilerParams(
            vmem_limit_bytes=60 << 20, collective_id=1, has_side_effects=True
        ),
        name="deliver",
    )(charge, fraction, corner, count, eps, pot, ion)


def give_back_kernel(size, sampled_ref, out_ref, came, send_sem, recv_sem):
    place = lax.axis_index("gz")
    capacity = came.shape[2]
    greet("gz", size)

    def copy_of(step, to, source):
        block = pl.ds(pl.multiple_of(to * capacity, capacity), capacity)
        return pltpu.make_async_remote_copy(
            src_ref=sampled_ref.at[:, block],
            dst_ref=came.at[source],
            send_sem=send_sem.at[step],
            recv_sem=recv_sem.at[step],
            device_id={"gz": to},
            device_id_type=MESH,
        )

    out = [copy_of(step, lax.rem(place + step, size), place) for step in range(1, size)]
    for copy in out:
        copy.start()

    def put(source, values):
        block = pl.ds(pl.multiple_of(source * capacity, capacity), capacity)
        out_ref[:, block] = values

    put(place, sampled_ref[:, pl.ds(pl.multiple_of(place * capacity, capacity), capacity)])
    for step in range(1, size):
        source = lax.rem(place + size - step, size)
        copy_of(step, lax.rem(place + step, size), source).wait_recv()
        put(source, came[source])
    for copy in out:
        copy.wait_send()


def give_back(size, sampled):
    slots = sampled.shape[1]
    vmem = pl.BlockSpec(memory_space=pltpu.VMEM)
    dma = pltpu.SemaphoreType.DMA
    return pl.pallas_call(
        functools.partial(give_back_kernel, size),
        out_shape=jax.ShapeDtypeStruct((1, slots), F),
        in_specs=[vmem],
        out_specs=vmem,
        scratch_shapes=[pltpu.VMEM((size, 1, slots // size), F), dma((size,)), dma((size,))],
        compiler_params=pltpu.CompilerParams(collective_id=2, has_side_effects=True),
        name="give_back",
    )(sampled)


def spread_kernel(span_y, index_ref, value_ref, out_ref, *scratch):
    tables, sem = scratch[:TABLES], scratch[TABLES]
    rows = out_ref.shape[0]
    block = 128

    def clear(i, _):
        for table in tables:
            table[pl.ds(pl.multiple_of(i * block, block), block), :] = jnp.zeros((block, LANES), F)
        return 0

    lax.fori_loop(0, rows // block, clear, 0)
    for table in tables:
        table[pl.ds(rows, 8), :] = jnp.zeros((8, LANES), F)
    row, pos = patterns()
    ya = jnp.where(row < 2, 1.0, 0.0).astype(F)
    yb = jnp.where(row < 2, -1.0, jnp.where(row < 4, 1.0, 0.0)).astype(F)
    plane = 2 * span_y

    steps = index_ref.shape[1] // SLOTS_PER_STEP

    def body(i, _):
        for first in range(0, SLOTS_PER_STEP, TABLES):
            items = []
            for which, table in enumerate(tables):
                s = i * SLOTS_PER_STEP + (first + which)
                r = pl.multiple_of(index_ref[0, s], 2)
                w = (ya + yb * value_ref[1, 0, s]) * z_hat(pos, value_ref[0, 0, s])
                near = table[pl.ds(r, 8), :] + w * value_ref[3, 0, s]
                far = table[pl.ds(r + plane, 8), :] + w * value_ref[4, 0, s]
                items.append((table, r, near, far))
            for table, r, near, far in items:
                table[pl.ds(r, 8), :] = near
                table[pl.ds(r + plane, 8), :] = far
        return 0

    lax.fori_loop(0, steps, body, 0)

    def combine(i, _):
        part = pl.ds(pl.multiple_of(i * block, block), block)
        total = tables[0][part, :]
        for table in tables[1:]:
            total = total + table[part, :]
        tables[0][part, :] = total
        return 0

    pieces, copies = rows // block // 4, []
    for n in range(4):
        lax.fori_loop(n * pieces, (n + 1) * pieces, combine, 0, unroll=2)
        part = pl.ds(n * pieces * block, pieces * block)
        copies.append(pltpu.make_async_copy(tables[0].at[part, :], out_ref.at[part, :], sem.at[n]))
        copies[-1].start()
    for copy in copies:
        copy.wait()


def spread(index, value, span):
    rows = span[0] * span[1] * 2
    return pl.pallas_call(
        functools.partial(spread_kernel, span[1]),
        out_shape=jax.ShapeDtypeStruct((rows, LANES), F),
        in_specs=[pl.BlockSpec(memory_space=pltpu.SMEM)] * 2,
        out_specs=pl.BlockSpec(memory_space=pl.ANY),
        scratch_shapes=[pltpu.VMEM((rows + 8, LANES), F)] * TABLES + [pltpu.SemaphoreType.DMA((4,))],
        compiler_params=pltpu.CompilerParams(vmem_limit_bytes=60 << 20),
        name="spread",
    )(index, value)


def sample_kernel(
    span_y, index_ref, value_ref, rows_ref, field_ref, out_ref, table, grid, parts, sums, sems
):
    rows = rows_ref.shape[0]
    load = pltpu.make_async_copy(rows_ref, table.at[pl.ds(8, rows), :], sems.at[1])
    load.start()
    table[pl.ds(0, 8), :] = jnp.zeros((8, LANES), F)
    table[pl.ds(rows + 8, 8), :] = jnp.zeros((8, LANES), F)
    load.wait()
    row, pos = patterns()
    first_row, second_row = row % 4 < 2, row < 4
    yb = jnp.where(first_row, -1.0, 1.0).astype(F)
    ya = jnp.where(first_row, 1.0, 0.0).astype(F)
    masks = [jnp.where(second_row, 1.0, 0.0).astype(F), jnp.where(second_row, 0.0, 1.0).astype(F)]
    weights = [(ya * mask, yb * mask) for mask in masks]
    plane = 2 * span_y
    span_x = grid.shape[0]
    turn = span_x // (index_ref.shape[1] // SLOTS_PER_STEP)
    halves = [pl.ds(n * (span_x // 2), span_x // 2) for n in (0, 1)]
    keeps = [pltpu.make_async_copy(grid.at[h], field_ref.at[h], sems.at[2 * n]) for n, h in enumerate(halves)]

    steps = index_ref.shape[1] // SLOTS_PER_STEP

    def body(i, _):
        for pair in range(SLOTS_PER_STEP // 2):
            total = None
            for which in (0, 1):
                s = i * SLOTS_PER_STEP + (2 * pair + which)
                r = pl.multiple_of(index_ref[0, s], 2) + (8 - 4 * which)
                wa, wb = weights[which]
                w = (wa + wb * value_ref[1, 0, s]) * z_hat(pos, value_ref[0, 0, s])
                near, far = table[pl.ds(r, 8), :], table[pl.ds(r + plane, 8), :]
                term = w * (near + value_ref[2, 0, s] * (far - near))
                total = term if total is None else total + term
            start = i * (SLOTS_PER_STEP // 2) + pair
            parts[pl.ds(pl.multiple_of(start * 8, 8), 8), :] = total

        for n in range(turn):
            x = i * turn + n
            for half in (0, 1):
                for t in range(0, span_y, CHUNK):
                    place = pl.ds(8 + x * plane + 2 * t + half, CHUNK, stride=2)
                    grid[x, pl.ds(t, CHUNK), half * LANES:(half + 1) * LANES] = table[place, :]

        @pl.when(i == steps // 2)
        def _():
            keeps[0].start()

        return 0

    lax.fori_loop(0, steps, body, 0)
    keeps[1].start()

    def fold(i, _):
        start = pl.multiple_of(i * 256, 256)
        total = parts[pl.ds(start, 64, stride=4), :]
        for j in range(1, 4):
            total = total + parts[pl.ds(start + j, 64, stride=4), :]
        sums[pl.ds(pl.multiple_of(i * 64, 64), 64), :] = total
        return 0

    lax.fori_loop(0, sums.shape[0] // 64, fold, 0)
    out_ref[...] = lax.dot_general(
        jnp.ones((8, LANES), F),
        sums[...],
        (((1,), (1,)), ((), ())),
        precision=lax.Precision.HIGHEST,
        preferred_element_type=F,
    )[0:1]
    for keep in keeps:
        keep.wait()


def sample(index, value, rows_field, span):
    span_y, rows = span[1], rows_field.shape[0]
    slots = index.shape[1]
    smem, anywhere = pl.BlockSpec(memory_space=pltpu.SMEM), pl.BlockSpec(memory_space=pl.ANY)
    return pl.pallas_call(
        functools.partial(sample_kernel, span_y),
        out_shape=(
            jax.ShapeDtypeStruct(span, F),
            jax.ShapeDtypeStruct((1, slots), F),
        ),
        in_specs=[smem, smem, anywhere],
        out_specs=(anywhere, pl.BlockSpec(memory_space=pltpu.VMEM)),
        scratch_shapes=[
            pltpu.VMEM((rows + 16, LANES), F),
            pltpu.VMEM(span, F),
            pltpu.VMEM((slots * 4, LANES), F),
            pltpu.VMEM((slots, LANES), F),
            pltpu.SemaphoreType.DMA((3,)),
        ],
        compiler_params=pltpu.CompilerParams(vmem_limit_bytes=60 << 20),
        name="sample",
    )(index, value, rows_field)


def harmonic(former, latter):
    return (2.0 * former * latter) * inverse_of(former + latter)


def stage_of(axes, sizes, places):
    number, count = 0, 1
    for axis in axes:
        number = number * sizes[axis] + places[axis]
        count *= sizes[axis]
    others = []
    for step in range(1, count):
        target, source, source_number, rest = {}, {}, 0, step
        moves = {}
        for axis in reversed(axes):
            moves[axis], rest = rest % sizes[axis], rest // sizes[axis]
        for axis in axes:
            size, move = sizes[axis], moves[axis]
            if move:
                target[axis] = lax.rem(places[axis] + move, size)
                source[axis] = lax.rem(places[axis] + size - move, size)
            source_number = source_number * size + source.get(axis, places[axis])
        others.append((target, source, source_number))
    return number, others


def krylov_kernel(
    sizes,
    b_ref, eps_ref, screen_ref, xh_ref, yh_ref, zh_ref,
    rows_ref,
    e, fx, fy, fz, fzm, rd, v0, v1, v2, b, sums,
    y_send, y_recv, z_send, z_recv, z_in, red,
    sem_in, send_sem, recv_sem, red_send, red_recv, sem_out,
):
    span_x, span_y, _ = eps_ref.shape
    places = [lax.axis_index(axis) for axis in AXES]
    lane = lax.broadcasted_iota(jnp.int32, (CHUNK, LANES), 1)
    at_first, at_last, odd = lane == 0, lane == LANES - 1, lane % 2 == 1
    chunks = range(0, span_y, CHUNK)
    body_rows = pl.ds(PAD, span_y)
    fields = (e, v0, v1, v2)
    part = span_x // PARTS

    def load_planes(src, dst, number, first, count, shift):
        out = []
        for start, many in ((first, min(count, span_x - first)), (0, count - min(count, span_x - first))):
            if many:
                out.append((src(start, many), dst(start + shift, many)))
        return [pltpu.make_async_copy(a, b, sem_in.at[number + n]) for n, (a, b) in enumerate(out)]

    tall = 2 * span_y
    loads = []
    for which in range(PARTS):
        group, base = [], 8 * which
        last = which == PARTS - 1
        for half in (0, 1):
            group += load_planes(
                lambda a, m: eps_ref.at[pl.ds(a, m), :, pl.ds(half * LANES, LANES)],
                lambda a, m: e.at[pl.ds(a, m), half, body_rows, :],
                base + 2 * half,
                START - 1 if which == 0 else START + part * which + 1,
                part + (2 if which == 0 else -2 if last else 0),
                1,
            )
        group += load_planes(
            lambda a, m: screen_ref.at[pl.ds(a, m)],
            lambda a, m: rd.at[pl.ds(a, m)],
            base + 4,
            START + part * which,
            part,
            0,
        )
        group += load_planes(
            lambda a, m: b_ref.at[pl.ds(a * tall, m * tall), :],
            lambda a, m: b.at[pl.ds(a * tall, m * tall), :],
            base + 6,
            START + part * which,
            part,
            0,
        )
        if which == 0:
            group.append(pltpu.make_async_copy(yh_ref, y_recv.at[0], sem_in.at[8 * PARTS]))
            group.append(pltpu.make_async_copy(zh_ref, z_recv.at[0, :, 0], sem_in.at[8 * PARTS + 1]))
            for side in (0, 1):
                x = span_x + 1 if side else 0
                group.append(
                    pltpu.make_async_copy(xh_ref.at[side], e.at[x, :, body_rows, :], sem_in.at[8 * PARTS + 2 + side])
                )
        loads.append(group)
    for group in loads:
        for load in group:
            load.start()

    zero = jnp.zeros((span_y, LANES), F)
    for field in (v0, v1, v2):
        for half in (0, 1):
            for x in (0, span_x + 1):
                field[x, half, body_rows, :] = zero
    for k in range(1, 4):
        for side in (0, 1):
            for which in range(PARTS):
                z_recv[k, side, which] = zero
            for half in (0, 1):
                y_recv[k, side, half] = jnp.zeros((span_x, LANES), F)

    barrier = pltpu.get_barrier_semaphore()
    stages = [stage_of(axes, dict(zip(AXES, sizes)), dict(zip(AXES, places))) for axes in STAGES]
    for _, others in stages:
        for target, _, _ in others:
            pl.semaphore_signal(barrier, inc=1, device_id=target, device_id_type=MESH)

    def halo_copies(k, x_faces, parts):
        pairs, field = [], fields[k]
        for n, (axis, place, size) in enumerate(zip(AXES, places, sizes)):
            if size == 1:
                continue
            for side in ((1,) if k == 3 else (0, 1)):
                ends = []
                if n == 0 and x_faces:
                    src = field.at[span_x if side == 0 else 1, :, body_rows, :]
                    ends.append((0, src, field.at[0 if side == 0 else span_x + 1, :, body_rows, :]))
                if n == 1:
                    for which in parts:
                        rows = pl.ds(pl.multiple_of(which * part, 8), part)
                        src = y_send.at[k, side, :, rows, :]
                        ends.append((1 + which, src, y_recv.at[k, side, :, rows, :]))
                if n == 2:
                    for which in parts:
                        ends.append((1 + PARTS + which, z_send.at[k, which], z_recv.at[k, side, which]))
                for kind, src, dst in ends:
                    copy = pltpu.make_async_remote_copy(
                        src_ref=src,
                        dst_ref=dst,
                        send_sem=send_sem.at[k, 2 * kind + side],
                        recv_sem=recv_sem.at[k, 2 * kind + side],
                        device_id={axis: place + 1 if side == 0 else place - 1},
                        device_id_type=MESH,
                    )
                    above, below = place < size - 1, place > 0
                    pairs.append((above if side == 0 else below, below if side == 0 else above, copy))
        return pairs

    def send(*exchange):
        for has_target, _, copy in halo_copies(*exchange):
            pl.when(has_target)(copy.start)

    def receive(*exchange):
        for _, has_source, copy in halo_copies(*exchange):
            pl.when(has_source)(copy.wait_recv)

    def sent(*exchange):
        for has_target, _, copy in halo_copies(*exchange):
            pl.when(has_target)(copy.wait_send)

    def eight(body, first):
        for n in range(8):
            body(first + n, 0)
        return 0

    def pack(k, which):
        field = fields[k]

        def rows_of(i, _):
            x = plane_of(i, span_x)
            for half in (0, 1):
                y_send[k, 1, half, pl.ds(i, 1), :] = field[x + 1, half, pl.ds(PAD, 1), :]
                y_send[k, 0, half, pl.ds(i, 1), :] = field[
                    x + 1, half, pl.ds(PAD + span_y - 1, 1), :
                ]
            return 0

        first = which * part
        lax.fori_loop(0, part // 8, lambda n, c: eight(rows_of, first + 8 * n), 0)
        accs = pack_columns(
            first,
            part,
            lambda x, t: [field[x + 1, half, pl.ds(PAD + t, CHUNK), :] for half in (0, 1)],
            lane,
            chunks,
            span_x,
        )
        for t, acc in zip(chunks, accs):
            z_send[k, which, pl.ds(t, CHUNK), :] = acc

    def unpack(k, which):
        field = fields[k]

        def rows_of(i, _):
            x = plane_of(i, span_x)
            for half in (0, 1):
                field[x + 1, half, pl.ds(PAD - 1, 1), :] = y_recv[k, 0, half, pl.ds(i, 1), :]
                field[x + 1, half, pl.ds(PAD + span_y, 1), :] = y_recv[k, 1, half, pl.ds(i, 1), :]
            return 0

        first = which * part
        lax.fori_loop(0, part // 8, lambda n, c: eight(rows_of, first + 8 * n), 0)
        for t in chunks:
            rows = pl.ds(t, CHUNK)
            held = which if k > 0 else 0
            low = pltpu.roll(z_recv[k, 0, held, rows, :], 2, 1)
            z_in[which, rows, :] = jnp.where(odd, low, z_recv[k, 1, held, rows, :])

    def z_neighbours(center, outer):
        after = [pltpu.roll(c, LANES - 1, 1) for c in center]
        before = [pltpu.roll(c, 1, 1) for c in center]
        after = [jnp.where(at_last, after[1], after[0]), jnp.where(at_last, outer, after[1])]
        before = [jnp.where(at_first, outer, before[0]), jnp.where(at_first, before[0], before[1])]
        return after, before

    def outer_z(which, t, x):
        return pltpu.roll(z_in[which, pl.ds(t, CHUNK), :], LANES - 1 - 2 * x, 1)

    def both_parts(body, carry, before, after, unroll):
        def one(which, carry):
            before(which)
            carry = lax.fori_loop(
                0, part, lambda n, c: body(which, which * part + n, c), carry, unroll=unroll
            )
            after(which)
            return carry

        return lax.fori_loop(0, PARTS, one, carry)

    def x_face(x):
        for half in (0, 1):
            for t in chunks:
                rows = pl.ds(PAD + t, CHUNK)
                fx[x, half, pl.ds(t, CHUNK), :] = harmonic(e[x, half, rows, :], e[x + 1, half, rows, :])

    def faces(which, i, total):
        x = plane_of(i, span_x)
        for half in (0, 1):
            fy[x, half, pl.ds(PAD - 1, 1), :] = harmonic(
                e[x + 1, half, pl.ds(PAD - 1, 1), :], e[x + 1, half, pl.ds(PAD, 1), :]
            )
        for t in chunks:
            rows, wide = pl.ds(t, CHUNK), pl.ds(PAD + t, CHUNK)
            center = [e[x + 1, half, wide, :] for half in (0, 1)]
            after, before = z_neighbours(center, outer_z(which, t, x))
            for half in (0, 1):
                c = center[half]
                x_next = harmonic(c, e[x + 2, half, wide, :])
                fx[x + 1, half, rows, :] = x_next
                y_next = harmonic(c, e[x + 1, half, pl.ds(PAD + t + 1, CHUNK), :])
                fy[x, half, wide, :] = y_next
                z_next, z_last = harmonic(c, after[half]), harmonic(c, before[half])
                fz[x, half, rows, :] = z_next
                fzm[x, half, rows, :] = z_last
                diagonal = (
                    x_next + fx[x, half, rows, :]
                    + y_next + fy[x, half, pl.ds(PAD + t - 1, CHUNK), :]
                    + z_next + z_last + rd[x, half, rows, :]
                )
                inverse = inverse_of(diagonal)
                rd[x, half, rows, :] = inverse
                source = b[pl.ds(x * (2 * span_y) + 2 * t + half, CHUNK, stride=2), :]
                value = source * inverse
                v0[x + 1, half, wide, :] = value
                total = total + source * value
        return total

    def ready(k):
        def before(which):
            @pl.when(which == PARTS - 1)
            def _():
                receive(k, True, ())

            receive(k, False, (which,))
            unpack(k, which)

        return before

    def ready_faces(which):
        for n in range(PARTS):

            @pl.when(which == n)
            def _(n=n):
                for load in loads[n]:
                    load.wait()

        unpack(0, which)
        for n, x in ((0, START), (PARTS - 1, 0)):

            @pl.when(which == n)
            def _(x=x):
                x_face(x)

    def done(k):
        def after(which):
            if k == 1:

                @pl.when(which == 0)
                def _():
                    pl.semaphore_wait(barrier, sum(len(others) for _, others in stages))

            @pl.when(which == PARTS - 1)
            def _():
                send(k, True, ())

            pack(k, which)
            send(k, False, (which,))

        return after

    nothing = jnp.zeros((CHUNK, LANES), F)
    sums[0] = both_parts(faces, nothing, ready_faces, done(1), UNROLL_FACES)

    def stencil(k):
        v, result = fields[k], fields[k + 1]

        def apply(which, i, carry):
            first, second = carry
            x = plane_of(i, span_x)
            for t in chunks:
                rows, wide = pl.ds(t, CHUNK), pl.ds(PAD + t, CHUNK)
                up, down = pl.ds(PAD + t + 1, CHUNK), pl.ds(PAD + t - 1, CHUNK)
                center = [v[x + 1, half, wide, :] for half in (0, 1)]
                after, before = z_neighbours(center, outer_z(which, t, x))
                for half in (0, 1):
                    image = (
                        fx[x + 1, half, rows, :] * v[x + 2, half, wide, :]
                        + fx[x, half, rows, :] * v[x, half, wide, :]
                        + fy[x, half, wide, :] * v[x + 1, half, up, :]
                        + fy[x, half, down, :] * v[x + 1, half, down, :]
                        + fz[x, half, rows, :] * after[half]
                        + fzm[x, half, rows, :] * before[half]
                    )
                    value = image * rd[x, half, rows, :]
                    result[x + 1, half, wide, :] = value
                    first = first + center[half] * image
                    second = second + image * value
            return first, second

        first, second = both_parts(apply, (nothing, nothing), ready(k), done(k + 1), UNROLL_APPLY)
        sums[2 * k - 1] = first
        sums[2 * k] = second

    stencil(1)
    stencil(2)

    def product(which, i, total):
        x = plane_of(i, span_x)
        for t in chunks:
            rows, wide = pl.ds(t, CHUNK), pl.ds(PAD + t, CHUNK)
            center = [v2[x + 1, half, wide, :] for half in (0, 1)]
            after = [pltpu.roll(c, LANES - 1, 1) for c in center]
            after = [
                jnp.where(at_last, after[1], after[0]),
                jnp.where(at_last, outer_z(which, t, x), after[1]),
            ]
            for half in (0, 1):
                image = (
                    fx[x + 1, half, rows, :] * v2[x + 2, half, wide, :]
                    + fy[x, half, wide, :] * v2[x + 1, half, pl.ds(PAD + t + 1, CHUNK), :]
                    + fz[x, half, rows, :] * after[half]
                )
                total = total + center[half] * image
        return total

    sums[5] = 2.0 * both_parts(product, nothing, ready(3), lambda which: None, UNROLL_APPLY)

    row = lax.broadcasted_iota(jnp.int32, (8, LANES), 0)
    mine = jnp.zeros((8, LANES), F)
    for n in range(6):
        folded = jnp.sum(sums[n], axis=0, keepdims=True)
        mine = mine + jnp.where(row == n, folded, 0.0)
    pending = []
    for n, (number, others) in enumerate(stages):
        red[n, number] = mine

        def copy_of(step, device, slot, n=n, number=number):
            return pltpu.make_async_remote_copy(
                src_ref=red.at[n, number],
                dst_ref=red.at[n, slot],
                send_sem=red_send.at[n, step],
                recv_sem=red_recv.at[n, step],
                device_id=device,
                device_id_type=MESH,
            )

        copies = [copy_of(step, target, number) for step, (target, _, _) in enumerate(others)]
        for copy in copies:
            copy.start()
        for step, (_, source, slot) in enumerate(others):
            copy_of(step, source, slot).wait_recv()
        pending.extend(copies)
        mine = red[n, 0]
        for other in range(1, len(others) + 1):
            mine = mine + red[n, other]
    totals = jnp.sum(mine, axis=1, keepdims=True)
    m = [totals[n:n + 1] for n in range(6)]
    m = [value / m[0] for value in m]

    h = [m[n] - m[n + 1] for n in range(5)]
    l1, l2 = h[1] / h[0], h[2] / h[0]
    d1 = h[2] - l1 * h[1]
    o1 = h[3] - l1 * h[2]
    l3 = o1 / d1
    d2 = h[4] - l2 * h[2] - l3 * o1
    r1 = m[1] - l1 * m[0]
    r2 = m[2] - l2 * m[0] - l3 * r1
    c2 = r2 / d2
    c1 = r1 / d1 - l3 * c2
    c0 = m[0] / h[0] - l1 * c1 - l2 * c2

    weights = [jnp.broadcast_to(c, (CHUNK, LANES)) for c in (c0, c1, c2)]

    def finish(x, _):
        for half in (0, 1):
            for t in chunks:
                wide = pl.ds(PAD + t, CHUNK)
                value = weights[0] * v0[x + 1, half, wide, :]
                value = value + weights[1] * v1[x + 1, half, wide, :]
                value = value + weights[2] * v2[x + 1, half, wide, :]
                b[pl.ds(x * (2 * span_y) + 2 * t + half, CHUNK, stride=2), :] = value
        return 0

    stores, some = [], span_x // 4
    for n in range(4):
        lax.fori_loop(n * some, (n + 1) * some, finish, 0, unroll=2)
        rows = pl.ds(n * some * tall, some * tall)
        stores.append(pltpu.make_async_copy(b.at[rows, :], rows_ref.at[rows, :], sem_out.at[n]))
        stores[-1].start()
    for k in range(1, 4):
        sent(k, True, range(PARTS))
    for copy in pending:
        copy.wait_send()
    for store in stores:
        store.wait()


def krylov(sizes, b, eps, screen, x_halo, y_halo, z_halo):
    span_x, span_y, span_z = eps.shape
    tall = span_y + 2 * PAD
    padded = pltpu.VMEM((span_x + 2, 2, tall, LANES), F)
    plain = pltpu.VMEM((span_x, 2, span_y, LANES), F)
    dma = pltpu.SemaphoreType.DMA
    anywhere = pl.BlockSpec(memory_space=pl.ANY)
    most = max(sizes[1], sizes[0] * sizes[2])
    return pl.pallas_call(
        functools.partial(krylov_kernel, sizes),
        out_shape=jax.ShapeDtypeStruct(b.shape, F),
        in_specs=[anywhere] * 6,
        out_specs=anywhere,
        scratch_shapes=[
            padded,
            pltpu.VMEM((span_x + 1, 2, span_y, LANES), F),
            pltpu.VMEM((span_x, 2, tall, LANES), F),
            plain,
            plain,
            plain,
            padded, padded, padded,
            pltpu.VMEM(b.shape, F),
            pltpu.VMEM((6, CHUNK, LANES), F),
            pltpu.VMEM((4, 2, 2, span_x, LANES), F),
            pltpu.VMEM((4, 2, 2, span_x, LANES), F),
            pltpu.VMEM((4, PARTS, span_y, LANES), F),
            pltpu.VMEM((4, 2, PARTS, span_y, LANES), F),
            pltpu.VMEM((PARTS, span_y, LANES), F),
            pltpu.VMEM((2, most, 8, LANES), F),
            dma((8 * PARTS + 4,)),
            dma((4, 2 + 4 * PARTS)),
            dma((4, 2 + 4 * PARTS)),
            dma((2, most)),
            dma((2, most)),
            dma((4,)),
        ],
        compiler_params=pltpu.CompilerParams(
            vmem_limit_bytes=60 << 20, collective_id=0, has_side_effects=True
        ),
        name="krylov",
    )(b, eps, screen, x_halo, y_halo, z_halo)


def per_device(
    atom_charge, atom_fraction, atom_corner, block_count, permittivity, base_potential, ion_access
):
    sizes = tuple(lax.axis_size(axis) for axis in AXES)
    slots = atom_charge.shape[3]
    index, value, live, screen, *halos = deliver(
        sizes,
        atom_charge, atom_fraction, atom_corner, block_count,
        permittivity, base_potential, ion_access,
    )
    sources = spread(index, value, permittivity.shape)
    rows_field = krylov(sizes, sources, permittivity, screen, *halos)
    solution_field, sampled = sample(index, value, rows_field, permittivity.shape)
    returned = give_back(sizes[2], sampled)
    return solution_field, jnp.where(live > 0.0, returned, 0.0).reshape(1, 1, 1, slots)


def solution(mesh):
    in_specs = (
        P("gx", "gy", "gz", None),
        P(None, "gx", "gy", "gz", None),
        P(None, "gx", "gy", "gz", None),
        P("gx", "gy", "gz", None),
        P("gx", "gy", "gz"),
        P("gx", "gy", "gz"),
        P("gx", "gy", "gz"),
    )
    out_specs = (P("gx", "gy", "gz"), P("gx", "gy", "gz", None))
    return jax.shard_map(
        per_device, mesh=mesh, in_specs=in_specs, out_specs=out_specs, check_vma=False
    )
```

```python
import functools

import jax
import jax.numpy as jnp
from jax import lax
from jax.experimental import pallas as pl
from jax.experimental.pallas import tpu as pltpu
from jax.sharding import PartitionSpec as P

F = jnp.float32
AXES = ("gx", "gy", "gz")
STAGES = (("gy",), ("gx", "gz"))
MESH = pl.DeviceIdType.MESH
LANES = 128
PAD = 8
CHUNK = 16
SLOTS_PER_STEP = 128
TABLES = 2
START = 8
PARTS = 4
UNROLL_FACES = 8
UNROLL_APPLY = 16


def patterns():
    row = lax.broadcasted_iota(jnp.int32, (8, LANES), 0)
    lane = lax.broadcasted_iota(jnp.int32, (8, LANES), 1)
    return row, ((row % 2) * LANES + lane).astype(F)


def z_hat(pos, z):
    return jnp.maximum(1.0 - jnp.abs(pos - z), 0.0)


def greet(axis, size):
    barrier, place = pltpu.get_barrier_semaphore(), lax.axis_index(axis)
    for step in range(1, size):
        pl.semaphore_signal(
            barrier, inc=1, device_id={axis: lax.rem(place + step, size)}, device_id_type=MESH
        )
    pl.semaphore_wait(barrier, size - 1)


def inverse_of(value):
    guess = pl.reciprocal(value, approx=True)
    return guess * (2.0 - value * guess)


def plane_of(i, span_x):
    return lax.rem(i + START, span_x)


def pack_columns(first, count, read, lane, chunks, span_x):
    def columns_of(n, accs):
        x = plane_of(first + n, span_x)
        out = []
        for t, acc in zip(chunks, accs):
            low, high = read(x, t)
            ends = jnp.where(lane == 0, low, jnp.where(lane == LANES - 1, high, 0.0))
            out.append(acc + pltpu.roll(ends, 2 * x, 1))
        return tuple(out)

    empty = tuple(jnp.zeros((CHUNK, LANES), F) for _ in chunks)
    return lax.fori_loop(0, count, columns_of, empty, unroll=16)


def deliver_kernel(
    sizes,
    q_ref, f_ref, c_ref, count_ref, eps_ref, pot_ref, ion_ref,
    index_ref, value_ref, live_ref, screen_ref, xh_ref, yh_ref, zh_ref,
    q_out, q_in, f_in, c_in, e, pot, ion, y_send, z_send, zeros,
    sem_in, sem_out, sem_zero, send_sem, recv_sem, halo_send, halo_recv,
):
    span_x, span_y, _ = eps_ref.shape
    size = sizes[2]
    places = [lax.axis_index(axis) for axis in AXES]
    place = places[2]
    capacity = q_out.shape[2]
    lane = lax.broadcasted_iota(jnp.int32, (CHUNK, LANES), 1)
    chunks = range(0, span_y, CHUNK)

    loads, pieces = [], [pl.ds(n * (span_x // 4), span_x // 4) for n in range(4)]
    for half in (0, 1):
        lanes = pl.ds(half * LANES, LANES)
        loads.append(pltpu.make_async_copy(eps_ref.at[:, :, lanes], e.at[:, half], sem_in.at[half]))
    for n, piece in enumerate(pieces):
        for m, (src, dst) in enumerate(((pot_ref, pot), (ion_ref, ion))):
            for half in (0, 1):
                lanes = pl.ds(half * LANES, LANES)
                sem = sem_in.at[2 + 4 * n + 2 * m + half]
                loads.append(pltpu.make_async_copy(src.at[piece, :, lanes], dst.at[piece, half], sem))
    for load in loads:
        load.start()

    barrier = pltpu.get_barrier_semaphore()
    greeted = 0
    for axis, own, count in zip(AXES, places, sizes):
        steps = range(1, count) if axis == "gz" else ((1, count - 1) if count > 1 else ())
        for step in steps:
            pl.semaphore_signal(
                barrier, inc=1, device_id={axis: lax.rem(own + step, count)}, device_id_type=MESH
            )
            greeted += 1

    slot = lax.broadcasted_iota(jnp.int32, (1, capacity), 1)
    for g in range(size):
        block = pl.ds(g * capacity, capacity)
        live = slot < count_ref[0, 0, 0, g]
        live_ref[:, block] = jnp.where(live, 1.0, 0.0)
        q_out[g] = jnp.where(live, q_ref[0, 0, :, block], 0.0)
    for half in (0, 1):
        zeros[half] = jnp.zeros((span_y, LANES), F)
    pl.semaphore_wait(barrier, greeted)

    def copies(step, to, source):
        block = pl.ds(pl.multiple_of(to * capacity, capacity), capacity)
        parts = (
            (q_out.at[to], q_in.at[source]),
            (f_ref.at[:, 0, 0, :, block], f_in.at[source]),
            (c_ref.at[:, 0, 0, :, block], c_in.at[source]),
        )
        return [
            pltpu.make_async_remote_copy(
                src_ref=src,
                dst_ref=dst,
                send_sem=send_sem.at[step, n],
                recv_sem=recv_sem.at[step, n],
                device_id={"gz": to},
                device_id_type=MESH,
            )
            for n, (src, dst) in enumerate(parts)
        ]

    out = []
    for step in range(1, size):
        out.extend(copies(step, lax.rem(place + step, size), place))
    for copy in out:
        copy.start()

    loads[0].wait()
    loads[1].wait()
    halos = []
    for n, (axis, own, count) in enumerate(zip(AXES, places, sizes)):
        for side in (0, 1):
            src = (e.at[span_x - 1 if side == 0 else 0], y_send.at[side], z_send)[n]
            dst = (xh_ref, yh_ref, zh_ref)[n].at[side]
            copy = fill = None
            if count > 1:
                copy = pltpu.make_async_remote_copy(
                    src_ref=src,
                    dst_ref=dst,
                    send_sem=halo_send.at[n, side],
                    recv_sem=halo_recv.at[n, side],
                    device_id={axis: own + 1 if side == 0 else own - 1},
                    device_id_type=MESH,
                )
            above, below = own < count - 1, own > 0
            fill = pltpu.make_async_copy(zeros.at[0] if n == 2 else zeros, dst, sem_zero.at[n, side])
            halos.append((n, above if side == 0 else below, below if side == 0 else above, copy, fill))

    def send(axis):
        for n, has_target, has_source, copy, fill in halos:
            if n == axis:
                if copy is not None:
                    pl.when(has_target)(copy.start)
                pl.when(jnp.logical_not(has_source))(fill.start)

    send(0)

    def rows_of(n, _):
        for m in range(8):
            i = 8 * n + m
            x = plane_of(i, span_x)
            for half in (0, 1):
                y_send[1, half, pl.ds(i, 1), :] = e[x, half, pl.ds(0, 1), :]
                y_send[0, half, pl.ds(i, 1), :] = e[x, half, pl.ds(span_y - 1, 1), :]
        return 0

    lax.fori_loop(0, span_x // 8, rows_of, 0)
    send(1)
    accs = pack_columns(
        0, span_x, lambda x, t: [e[x, half, pl.ds(t, CHUNK), :] for half in (0, 1)], lane, chunks, span_x
    )
    for t, acc in zip(chunks, accs):
        z_send[pl.ds(t, CHUNK), :] = acc
    send(2)

    def screen(x, _):
        for half in (0, 1):
            for t in chunks:
                rows = pl.ds(t, CHUNK)
                up = jnp.exp(pot[x, half, rows, :])
                pot[x, half, rows, :] = ion[x, half, rows, :] * (0.5 * (up + inverse_of(up)))
        return 0

    stores = []
    for n, piece in enumerate(pieces):
        for load in loads[2 + 4 * n:6 + 4 * n]:
            load.wait()
        lax.fori_loop(n * (span_x // 4), (n + 1) * (span_x // 4), screen, 0, unroll=4)
        stores.append(pltpu.make_async_copy(pot.at[piece], screen_ref.at[piece], sem_out.at[n]))
        stores[-1].start()

    def work_out(source, q, f, c):
        block = pl.ds(pl.multiple_of(source * capacity, capacity), capacity)
        index_ref[:, block] = (c[0] * span_y + c[1]) * 2
        value_ref[0, :, block] = c[2].astype(F) + f[2]
        value_ref[1, :, block] = f[1]
        value_ref[2, :, block] = f[0]
        value_ref[3, :, block] = q * (1.0 - f[0])
        value_ref[4, :, block] = q * f[0]

    own_block = pl.ds(pl.multiple_of(place * capacity, capacity), capacity)
    work_out(
        place,
        q_out[place],
        [f_ref[k, 0, 0, :, own_block] for k in range(3)],
        [c_ref[k, 0, 0, :, own_block] for k in range(3)],
    )
    for step in range(1, size):
        source = lax.rem(place + size - step, size)
        for copy in copies(step, lax.rem(place + step, size), source):
            copy.wait_recv()
        work_out(
            source,
            q_in[source],
            [f_in[source, k] for k in range(3)],
            [c_in[source, k] for k in range(3)],
        )
    for _, has_target, has_source, copy, fill in halos:
        if copy is not None:
            pl.when(has_source)(copy.wait_recv)
            pl.when(has_target)(copy.wait_send)
        pl.when(jnp.logical_not(has_source))(fill.wait)
    for copy in out:
        copy.wait_send()
    for store in stores:
        store.wait()


def deliver(sizes, charge, fraction, corner, count, eps, pot, ion):
    size = sizes[2]
    capacity = charge.shape[3] // size
    span_x, span_y, _ = eps.shape
    vmem, anywhere = pl.BlockSpec(memory_space=pltpu.VMEM), pl.BlockSpec(memory_space=pl.ANY)
    dma = pltpu.SemaphoreType.DMA
    plain = (span_x, 2, span_y, LANES)
    return pl.pallas_call(
        functools.partial(deliver_kernel, sizes),
        out_shape=(
            jax.ShapeDtypeStruct((1, size * capacity), jnp.int32),
            jax.ShapeDtypeStruct((5, 1, size * capacity), F),
            jax.ShapeDtypeStruct((1, size * capacity), F),
            jax.ShapeDtypeStruct(plain, F),
            jax.ShapeDtypeStruct((2, 2, span_y, LANES), F),
            jax.ShapeDtypeStruct((2, 2, span_x, LANES), F),
            jax.ShapeDtypeStruct((2, span_y, LANES), F),
        ),
        in_specs=[vmem, vmem, vmem, pl.BlockSpec(memory_space=pltpu.SMEM)] + [anywhere] * 3,
        out_specs=(vmem,) * 3 + (anywhere,) * 4,
        scratch_shapes=[
            pltpu.VMEM((size, 1, capacity), F),
            pltpu.VMEM((size, 1, capacity), F),
            pltpu.VMEM((size, 3, 1, capacity), F),
            pltpu.VMEM((size, 3, 1, capacity), jnp.int32),
            pltpu.VMEM(plain, F),
            pltpu.VMEM(plain, F),
            pltpu.VMEM(plain, F),
            pltpu.VMEM((2, 2, span_x, LANES), F),
            pltpu.VMEM((span_y, LANES), F),
            pltpu.VMEM((2, span_y, LANES), F),
            dma((18,)),
            dma((4,)),
            dma((3, 2)),
            dma((size, 3)),
            dma((size, 3)),
            dma((3, 2)),
            dma((3, 2)),
        ],
        compiler_params=pltpu.CompilerParams(
            vmem_limit_bytes=60 << 20, collective_id=1, has_side_effects=True
        ),
        name="deliver",
    )(charge, fraction, corner, count, eps, pot, ion)


def give_back_kernel(size, sampled_ref, out_ref, came, send_sem, recv_sem):
    place = lax.axis_index("gz")
    capacity = came.shape[2]
    greet("gz", size)

    def copy_of(step, to, source):
        block = pl.ds(pl.multiple_of(to * capacity, capacity), capacity)
        return pltpu.make_async_remote_copy(
            src_ref=sampled_ref.at[:, block],
            dst_ref=came.at[source],
            send_sem=send_sem.at[step],
            recv_sem=recv_sem.at[step],
            device_id={"gz": to},
            device_id_type=MESH,
        )

    out = [copy_of(step, lax.rem(place + step, size), place) for step in range(1, size)]
    for copy in out:
        copy.start()

    def put(source, values):
        block = pl.ds(pl.multiple_of(source * capacity, capacity), capacity)
        out_ref[:, block] = values

    put(place, sampled_ref[:, pl.ds(pl.multiple_of(place * capacity, capacity), capacity)])
    for step in range(1, size):
        source = lax.rem(place + size - step, size)
        copy_of(step, lax.rem(place + step, size), source).wait_recv()
        put(source, came[source])
    for copy in out:
        copy.wait_send()


def give_back(size, sampled):
    slots = sampled.shape[1]
    vmem = pl.BlockSpec(memory_space=pltpu.VMEM)
    dma = pltpu.SemaphoreType.DMA
    return pl.pallas_call(
        functools.partial(give_back_kernel, size),
        out_shape=jax.ShapeDtypeStruct((1, slots), F),
        in_specs=[vmem],
        out_specs=vmem,
        scratch_shapes=[pltpu.VMEM((size, 1, slots // size), F), dma((size,)), dma((size,))],
        compiler_params=pltpu.CompilerParams(collective_id=2, has_side_effects=True),
        name="give_back",
    )(sampled)


def spread_kernel(span_y, index_ref, value_ref, out_ref, *scratch):
    tables, sem = scratch[:TABLES], scratch[TABLES]
    rows = out_ref.shape[0]
    block = 128

    def clear(i, _):
        for table in tables:
            table[pl.ds(pl.multiple_of(i * block, block), block), :] = jnp.zeros((block, LANES), F)
        return 0

    lax.fori_loop(0, rows // block, clear, 0)
    for table in tables:
        table[pl.ds(rows, 8), :] = jnp.zeros((8, LANES), F)
    row, pos = patterns()
    ya = jnp.where(row < 2, 1.0, 0.0).astype(F)
    yb = jnp.where(row < 2, -1.0, jnp.where(row < 4, 1.0, 0.0)).astype(F)
    plane = 2 * span_y

    steps = index_ref.shape[1] // SLOTS_PER_STEP

    def body(i, _):
        for first in range(0, SLOTS_PER_STEP, TABLES):
            items = []
            for which, table in enumerate(tables):
                s = i * SLOTS_PER_STEP + (first + which)
                r = pl.multiple_of(index_ref[0, s], 2)
                w = (ya + yb * value_ref[1, 0, s]) * z_hat(pos, value_ref[0, 0, s])
                near = table[pl.ds(r, 8), :] + w * value_ref[3, 0, s]
                far = table[pl.ds(r + plane, 8), :] + w * value_ref[4, 0, s]
                items.append((table, r, near, far))
            for table, r, near, far in items:
                table[pl.ds(r, 8), :] = near
                table[pl.ds(r + plane, 8), :] = far
        return 0

    lax.fori_loop(0, steps, body, 0)

    def combine(i, _):
        part = pl.ds(pl.multiple_of(i * block, block), block)
        total = tables[0][part, :]
        for table in tables[1:]:
            total = total + table[part, :]
        tables[0][part, :] = total
        return 0

    pieces, copies = rows // block // 4, []
    for n in range(4):
        lax.fori_loop(n * pieces, (n + 1) * pieces, combine, 0, unroll=2)
        part = pl.ds(n * pieces * block, pieces * block)
        copies.append(pltpu.make_async_copy(tables[0].at[part, :], out_ref.at[part, :], sem.at[n]))
        copies[-1].start()
    for copy in copies:
        copy.wait()


def spread(index, value, span):
    rows = span[0] * span[1] * 2
    return pl.pallas_call(
        functools.partial(spread_kernel, span[1]),
        out_shape=jax.ShapeDtypeStruct((rows, LANES), F),
        in_specs=[pl.BlockSpec(memory_space=pltpu.SMEM)] * 2,
        out_specs=pl.BlockSpec(memory_space=pl.ANY),
        scratch_shapes=[pltpu.VMEM((rows + 8, LANES), F)] * TABLES + [pltpu.SemaphoreType.DMA((4,))],
        compiler_params=pltpu.CompilerParams(vmem_limit_bytes=60 << 20),
        name="spread",
    )(index, value)


def sample_kernel(
    span_y, index_ref, value_ref, rows_ref, field_ref, out_ref, table, grid, parts, sums, sems
):
    rows = rows_ref.shape[0]
    load = pltpu.make_async_copy(rows_ref, table.at[pl.ds(8, rows), :], sems.at[1])
    load.start()
    table[pl.ds(0, 8), :] = jnp.zeros((8, LANES), F)
    table[pl.ds(rows + 8, 8), :] = jnp.zeros((8, LANES), F)
    load.wait()
    row, pos = patterns()
    first_row, second_row = row % 4 < 2, row < 4
    yb = jnp.where(first_row, -1.0, 1.0).astype(F)
    ya = jnp.where(first_row, 1.0, 0.0).astype(F)
    masks = [jnp.where(second_row, 1.0, 0.0).astype(F), jnp.where(second_row, 0.0, 1.0).astype(F)]
    weights = [(ya * mask, yb * mask) for mask in masks]
    plane = 2 * span_y
    span_x = grid.shape[0]
    turn = span_x // (index_ref.shape[1] // SLOTS_PER_STEP)
    halves = [pl.ds(n * (span_x // 2), span_x // 2) for n in (0, 1)]
    keeps = [pltpu.make_async_copy(grid.at[h], field_ref.at[h], sems.at[2 * n]) for n, h in enumerate(halves)]

    steps = index_ref.shape[1] // SLOTS_PER_STEP

    def body(i, _):
        for pair in range(SLOTS_PER_STEP // 2):
            total = None
            for which in (0, 1):
                s = i * SLOTS_PER_STEP + (2 * pair + which)
                r = pl.multiple_of(index_ref[0, s], 2) + (8 - 4 * which)
                wa, wb = weights[which]
                w = (wa + wb * value_ref[1, 0, s]) * z_hat(pos, value_ref[0, 0, s])
                near, far = table[pl.ds(r, 8), :], table[pl.ds(r + plane, 8), :]
                term = w * (near + value_ref[2, 0, s] * (far - near))
                total = term if total is None else total + term
            start = i * (SLOTS_PER_STEP // 2) + pair
            parts[pl.ds(pl.multiple_of(start * 8, 8), 8), :] = total

        for n in range(turn):
            x = i * turn + n
            for half in (0, 1):
                for t in range(0, span_y, CHUNK):
                    place = pl.ds(8 + x * plane + 2 * t + half, CHUNK, stride=2)
                    grid[x, pl.ds(t, CHUNK), half * LANES:(half + 1) * LANES] = table[place, :]

        @pl.when(i == steps // 2)
        def _():
            keeps[0].start()

        return 0

    lax.fori_loop(0, steps, body, 0)
    keeps[1].start()

    def fold(i, _):
        start = pl.multiple_of(i * 256, 256)
        total = parts[pl.ds(start, 64, stride=4), :]
        for j in range(1, 4):
            total = total + parts[pl.ds(start + j, 64, stride=4), :]
        sums[pl.ds(pl.multiple_of(i * 64, 64), 64), :] = total
        return 0

    lax.fori_loop(0, sums.shape[0] // 64, fold, 0)
    out_ref[...] = lax.dot_general(
        jnp.ones((8, LANES), F),
        sums[...],
        (((1,), (1,)), ((), ())),
        precision=lax.Precision.HIGHEST,
        preferred_element_type=F,
    )[0:1]
    for keep in keeps:
        keep.wait()


def sample(index, value, rows_field, span):
    span_y, rows = span[1], rows_field.shape[0]
    slots = index.shape[1]
    smem, anywhere = pl.BlockSpec(memory_space=pltpu.SMEM), pl.BlockSpec(memory_space=pl.ANY)
    return pl.pallas_call(
        functools.partial(sample_kernel, span_y),
        out_shape=(
            jax.ShapeDtypeStruct(span, F),
            jax.ShapeDtypeStruct((1, slots), F),
        ),
        in_specs=[smem, smem, anywhere],
        out_specs=(anywhere, pl.BlockSpec(memory_space=pltpu.VMEM)),
        scratch_shapes=[
            pltpu.VMEM((rows + 16, LANES), F),
            pltpu.VMEM(span, F),
            pltpu.VMEM((slots * 4, LANES), F),
            pltpu.VMEM((slots, LANES), F),
            pltpu.SemaphoreType.DMA((3,)),
        ],
        compiler_params=pltpu.CompilerParams(vmem_limit_bytes=60 << 20),
        name="sample",
    )(index, value, rows_field)


def harmonic(former, latter):
    return (2.0 * former * latter) * inverse_of(former + latter)


def stage_of(axes, sizes, places):
    number, count = 0, 1
    for axis in axes:
        number = number * sizes[axis] + places[axis]
        count *= sizes[axis]
    others = []
    for step in range(1, count):
        target, source, source_number, rest = {}, {}, 0, step
        moves = {}
        for axis in reversed(axes):
            moves[axis], rest = rest % sizes[axis], rest // sizes[axis]
        for axis in axes:
            size, move = sizes[axis], moves[axis]
            if move:
                target[axis] = lax.rem(places[axis] + move, size)
                source[axis] = lax.rem(places[axis] + size - move, size)
            source_number = source_number * size + source.get(axis, places[axis])
        others.append((target, source, source_number))
    return number, others


def krylov_kernel(
    sizes,
    b_ref, eps_ref, screen_ref, xh_ref, yh_ref, zh_ref,
    rows_ref,
    e, fx, fy, fz, fzm, rd, v0, v1, v2, b, sums,
    y_send, y_recv, z_send, z_recv, z_in, red,
    sem_in, send_sem, recv_sem, red_send, red_recv, sem_out,
):
    span_x, span_y, _ = eps_ref.shape
    places = [lax.axis_index(axis) for axis in AXES]
    lane = lax.broadcasted_iota(jnp.int32, (CHUNK, LANES), 1)
    at_first, at_last, odd = lane == 0, lane == LANES - 1, lane % 2 == 1
    chunks = range(0, span_y, CHUNK)
    body_rows = pl.ds(PAD, span_y)
    fields = (e, v0, v1, v2)
    part = span_x // PARTS

    def load_planes(src, dst, number, first, count, shift):
        out = []
        for start, many in ((first, min(count, span_x - first)), (0, count - min(count, span_x - first))):
            if many:
                out.append((src(start, many), dst(start + shift, many)))
        return [pltpu.make_async_copy(a, b, sem_in.at[number + n]) for n, (a, b) in enumerate(out)]

    tall = 2 * span_y
    loads = []
    for which in range(PARTS):
        group, base = [], 8 * which
        last = which == PARTS - 1
        for half in (0, 1):
            group += load_planes(
                lambda a, m: eps_ref.at[pl.ds(a, m), :, pl.ds(half * LANES, LANES)],
                lambda a, m: e.at[pl.ds(a, m), half, body_rows, :],
                base + 2 * half,
                START - 1 if which == 0 else START + part * which + 1,
                part + (2 if which == 0 else -2 if last else 0),
                1,
            )
        group += load_planes(
            lambda a, m: screen_ref.at[pl.ds(a, m)],
            lambda a, m: rd.at[pl.ds(a, m)],
            base + 4,
            START + part * which,
            part,
            0,
        )
        group += load_planes(
            lambda a, m: b_ref.at[pl.ds(a * tall, m * tall), :],
            lambda a, m: b.at[pl.ds(a * tall, m * tall), :],
            base + 6,
            START + part * which,
            part,
            0,
        )
        if which == 0:
            group.append(pltpu.make_async_copy(yh_ref, y_recv.at[0], sem_in.at[8 * PARTS]))
            group.append(pltpu.make_async_copy(zh_ref, z_recv.at[0, :, 0], sem_in.at[8 * PARTS + 1]))
            for side in (0, 1):
                x = span_x + 1 if side else 0
                group.append(
                    pltpu.make_async_copy(xh_ref.at[side], e.at[x, :, body_rows, :], sem_in.at[8 * PARTS + 2 + side])
                )
        loads.append(group)
    for group in loads:
        for load in group:
            load.start()

    zero = jnp.zeros((span_y, LANES), F)
    for field in (v0, v1, v2):
        for half in (0, 1):
            for x in (0, span_x + 1):
                field[x, half, body_rows, :] = zero
    for k in range(1, 4):
        for side in (0, 1):
            for which in range(PARTS):
                z_recv[k, side, which] = zero
            for half in (0, 1):
                y_recv[k, side, half] = jnp.zeros((span_x, LANES), F)

    barrier = pltpu.get_barrier_semaphore()
    stages = [stage_of(axes, dict(zip(AXES, sizes)), dict(zip(AXES, places))) for axes in STAGES]
    for _, others in stages:
        for target, _, _ in others:
            pl.semaphore_signal(barrier, inc=1, device_id=target, device_id_type=MESH)

    def halo_copies(k, x_faces, parts):
        pairs, field = [], fields[k]
        for n, (axis, place, size) in enumerate(zip(AXES, places, sizes)):
            if size == 1:
                continue
            for side in ((1,) if k == 3 else (0, 1)):
                ends = []
                if n == 0 and x_faces:
                    src = field.at[span_x if side == 0 else 1, :, body_rows, :]
                    ends.append((0, src, field.at[0 if side == 0 else span_x + 1, :, body_rows, :]))
                if n == 1:
                    for which in parts:
                        rows = pl.ds(pl.multiple_of(which * part, 8), part)
                        src = y_send.at[k, side, :, rows, :]
                        ends.append((1 + which, src, y_recv.at[k, side, :, rows, :]))
                if n == 2:
                    for which in parts:
                        ends.append((1 + PARTS + which, z_send.at[k, which], z_recv.at[k, side, which]))
                for kind, src, dst in ends:
                    copy = pltpu.make_async_remote_copy(
                        src_ref=src,
                        dst_ref=dst,
                        send_sem=send_sem.at[k, 2 * kind + side],
                        recv_sem=recv_sem.at[k, 2 * kind + side],
                        device_id={axis: place + 1 if side == 0 else place - 1},
                        device_id_type=MESH,
                    )
                    above, below = place < size - 1, place > 0
                    pairs.append((above if side == 0 else below, below if side == 0 else above, copy))
        return pairs

    def send(*exchange):
        for has_target, _, copy in halo_copies(*exchange):
            pl.when(has_target)(copy.start)

    def receive(*exchange):
        for _, has_source, copy in halo_copies(*exchange):
            pl.when(has_source)(copy.wait_recv)

    def sent(*exchange):
        for has_target, _, copy in halo_copies(*exchange):
            pl.when(has_target)(copy.wait_send)

    def eight(body, first):
        for n in range(8):
            body(first + n, 0)
        return 0

    def pack(k, which):
        field = fields[k]

        def rows_of(i, _):
            x = plane_of(i, span_x)
            for half in (0, 1):
                y_send[k, 1, half, pl.ds(i, 1), :] = field[x + 1, half, pl.ds(PAD, 1), :]
                y_send[k, 0, half, pl.ds(i, 1), :] = field[
                    x + 1, half, pl.ds(PAD + span_y - 1, 1), :
                ]
            return 0

        first = which * part
        lax.fori_loop(0, part // 8, lambda n, c: eight(rows_of, first + 8 * n), 0)
        accs = pack_columns(
            first,
            part,
            lambda x, t: [field[x + 1, half, pl.ds(PAD + t, CHUNK), :] for half in (0, 1)],
            lane,
            chunks,
            span_x,
        )
        for t, acc in zip(chunks, accs):
            z_send[k, which, pl.ds(t, CHUNK), :] = acc

    def unpack(k, which):
        field = fields[k]

        def rows_of(i, _):
            x = plane_of(i, span_x)
            for half in (0, 1):
                field[x + 1, half, pl.ds(PAD - 1, 1), :] = y_recv[k, 0, half, pl.ds(i, 1), :]
                field[x + 1, half, pl.ds(PAD + span_y, 1), :] = y_recv[k, 1, half, pl.ds(i, 1), :]
            return 0

        first = which * part
        lax.fori_loop(0, part // 8, lambda n, c: eight(rows_of, first + 8 * n), 0)
        for t in chunks:
            rows = pl.ds(t, CHUNK)
            held = which if k > 0 else 0
            low = pltpu.roll(z_recv[k, 0, held, rows, :], 2, 1)
            z_in[which, rows, :] = jnp.where(odd, low, z_recv[k, 1, held, rows, :])

    def z_neighbours(center, outer):
        after = [pltpu.roll(c, LANES - 1, 1) for c in center]
        before = [pltpu.roll(c, 1, 1) for c in center]
        after = [jnp.where(at_last, after[1], after[0]), jnp.where(at_last, outer, after[1])]
        before = [jnp.where(at_first, outer, before[0]), jnp.where(at_first, before[0], before[1])]
        return after, before

    def outer_z(which, t, x):
        return pltpu.roll(z_in[which, pl.ds(t, CHUNK), :], LANES - 1 - 2 * x, 1)

    def both_parts(body, carry, before, after, unroll):
        def one(which, carry):
            before(which)
            carry = lax.fori_loop(
                0, part, lambda n, c: body(which, which * part + n, c), carry, unroll=unroll
            )
            after(which)
            return carry

        return lax.fori_loop(0, PARTS, one, carry)

    def x_face(x):
        for half in (0, 1):
            for t in chunks:
                rows = pl.ds(PAD + t, CHUNK)
                fx[x, half, pl.ds(t, CHUNK), :] = harmonic(e[x, half, rows, :], e[x + 1, half, rows, :])

    def faces(which, i, total):
        x = plane_of(i, span_x)
        for half in (0, 1):
            fy[x, half, pl.ds(PAD - 1, 1), :] = harmonic(
                e[x + 1, half, pl.ds(PAD - 1, 1), :], e[x + 1, half, pl.ds(PAD, 1), :]
            )
        for t in chunks:
            rows, wide = pl.ds(t, CHUNK), pl.ds(PAD + t, CHUNK)
            center = [e[x + 1, half, wide, :] for half in (0, 1)]
            after, before = z_neighbours(center, outer_z(which, t, x))
            for half in (0, 1):
                c = center[half]
                x_next = harmonic(c, e[x + 2, half, wide, :])
                fx[x + 1, half, rows, :] = x_next
                y_next = harmonic(c, e[x + 1, half, pl.ds(PAD + t + 1, CHUNK), :])
                fy[x, half, wide, :] = y_next
                z_next, z_last = harmonic(c, after[half]), harmonic(c, before[half])
                fz[x, half, rows, :] = z_next
                fzm[x, half, rows, :] = z_last
                diagonal = (
                    x_next + fx[x, half, rows, :]
                    + y_next + fy[x, half, pl.ds(PAD + t - 1, CHUNK), :]
                    + z_next + z_last + rd[x, half, rows, :]
                )
                inverse = inverse_of(diagonal)
                rd[x, half, rows, :] = inverse
                source = b[pl.ds(x * (2 * span_y) + 2 * t + half, CHUNK, stride=2), :]
                value = source * inverse
                v0[x + 1, half, wide, :] = value
                total = total + source * value
        return total

    def ready(k):
        def before(which):
            @pl.when(which == PARTS - 1)
            def _():
                receive(k, True, ())

            receive(k, False, (which,))
            unpack(k, which)

        return before

    def ready_faces(which):
        for n in range(PARTS):

            @pl.when(which == n)
            def _(n=n):
                for load in loads[n]:
                    load.wait()

        unpack(0, which)
        for n, x in ((0, START), (PARTS - 1, 0)):

            @pl.when(which == n)
            def _(x=x):
                x_face(x)

    def done(k):
        def after(which):
            if k == 1:

                @pl.when(which == 0)
                def _():
                    pl.semaphore_wait(barrier, sum(len(others) for _, others in stages))

            @pl.when(which == PARTS - 1)
            def _():
                send(k, True, ())

            pack(k, which)
            send(k, False, (which,))

        return after

    nothing = jnp.zeros((CHUNK, LANES), F)
    sums[0] = both_parts(faces, nothing, ready_faces, done(1), UNROLL_FACES)

    def stencil(k):
        v, result = fields[k], fields[k + 1]

        def apply(which, i, carry):
            first, second = carry
            x = plane_of(i, span_x)
            for t in chunks:
                rows, wide = pl.ds(t, CHUNK), pl.ds(PAD + t, CHUNK)
                up, down = pl.ds(PAD + t + 1, CHUNK), pl.ds(PAD + t - 1, CHUNK)
                center = [v[x + 1, half, wide, :] for half in (0, 1)]
                after, before = z_neighbours(center, outer_z(which, t, x))
                for half in (0, 1):
                    image = (
                        fx[x + 1, half, rows, :] * v[x + 2, half, wide, :]
                        + fx[x, half, rows, :] * v[x, half, wide, :]
                        + fy[x, half, wide, :] * v[x + 1, half, up, :]
                        + fy[x, half, down, :] * v[x + 1, half, down, :]
                        + fz[x, half, rows, :] * after[half]
                        + fzm[x, half, rows, :] * before[half]
                    )
                    value = image * rd[x, half, rows, :]
                    result[x + 1, half, wide, :] = value
                    first = first + center[half] * image
                    second = second + image * value
            return first, second

        first, second = both_parts(apply, (nothing, nothing), ready(k), done(k + 1), UNROLL_APPLY)
        sums[2 * k - 1] = first
        sums[2 * k] = second

    stencil(1)
    stencil(2)

    def product(which, i, total):
        x = plane_of(i, span_x)
        for t in chunks:
            rows, wide = pl.ds(t, CHUNK), pl.ds(PAD + t, CHUNK)
            center = [v2[x + 1, half, wide, :] for half in (0, 1)]
            after = [pltpu.roll(c, LANES - 1, 1) for c in center]
            after = [
                jnp.where(at_last, after[1], after[0]),
                jnp.where(at_last, outer_z(which, t, x), after[1]),
            ]
            for half in (0, 1):
                image = (
                    fx[x + 1, half, rows, :] * v2[x + 2, half, wide, :]
                    + fy[x, half, wide, :] * v2[x + 1, half, pl.ds(PAD + t + 1, CHUNK), :]
                    + fz[x, half, rows, :] * after[half]
                )
                total = total + center[half] * image
        return total

    sums[5] = 2.0 * both_parts(product, nothing, ready(3), lambda which: None, UNROLL_APPLY)

    row = lax.broadcasted_iota(jnp.int32, (8, LANES), 0)
    mine = jnp.zeros((8, LANES), F)
    for n in range(6):
        folded = jnp.sum(sums[n], axis=0, keepdims=True)
        mine = mine + jnp.where(row == n, folded, 0.0)
    pending = []
    for n, (number, others) in enumerate(stages):
        red[n, number] = mine

        def copy_of(step, device, slot, n=n, number=number):
            return pltpu.make_async_remote_copy(
                src_ref=red.at[n, number],
                dst_ref=red.at[n, slot],
                send_sem=red_send.at[n, step],
                recv_sem=red_recv.at[n, step],
                device_id=device,
                device_id_type=MESH,
            )

        copies = [copy_of(step, target, number) for step, (target, _, _) in enumerate(others)]
        for copy in copies:
            copy.start()
        for step, (_, source, slot) in enumerate(others):
            copy_of(step, source, slot).wait_recv()
        pending.extend(copies)
        mine = red[n, 0]
        for other in range(1, len(others) + 1):
            mine = mine + red[n, other]
    totals = jnp.sum(mine, axis=1, keepdims=True)
    m = [totals[n:n + 1] for n in range(6)]
    m = [value / m[0] for value in m]

    h = [m[n] - m[n + 1] for n in range(5)]
    l1, l2 = h[1] / h[0], h[2] / h[0]
    d1 = h[2] - l1 * h[1]
    o1 = h[3] - l1 * h[2]
    l3 = o1 / d1
    d2 = h[4] - l2 * h[2] - l3 * o1
    r1 = m[1] - l1 * m[0]
    r2 = m[2] - l2 * m[0] - l3 * r1
    c2 = r2 / d2
    c1 = r1 / d1 - l3 * c2
    c0 = m[0] / h[0] - l1 * c1 - l2 * c2

    weights = [jnp.broadcast_to(c, (CHUNK, LANES)) for c in (c0, c1, c2)]

    def finish(x, _):
        for half in (0, 1):
            for t in chunks:
                wide = pl.ds(PAD + t, CHUNK)
                value = weights[0] * v0[x + 1, half, wide, :]
                value = value + weights[1] * v1[x + 1, half, wide, :]
                value = value + weights[2] * v2[x + 1, half, wide, :]
                b[pl.ds(x * (2 * span_y) + 2 * t + half, CHUNK, stride=2), :] = value
        return 0

    stores, some = [], span_x // 4
    for n in range(4):
        lax.fori_loop(n * some, (n + 1) * some, finish, 0, unroll=2)
        rows = pl.ds(n * some * tall, some * tall)
        stores.append(pltpu.make_async_copy(b.at[rows, :], rows_ref.at[rows, :], sem_out.at[n]))
        stores[-1].start()
    for k in range(1, 4):
        sent(k, True, range(PARTS))
    for copy in pending:
        copy.wait_send()
    for store in stores:
        store.wait()


def krylov(sizes, b, eps, screen, x_halo, y_halo, z_halo):
    span_x, span_y, span_z = eps.shape
    tall = span_y + 2 * PAD
    padded = pltpu.VMEM((span_x + 2, 2, tall, LANES), F)
    plain = pltpu.VMEM((span_x, 2, span_y, LANES), F)
    dma = pltpu.SemaphoreType.DMA
    anywhere = pl.BlockSpec(memory_space=pl.ANY)
    most = max(sizes[1], sizes[0] * sizes[2])
    return pl.pallas_call(
        functools.partial(krylov_kernel, sizes),
        out_shape=jax.ShapeDtypeStruct(b.shape, F),
        in_specs=[anywhere] * 6,
        out_specs=anywhere,
        scratch_shapes=[
            padded,
            pltpu.VMEM((span_x + 1, 2, span_y, LANES), F),
            pltpu.VMEM((span_x, 2, tall, LANES), F),
            plain,
            plain,
            plain,
            padded, padded, padded,
            pltpu.VMEM(b.shape, F),
            pltpu.VMEM((6, CHUNK, LANES), F),
            pltpu.VMEM((4, 2, 2, span_x, LANES), F),
            pltpu.VMEM((4, 2, 2, span_x, LANES), F),
            pltpu.VMEM((4, PARTS, span_y, LANES), F),
            pltpu.VMEM((4, 2, PARTS, span_y, LANES), F),
            pltpu.VMEM((PARTS, span_y, LANES), F),
            pltpu.VMEM((2, most, 8, LANES), F),
            dma((8 * PARTS + 4,)),
            dma((4, 2 + 4 * PARTS)),
            dma((4, 2 + 4 * PARTS)),
            dma((2, most)),
            dma((2, most)),
            dma((4,)),
        ],
        compiler_params=pltpu.CompilerParams(
            vmem_limit_bytes=60 << 20, collective_id=0, has_side_effects=True
        ),
        name="krylov",
    )(b, eps, screen, x_halo, y_halo, z_halo)


def per_device(
    atom_charge, atom_fraction, atom_corner, block_count, permittivity, base_potential, ion_access
):
    sizes = tuple(lax.axis_size(axis) for axis in AXES)
    slots = atom_charge.shape[3]
    index, value, live, screen, *halos = deliver(
        sizes,
        atom_charge, atom_fraction, atom_corner, block_count,
        permittivity, base_potential, ion_access,
    )
    sources = spread(index, value, permittivity.shape)
    rows_field = krylov(sizes, sources, permittivity, screen, *halos)
    solution_field, sampled = sample(index, value, rows_field, permittivity.shape)
    returned = give_back(sizes[2], sampled)
    return solution_field, jnp.where(live > 0.0, returned, 0.0).reshape(1, 1, 1, slots)


def solution(mesh):
    in_specs = (
        P("gx", "gy", "gz", None),
        P(None, "gx", "gy", "gz", None),
        P(None, "gx", "gy", "gz", None),
        P("gx", "gy", "gz", None),
        P("gx", "gy", "gz"),
        P("gx", "gy", "gz"),
        P("gx", "gy", "gz"),
    )
    out_specs = (P("gx", "gy", "gz"), P("gx", "gy", "gz", None))
    return jax.shard_map(
        per_device, mesh=mesh, in_specs=in_specs, out_specs=out_specs, check_vma=False
    )
```

```python
import functools

import jax
import jax.numpy as jnp
from jax import lax
from jax.experimental import pallas as pl
from jax.experimental.pallas import tpu as pltpu
from jax.sharding import PartitionSpec as P

F = jnp.float32
AXES = ("gx", "gy", "gz")
STAGES = (("gy",), ("gx", "gz"))
MESH = pl.DeviceIdType.MESH
LANES = 128
PAD = 8
CHUNK = 16
SLOTS_PER_STEP = 128
TABLES = 2
START = 8
PARTS = 4
UNROLL_FACES = 8
UNROLL_APPLY = 16


def patterns():
    row = lax.broadcasted_iota(jnp.int32, (8, LANES), 0)
    lane = lax.broadcasted_iota(jnp.int32, (8, LANES), 1)
    return row, ((row % 2) * LANES + lane).astype(F)


def z_hat(pos, z):
    return jnp.maximum(1.0 - jnp.abs(pos - z), 0.0)


def greet(axis, size):
    barrier, place = pltpu.get_barrier_semaphore(), lax.axis_index(axis)
    for step in range(1, size):
        pl.semaphore_signal(
            barrier, inc=1, device_id={axis: lax.rem(place + step, size)}, device_id_type=MESH
        )
    pl.semaphore_wait(barrier, size - 1)


def inverse_of(value):
    guess = pl.reciprocal(value, approx=True)
    return guess * (2.0 - value * guess)


def plane_of(i, span_x):
    return lax.rem(i + START, span_x)


def pack_columns(first, count, read, lane, chunks, span_x):
    def columns_of(n, accs):
        x = plane_of(first + n, span_x)
        out = []
        for t, acc in zip(chunks, accs):
            low, high = read(x, t)
            ends = jnp.where(lane == 0, low, jnp.where(lane == LANES - 1, high, 0.0))
            out.append(acc + pltpu.roll(ends, 2 * x, 1))
        return tuple(out)

    empty = tuple(jnp.zeros((CHUNK, LANES), F) for _ in chunks)
    return lax.fori_loop(0, count, columns_of, empty, unroll=16)


def deliver_kernel(
    sizes,
    q_ref, f_ref, c_ref, count_ref, eps_ref, pot_ref, ion_ref,
    index_ref, value_ref, live_ref, screen_ref, xh_ref, yh_ref, zh_ref,
    q_out, q_in, f_in, c_in, e, pot, ion, y_send, z_send, zeros,
    sem_in, sem_out, sem_zero, send_sem, recv_sem, halo_send, halo_recv,
):
    span_x, span_y, _ = eps_ref.shape
    size = sizes[2]
    places = [lax.axis_index(axis) for axis in AXES]
    place = places[2]
    capacity = q_out.shape[2]
    lane = lax.broadcasted_iota(jnp.int32, (CHUNK, LANES), 1)
    chunks = range(0, span_y, CHUNK)

    loads, pieces = [], [pl.ds(n * (span_x // 4), span_x // 4) for n in range(4)]
    for half in (0, 1):
        lanes = pl.ds(half * LANES, LANES)
        loads.append(pltpu.make_async_copy(eps_ref.at[:, :, lanes], e.at[:, half], sem_in.at[half]))
    for n, piece in enumerate(pieces):
        for m, (src, dst) in enumerate(((pot_ref, pot), (ion_ref, ion))):
            for half in (0, 1):
                lanes = pl.ds(half * LANES, LANES)
                sem = sem_in.at[2 + 4 * n + 2 * m + half]
                loads.append(pltpu.make_async_copy(src.at[piece, :, lanes], dst.at[piece, half], sem))
    for load in loads:
        load.start()

    barrier = pltpu.get_barrier_semaphore()
    greeted = 0
    for axis, own, count in zip(AXES, places, sizes):
        steps = range(1, count) if axis == "gz" else ((1, count - 1) if count > 1 else ())
        for step in steps:
            pl.semaphore_signal(
                barrier, inc=1, device_id={axis: lax.rem(own + step, count)}, device_id_type=MESH
            )
            greeted += 1

    slot = lax.broadcasted_iota(jnp.int32, (1, capacity), 1)
    for g in range(size):
        block = pl.ds(g * capacity, capacity)
        live = slot < count_ref[0, 0, 0, g]
        live_ref[:, block] = jnp.where(live, 1.0, 0.0)
        q_out[g] = jnp.where(live, q_ref[0, 0, :, block], 0.0)
    for half in (0, 1):
        zeros[half] = jnp.zeros((span_y, LANES), F)
    pl.semaphore_wait(barrier, greeted)

    def copies(step, to, source):
        block = pl.ds(pl.multiple_of(to * capacity, capacity), capacity)
        parts = (
            (q_out.at[to], q_in.at[source]),
            (f_ref.at[:, 0, 0, :, block], f_in.at[source]),
            (c_ref.at[:, 0, 0, :, block], c_in.at[source]),
        )
        return [
            pltpu.make_async_remote_copy(
                src_ref=src,
                dst_ref=dst,
                send_sem=send_sem.at[step, n],
                recv_sem=recv_sem.at[step, n],
                device_id={"gz": to},
                device_id_type=MESH,
            )
            for n, (src, dst) in enumerate(parts)
        ]

    out = []
    for step in range(1, size):
        out.extend(copies(step, lax.rem(place + step, size), place))
    for copy in out:
        copy.start()

    loads[0].wait()
    loads[1].wait()
    halos = []
    for n, (axis, own, count) in enumerate(zip(AXES, places, sizes)):
        for side in (0, 1):
            src = (e.at[span_x - 1 if side == 0 else 0], y_send.at[side], z_send)[n]
            dst = (xh_ref, yh_ref, zh_ref)[n].at[side]
            copy = fill = None
            if count > 1:
                copy = pltpu.make_async_remote_copy(
                    src_ref=src,
                    dst_ref=dst,
                    send_sem=halo_send.at[n, side],
                    recv_sem=halo_recv.at[n, side],
                    device_id={axis: own + 1 if side == 0 else own - 1},
                    device_id_type=MESH,
                )
            above, below = own < count - 1, own > 0
            fill = pltpu.make_async_copy(zeros.at[0] if n == 2 else zeros, dst, sem_zero.at[n, side])
            halos.append((n, above if side == 0 else below, below if side == 0 else above, copy, fill))

    def send(axis):
        for n, has_target, has_source, copy, fill in halos:
            if n == axis:
                if copy is not None:
                    pl.when(has_target)(copy.start)
                pl.when(jnp.logical_not(has_source))(fill.start)

    send(0)

    def rows_of(n, _):
        for m in range(8):
            i = 8 * n + m
            x = plane_of(i, span_x)
            for half in (0, 1):
                y_send[1, half, pl.ds(i, 1), :] = e[x, half, pl.ds(0, 1), :]
                y_send[0, half, pl.ds(i, 1), :] = e[x, half, pl.ds(span_y - 1, 1), :]
        return 0

    lax.fori_loop(0, span_x // 8, rows_of, 0)
    send(1)
    accs = pack_columns(
        0, span_x, lambda x, t: [e[x, half, pl.ds(t, CHUNK), :] for half in (0, 1)], lane, chunks, span_x
    )
    for t, acc in zip(chunks, accs):
        z_send[pl.ds(t, CHUNK), :] = acc
    send(2)

    def screen(x, _):
        for half in (0, 1):
            for t in chunks:
                rows = pl.ds(t, CHUNK)
                up = jnp.exp(pot[x, half, rows, :])
                pot[x, half, rows, :] = ion[x, half, rows, :] * (0.5 * (up + inverse_of(up)))
        return 0

    stores = []
    for n, piece in enumerate(pieces):
        for load in loads[2 + 4 * n:6 + 4 * n]:
            load.wait()
        lax.fori_loop(n * (span_x // 4), (n + 1) * (span_x // 4), screen, 0, unroll=4)
        stores.append(pltpu.make_async_copy(pot.at[piece], screen_ref.at[piece], sem_out.at[n]))
        stores[-1].start()

    def work_out(source, q, f, c):
        block = pl.ds(pl.multiple_of(source * capacity, capacity), capacity)
        index_ref[:, block] = (c[0] * span_y + c[1]) * 2
        value_ref[0, :, block] = c[2].astype(F) + f[2]
        value_ref[1, :, block] = f[1]
        value_ref[2, :, block] = f[0]
        value_ref[3, :, block] = q * (1.0 - f[0])
        value_ref[4, :, block] = q * f[0]

    own_block = pl.ds(pl.multiple_of(place * capacity, capacity), capacity)
    work_out(
        place,
        q_out[place],
        [f_ref[k, 0, 0, :, own_block] for k in range(3)],
        [c_ref[k, 0, 0, :, own_block] for k in range(3)],
    )
    for step in range(1, size):
        source = lax.rem(place + size - step, size)
        for copy in copies(step, lax.rem(place + step, size), source):
            copy.wait_recv()
        work_out(
            source,
            q_in[source],
            [f_in[source, k] for k in range(3)],
            [c_in[source, k] for k in range(3)],
        )
    for _, has_target, has_source, copy, fill in halos:
        if copy is not None:
            pl.when(has_source)(copy.wait_recv)
            pl.when(has_target)(copy.wait_send)
        pl.when(jnp.logical_not(has_source))(fill.wait)
    for copy in out:
        copy.wait_send()
    for store in stores:
        store.wait()


def deliver(sizes, charge, fraction, corner, count, eps, pot, ion):
    size = sizes[2]
    capacity = charge.shape[3] // size
    span_x, span_y, _ = eps.shape
    vmem, anywhere = pl.BlockSpec(memory_space=pltpu.VMEM), pl.BlockSpec(memory_space=pl.ANY)
    dma = pltpu.SemaphoreType.DMA
    plain = (span_x, 2, span_y, LANES)
    return pl.pallas_call(
        functools.partial(deliver_kernel, sizes),
        out_shape=(
            jax.ShapeDtypeStruct((1, size * capacity), jnp.int32),
            jax.ShapeDtypeStruct((5, 1, size * capacity), F),
            jax.ShapeDtypeStruct((1, size * capacity), F),
            jax.ShapeDtypeStruct(plain, F),
            jax.ShapeDtypeStruct((2, 2, span_y, LANES), F),
            jax.ShapeDtypeStruct((2, 2, span_x, LANES), F),
            jax.ShapeDtypeStruct((2, span_y, LANES), F),
        ),
        in_specs=[vmem, vmem, vmem, pl.BlockSpec(memory_space=pltpu.SMEM)] + [anywhere] * 3,
        out_specs=(vmem,) * 3 + (anywhere,) * 4,
        scratch_shapes=[
            pltpu.VMEM((size, 1, capacity), F),
            pltpu.VMEM((size, 1, capacity), F),
            pltpu.VMEM((size, 3, 1, capacity), F),
            pltpu.VMEM((size, 3, 1, capacity), jnp.int32),
            pltpu.VMEM(plain, F),
            pltpu.VMEM(plain, F),
            pltpu.VMEM(plain, F),
            pltpu.VMEM((2, 2, span_x, LANES), F),
            pltpu.VMEM((span_y, LANES), F),
            pltpu.VMEM((2, span_y, LANES), F),
            dma((18,)),
            dma((4,)),
            dma((3, 2)),
            dma((size, 3)),
            dma((size, 3)),
            dma((3, 2)),
            dma((3, 2)),
        ],
        compiler_params=pltpu.CompilerParams(
            vmem_limit_bytes=60 << 20, collective_id=1, has_side_effects=True
        ),
        name="deliver",
    )(charge, fraction, corner, count, eps, pot, ion)


def give_back_kernel(size, sampled_ref, out_ref, came, send_sem, recv_sem):
    place = lax.axis_index("gz")
    capacity = came.shape[2]
    greet("gz", size)

    def copy_of(step, to, source):
        block = pl.ds(pl.multiple_of(to * capacity, capacity), capacity)
        return pltpu.make_async_remote_copy(
            src_ref=sampled_ref.at[:, block],
            dst_ref=came.at[source],
            send_sem=send_sem.at[step],
            recv_sem=recv_sem.at[step],
            device_id={"gz": to},
            device_id_type=MESH,
        )

    out = [copy_of(step, lax.rem(place + step, size), place) for step in range(1, size)]
    for copy in out:
        copy.start()

    def put(source, values):
        block = pl.ds(pl.multiple_of(source * capacity, capacity), capacity)
        out_ref[:, block] = values

    put(place, sampled_ref[:, pl.ds(pl.multiple_of(place * capacity, capacity), capacity)])
    for step in range(1, size):
        source = lax.rem(place + size - step, size)
        copy_of(step, lax.rem(place + step, size), source).wait_recv()
        put(source, came[source])
    for copy in out:
        copy.wait_send()


def give_back(size, sampled):
    slots = sampled.shape[1]
    vmem = pl.BlockSpec(memory_space=pltpu.VMEM)
    dma = pltpu.SemaphoreType.DMA
    return pl.pallas_call(
        functools.partial(give_back_kernel, size),
        out_shape=jax.ShapeDtypeStruct((1, slots), F),
        in_specs=[vmem],
        out_specs=vmem,
        scratch_shapes=[pltpu.VMEM((size, 1, slots // size), F), dma((size,)), dma((size,))],
        compiler_params=pltpu.CompilerParams(collective_id=2, has_side_effects=True),
        name="give_back",
    )(sampled)


def spread_kernel(span_y, index_ref, value_ref, out_ref, *scratch):
    tables, sem = scratch[:TABLES], scratch[TABLES]
    rows = out_ref.shape[0]
    block = 128

    def clear(i, _):
        for table in tables:
            table[pl.ds(pl.multiple_of(i * block, block), block), :] = jnp.zeros((block, LANES), F)
        return 0

    lax.fori_loop(0, rows // block, clear, 0)
    for table in tables:
        table[pl.ds(rows, 8), :] = jnp.zeros((8, LANES), F)
    row, pos = patterns()
    ya = jnp.where(row < 2, 1.0, 0.0).astype(F)
    yb = jnp.where(row < 2, -1.0, jnp.where(row < 4, 1.0, 0.0)).astype(F)
    plane = 2 * span_y

    steps = index_ref.shape[1] // SLOTS_PER_STEP

    def body(i, _):
        for first in range(0, SLOTS_PER_STEP, TABLES):
            items = []
            for which, table in enumerate(tables):
                s = i * SLOTS_PER_STEP + (first + which)
                r = pl.multiple_of(index_ref[0, s], 2)
                w = (ya + yb * value_ref[1, 0, s]) * z_hat(pos, value_ref[0, 0, s])
                near = table[pl.ds(r, 8), :] + w * value_ref[3, 0, s]
                far = table[pl.ds(r + plane, 8), :] + w * value_ref[4, 0, s]
                items.append((table, r, near, far))
            for table, r, near, far in items:
                table[pl.ds(r, 8), :] = near
                table[pl.ds(r + plane, 8), :] = far
        return 0

    lax.fori_loop(0, steps, body, 0)

    def combine(i, _):
        part = pl.ds(pl.multiple_of(i * block, block), block)
        total = tables[0][part, :]
        for table in tables[1:]:
            total = total + table[part, :]
        tables[0][part, :] = total
        return 0

    pieces, copies = rows // block // 4, []
    for n in range(4):
        lax.fori_loop(n * pieces, (n + 1) * pieces, combine, 0, unroll=2)
        part = pl.ds(n * pieces * block, pieces * block)
        copies.append(pltpu.make_async_copy(tables[0].at[part, :], out_ref.at[part, :], sem.at[n]))
        copies[-1].start()
    for copy in copies:
        copy.wait()


def spread(index, value, span):
    rows = span[0] * span[1] * 2
    return pl.pallas_call(
        functools.partial(spread_kernel, span[1]),
        out_shape=jax.ShapeDtypeStruct((rows, LANES), F),
        in_specs=[pl.BlockSpec(memory_space=pltpu.SMEM)] * 2,
        out_specs=pl.BlockSpec(memory_space=pl.ANY),
        scratch_shapes=[pltpu.VMEM((rows + 8, LANES), F)] * TABLES + [pltpu.SemaphoreType.DMA((4,))],
        compiler_params=pltpu.CompilerParams(vmem_limit_bytes=60 << 20),
        name="spread",
    )(index, value)


def sample_kernel(
    span_y, index_ref, value_ref, rows_ref, field_ref, out_ref, table, grid, parts, sums, sems
):
    rows = rows_ref.shape[0]
    load = pltpu.make_async_copy(rows_ref, table.at[pl.ds(8, rows), :], sems.at[1])
    load.start()
    table[pl.ds(0, 8), :] = jnp.zeros((8, LANES), F)
    table[pl.ds(rows + 8, 8), :] = jnp.zeros((8, LANES), F)
    load.wait()
    row, pos = patterns()
    first_row, second_row = row % 4 < 2, row < 4
    yb = jnp.where(first_row, -1.0, 1.0).astype(F)
    ya = jnp.where(first_row, 1.0, 0.0).astype(F)
    masks = [jnp.where(second_row, 1.0, 0.0).astype(F), jnp.where(second_row, 0.0, 1.0).astype(F)]
    weights = [(ya * mask, yb * mask) for mask in masks]
    plane = 2 * span_y
    span_x = grid.shape[0]
    turn = span_x // (index_ref.shape[1] // SLOTS_PER_STEP)
    halves = [pl.ds(n * (span_x // 2), span_x // 2) for n in (0, 1)]
    keeps = [pltpu.make_async_copy(grid.at[h], field_ref.at[h], sems.at[2 * n]) for n, h in enumerate(halves)]

    steps = index_ref.shape[1] // SLOTS_PER_STEP

    def body(i, _):
        for pair in range(SLOTS_PER_STEP // 2):
            total = None
            for which in (0, 1):
                s = i * SLOTS_PER_STEP + (2 * pair + which)
                r = pl.multiple_of(index_ref[0, s], 2) + (8 - 4 * which)
                wa, wb = weights[which]
                w = (wa + wb * value_ref[1, 0, s]) * z_hat(pos, value_ref[0, 0, s])
                near, far = table[pl.ds(r, 8), :], table[pl.ds(r + plane, 8), :]
                term = w * (near + value_ref[2, 0, s] * (far - near))
                total = term if total is None else total + term
            start = i * (SLOTS_PER_STEP // 2) + pair
            parts[pl.ds(pl.multiple_of(start * 8, 8), 8), :] = total

        for n in range(turn):
            x = i * turn + n
            for half in (0, 1):
                for t in range(0, span_y, CHUNK):
                    place = pl.ds(8 + x * plane + 2 * t + half, CHUNK, stride=2)
                    grid[x, pl.ds(t, CHUNK), half * LANES:(half + 1) * LANES] = table[place, :]

        @pl.when(i == steps // 2)
        def _():
            keeps[0].start()

        return 0

    lax.fori_loop(0, steps, body, 0)
    keeps[1].start()

    def fold(i, _):
        start = pl.multiple_of(i * 256, 256)
        total = parts[pl.ds(start, 64, stride=4), :]
        for j in range(1, 4):
            total = total + parts[pl.ds(start + j, 64, stride=4), :]
        sums[pl.ds(pl.multiple_of(i * 64, 64), 64), :] = total
        return 0

    lax.fori_loop(0, sums.shape[0] // 64, fold, 0)
    out_ref[...] = lax.dot_general(
        jnp.ones((8, LANES), F),
        sums[...],
        (((1,), (1,)), ((), ())),
        precision=lax.Precision.HIGHEST,
        preferred_element_type=F,
    )[0:1]
    for keep in keeps:
        keep.wait()


def sample(index, value, rows_field, span):
    span_y, rows = span[1], rows_field.shape[0]
    slots = index.shape[1]
    smem, anywhere = pl.BlockSpec(memory_space=pltpu.SMEM), pl.BlockSpec(memory_space=pl.ANY)
    return pl.pallas_call(
        functools.partial(sample_kernel, span_y),
        out_shape=(
            jax.ShapeDtypeStruct(span, F),
            jax.ShapeDtypeStruct((1, slots), F),
        ),
        in_specs=[smem, smem, anywhere],
        out_specs=(anywhere, pl.BlockSpec(memory_space=pltpu.VMEM)),
        scratch_shapes=[
            pltpu.VMEM((rows + 16, LANES), F),
            pltpu.VMEM(span, F),
            pltpu.VMEM((slots * 4, LANES), F),
            pltpu.VMEM((slots, LANES), F),
            pltpu.SemaphoreType.DMA((3,)),
        ],
        compiler_params=pltpu.CompilerParams(vmem_limit_bytes=60 << 20),
        name="sample",
    )(index, value, rows_field)


def harmonic(former, latter):
    return (2.0 * former * latter) * inverse_of(former + latter)


def stage_of(axes, sizes, places):
    number, count = 0, 1
    for axis in axes:
        number = number * sizes[axis] + places[axis]
        count *= sizes[axis]
    others = []

    def hops(step):
        total = 0
        for axis in reversed(axes):
            move, step = step % sizes[axis], step // sizes[axis]
            total += min(move, sizes[axis] - move)
        return total

    for step in sorted(range(1, count), key=hops, reverse=True):
        target, source, source_number, rest = {}, {}, 0, step
        moves = {}
        for axis in reversed(axes):
            moves[axis], rest = rest % sizes[axis], rest // sizes[axis]
        for axis in axes:
            size, move = sizes[axis], moves[axis]
            if move:
                target[axis] = lax.rem(places[axis] + move, size)
                source[axis] = lax.rem(places[axis] + size - move, size)
            source_number = source_number * size + source.get(axis, places[axis])
        others.append((target, source, source_number))
    return number, others


def krylov_kernel(
    sizes,
    b_ref, eps_ref, screen_ref, xh_ref, yh_ref, zh_ref,
    rows_ref,
    e, fx, fy, fz, fzm, rd, v0, v1, v2, b, sums,
    y_send, y_recv, z_send, z_recv, z_in, red,
    sem_in, send_sem, recv_sem, red_send, red_recv, sem_out,
):
    span_x, span_y, _ = eps_ref.shape
    places = [lax.axis_index(axis) for axis in AXES]
    lane = lax.broadcasted_iota(jnp.int32, (CHUNK, LANES), 1)
    at_first, at_last, odd = lane == 0, lane == LANES - 1, lane % 2 == 1
    chunks = range(0, span_y, CHUNK)
    body_rows = pl.ds(PAD, span_y)
    fields = (e, v0, v1, v2)
    part = span_x // PARTS

    def load_planes(src, dst, number, first, count, shift):
        out = []
        for start, many in ((first, min(count, span_x - first)), (0, count - min(count, span_x - first))):
            if many:
                out.append((src(start, many), dst(start + shift, many)))
        return [pltpu.make_async_copy(a, b, sem_in.at[number + n]) for n, (a, b) in enumerate(out)]

    tall = 2 * span_y
    loads = []
    for which in range(PARTS):
        group, base = [], 8 * which
        last = which == PARTS - 1
        for half in (0, 1):
            group += load_planes(
                lambda a, m: eps_ref.at[pl.ds(a, m), :, pl.ds(half * LANES, LANES)],
                lambda a, m: e.at[pl.ds(a, m), half, body_rows, :],
                base + 2 * half,
                START - 1 if which == 0 else START + part * which + 1,
                part + (2 if which == 0 else -2 if last else 0),
                1,
            )
        group += load_planes(
            lambda a, m: screen_ref.at[pl.ds(a, m)],
            lambda a, m: rd.at[pl.ds(a, m)],
            base + 4,
            START + part * which,
            part,
            0,
        )
        group += load_planes(
            lambda a, m: b_ref.at[pl.ds(a * tall, m * tall), :],
            lambda a, m: b.at[pl.ds(a * tall, m * tall), :],
            base + 6,
            START + part * which,
            part,
            0,
        )
        if which == 0:
            group.append(pltpu.make_async_copy(yh_ref, y_recv.at[0], sem_in.at[8 * PARTS]))
            group.append(pltpu.make_async_copy(zh_ref, z_recv.at[0, :, 0], sem_in.at[8 * PARTS + 1]))
            for side in (0, 1):
                x = span_x + 1 if side else 0
                group.append(
                    pltpu.make_async_copy(xh_ref.at[side], e.at[x, :, body_rows, :], sem_in.at[8 * PARTS + 2 + side])
                )
        loads.append(group)
    for group in loads:
        for load in group:
            load.start()

    zero = jnp.zeros((span_y, LANES), F)
    for field in (v0, v1, v2):
        for half in (0, 1):
            for x in (0, span_x + 1):
                field[x, half, body_rows, :] = zero
    for k in range(1, 4):
        for side in (0, 1):
            for which in range(PARTS):
                z_recv[k, side, which] = zero
            for half in (0, 1):
                y_recv[k, side, half] = jnp.zeros((span_x, LANES), F)

    barrier = pltpu.get_barrier_semaphore()
    stages = [stage_of(axes, dict(zip(AXES, sizes)), dict(zip(AXES, places))) for axes in STAGES]
    for _, others in stages:
        for target, _, _ in others:
            pl.semaphore_signal(barrier, inc=1, device_id=target, device_id_type=MESH)

    def halo_copies(k, x_faces, parts):
        pairs, field = [], fields[k]
        for n, (axis, place, size) in enumerate(zip(AXES, places, sizes)):
            if size == 1:
                continue
            for side in ((1,) if k == 3 else (0, 1)):
                ends = []
                if n == 0 and x_faces:
                    src = field.at[span_x if side == 0 else 1, :, body_rows, :]
                    ends.append((0, src, field.at[0 if side == 0 else span_x + 1, :, body_rows, :]))
                if n == 1:
                    for which in parts:
                        rows = pl.ds(pl.multiple_of(which * part, 8), part)
                        src = y_send.at[k, side, :, rows, :]
                        ends.append((1 + which, src, y_recv.at[k, side, :, rows, :]))
                if n == 2:
                    for which in parts:
                        ends.append((1 + PARTS + which, z_send.at[k, which], z_recv.at[k, side, which]))
                for kind, src, dst in ends:
                    copy = pltpu.make_async_remote_copy(
                        src_ref=src,
                        dst_ref=dst,
                        send_sem=send_sem.at[k, 2 * kind + side],
                        recv_sem=recv_sem.at[k, 2 * kind + side],
                        device_id={axis: place + 1 if side == 0 else place - 1},
                        device_id_type=MESH,
                    )
                    above, below = place < size - 1, place > 0
                    pairs.append((above if side == 0 else below, below if side == 0 else above, copy))
        return pairs

    def send(*exchange):
        for has_target, _, copy in halo_copies(*exchange):
            pl.when(has_target)(copy.start)

    def receive(*exchange):
        for _, has_source, copy in halo_copies(*exchange):
            pl.when(has_source)(copy.wait_recv)

    def sent(*exchange):
        for has_target, _, copy in halo_copies(*exchange):
            pl.when(has_target)(copy.wait_send)

    def eight(body, first):
        for n in range(8):
            body(first + n, 0)
        return 0

    def pack(k, which):
        field = fields[k]

        def rows_of(i, _):
            x = plane_of(i, span_x)
            for half in (0, 1):
                y_send[k, 1, half, pl.ds(i, 1), :] = field[x + 1, half, pl.ds(PAD, 1), :]
                y_send[k, 0, half, pl.ds(i, 1), :] = field[
                    x + 1, half, pl.ds(PAD + span_y - 1, 1), :
                ]
            return 0

        first = which * part
        lax.fori_loop(0, part // 8, lambda n, c: eight(rows_of, first + 8 * n), 0)
        accs = pack_columns(
            first,
            part,
            lambda x, t: [field[x + 1, half, pl.ds(PAD + t, CHUNK), :] for half in (0, 1)],
            lane,
            chunks,
            span_x,
        )
        for t, acc in zip(chunks, accs):
            z_send[k, which, pl.ds(t, CHUNK), :] = acc

    def unpack(k, which):
        field = fields[k]

        def rows_of(i, _):
            x = plane_of(i, span_x)
            for half in (0, 1):
                field[x + 1, half, pl.ds(PAD - 1, 1), :] = y_recv[k, 0, half, pl.ds(i, 1), :]
                field[x + 1, half, pl.ds(PAD + span_y, 1), :] = y_recv[k, 1, half, pl.ds(i, 1), :]
            return 0

        first = which * part
        lax.fori_loop(0, part // 8, lambda n, c: eight(rows_of, first + 8 * n), 0)
        for t in chunks:
            rows = pl.ds(t, CHUNK)
            held = which if k > 0 else 0
            low = pltpu.roll(z_recv[k, 0, held, rows, :], 2, 1)
            z_in[which, rows, :] = jnp.where(odd, low, z_recv[k, 1, held, rows, :])

    def z_neighbours(center, outer):
        after = [pltpu.roll(c, LANES - 1, 1) for c in center]
        before = [pltpu.roll(c, 1, 1) for c in center]
        after = [jnp.where(at_last, after[1], after[0]), jnp.where(at_last, outer, after[1])]
        before = [jnp.where(at_first, outer, before[0]), jnp.where(at_first, before[0], before[1])]
        return after, before

    def outer_z(which, t, x):
        return pltpu.roll(z_in[which, pl.ds(t, CHUNK), :], LANES - 1 - 2 * x, 1)

    def both_parts(body, carry, before, after, unroll):
        def one(which, carry):
            before(which)
            carry = lax.fori_loop(
                0, part, lambda n, c: body(which, which * part + n, c), carry, unroll=unroll
            )
            after(which)
            return carry

        return lax.fori_loop(0, PARTS, one, carry)

    def x_face(x):
        for half in (0, 1):
            for t in chunks:
                rows = pl.ds(PAD + t, CHUNK)
                fx[x, half, pl.ds(t, CHUNK), :] = harmonic(e[x, half, rows, :], e[x + 1, half, rows, :])

    def faces(which, i, total):
        x = plane_of(i, span_x)
        for half in (0, 1):
            fy[x, half, pl.ds(PAD - 1, 1), :] = harmonic(
                e[x + 1, half, pl.ds(PAD - 1, 1), :], e[x + 1, half, pl.ds(PAD, 1), :]
            )
        for t in chunks:
            rows, wide = pl.ds(t, CHUNK), pl.ds(PAD + t, CHUNK)
            center = [e[x + 1, half, wide, :] for half in (0, 1)]
            after, before = z_neighbours(center, outer_z(which, t, x))
            for half in (0, 1):
                c = center[half]
                x_next = harmonic(c, e[x + 2, half, wide, :])
                fx[x + 1, half, rows, :] = x_next
                y_next = harmonic(c, e[x + 1, half, pl.ds(PAD + t + 1, CHUNK), :])
                fy[x, half, wide, :] = y_next
                z_next, z_last = harmonic(c, after[half]), harmonic(c, before[half])
                fz[x, half, rows, :] = z_next
                fzm[x, half, rows, :] = z_last
                diagonal = (
                    x_next + fx[x, half, rows, :]
                    + y_next + fy[x, half, pl.ds(PAD + t - 1, CHUNK), :]
                    + z_next + z_last + rd[x, half, rows, :]
                )
                inverse = inverse_of(diagonal)
                rd[x, half, rows, :] = inverse
                source = b[pl.ds(x * (2 * span_y) + 2 * t + half, CHUNK, stride=2), :]
                value = source * inverse
                v0[x + 1, half, wide, :] = value
                total = total + source * value
        return total

    def ready(k):
        def before(which):
            @pl.when(which == PARTS - 1)
            def _():
                receive(k, True, ())

            receive(k, False, (which,))
            unpack(k, which)

        return before

    def ready_faces(which):
        for n in range(PARTS):

            @pl.when(which == n)
            def _(n=n):
                for load in loads[n]:
                    load.wait()

        unpack(0, which)
        for n, x in ((0, START), (PARTS - 1, 0)):

            @pl.when(which == n)
            def _(x=x):
                x_face(x)

    def done(k):
        def after(which):
            if k == 1:

                @pl.when(which == 0)
                def _():
                    pl.semaphore_wait(barrier, sum(len(others) for _, others in stages))

            @pl.when(which == PARTS - 1)
            def _():
                send(k, True, ())

            pack(k, which)
            send(k, False, (which,))

        return after

    nothing = jnp.zeros((CHUNK, LANES), F)
    sums[0] = both_parts(faces, nothing, ready_faces, done(1), UNROLL_FACES)

    def stencil(k):
        v, result = fields[k], fields[k + 1]

        def apply(which, i, carry):
            first, second = carry
            x = plane_of(i, span_x)
            for t in chunks:
                rows, wide = pl.ds(t, CHUNK), pl.ds(PAD + t, CHUNK)
                up, down = pl.ds(PAD + t + 1, CHUNK), pl.ds(PAD + t - 1, CHUNK)
                center = [v[x + 1, half, wide, :] for half in (0, 1)]
                after, before = z_neighbours(center, outer_z(which, t, x))
                for half in (0, 1):
                    image = (
                        fx[x + 1, half, rows, :] * v[x + 2, half, wide, :]
                        + fx[x, half, rows, :] * v[x, half, wide, :]
                        + fy[x, half, wide, :] * v[x + 1, half, up, :]
                        + fy[x, half, down, :] * v[x + 1, half, down, :]
                        + fz[x, half, rows, :] * after[half]
                        + fzm[x, half, rows, :] * before[half]
                    )
                    value = image * rd[x, half, rows, :]
                    result[x + 1, half, wide, :] = value
                    first = first + center[half] * image
                    second = second + image * value
            return first, second

        first, second = both_parts(apply, (nothing, nothing), ready(k), done(k + 1), UNROLL_APPLY)
        sums[2 * k - 1] = first
        sums[2 * k] = second

    stencil(1)
    stencil(2)

    def product(which, i, total):
        x = plane_of(i, span_x)
        for t in chunks:
            rows, wide = pl.ds(t, CHUNK), pl.ds(PAD + t, CHUNK)
            center = [v2[x + 1, half, wide, :] for half in (0, 1)]
            after = [pltpu.roll(c, LANES - 1, 1) for c in center]
            after = [
                jnp.where(at_last, after[1], after[0]),
                jnp.where(at_last, outer_z(which, t, x), after[1]),
            ]
            for half in (0, 1):
                image = (
                    fx[x + 1, half, rows, :] * v2[x + 2, half, wide, :]
                    + fy[x, half, wide, :] * v2[x + 1, half, pl.ds(PAD + t + 1, CHUNK), :]
                    + fz[x, half, rows, :] * after[half]
                )
                total = total + center[half] * image
        return total

    sums[5] = 2.0 * both_parts(product, nothing, ready(3), lambda which: None, UNROLL_APPLY)

    row = lax.broadcasted_iota(jnp.int32, (8, LANES), 0)
    mine = jnp.zeros((8, LANES), F)
    for n in range(6):
        folded = jnp.sum(sums[n], axis=0, keepdims=True)
        mine = mine + jnp.where(row == n, folded, 0.0)
    pending = []
    for n, (number, others) in enumerate(stages):
        red[n, number] = mine

        def copy_of(step, device, slot, n=n, number=number):
            return pltpu.make_async_remote_copy(
                src_ref=red.at[n, number],
                dst_ref=red.at[n, slot],
                send_sem=red_send.at[n, step],
                recv_sem=red_recv.at[n, step],
                device_id=device,
                device_id_type=MESH,
            )

        copies = [copy_of(step, target, number) for step, (target, _, _) in enumerate(others)]
        for copy in copies:
            copy.start()
        for step, (_, source, slot) in enumerate(others):
            copy_of(step, source, slot).wait_recv()
        pending.extend(copies)
        mine = red[n, 0]
        for other in range(1, len(others) + 1):
            mine = mine + red[n, other]
    totals = jnp.sum(mine, axis=1, keepdims=True)
    m = [totals[n:n + 1] for n in range(6)]
    m = [value / m[0] for value in m]

    h = [m[n] - m[n + 1] for n in range(5)]
    l1, l2 = h[1] / h[0], h[2] / h[0]
    d1 = h[2] - l1 * h[1]
    o1 = h[3] - l1 * h[2]
    l3 = o1 / d1
    d2 = h[4] - l2 * h[2] - l3 * o1
    r1 = m[1] - l1 * m[0]
    r2 = m[2] - l2 * m[0] - l3 * r1
    c2 = r2 / d2
    c1 = r1 / d1 - l3 * c2
    c0 = m[0] / h[0] - l1 * c1 - l2 * c2

    weights = [jnp.broadcast_to(c, (CHUNK, LANES)) for c in (c0, c1, c2)]

    def finish(x, _):
        for half in (0, 1):
            for t in chunks:
                wide = pl.ds(PAD + t, CHUNK)
                value = weights[0] * v0[x + 1, half, wide, :]
                value = value + weights[1] * v1[x + 1, half, wide, :]
                value = value + weights[2] * v2[x + 1, half, wide, :]
                b[pl.ds(x * (2 * span_y) + 2 * t + half, CHUNK, stride=2), :] = value
        return 0

    stores, some = [], span_x // 4
    for n in range(4):
        lax.fori_loop(n * some, (n + 1) * some, finish, 0, unroll=2)
        rows = pl.ds(n * some * tall, some * tall)
        stores.append(pltpu.make_async_copy(b.at[rows, :], rows_ref.at[rows, :], sem_out.at[n]))
        stores[-1].start()
    for k in range(1, 4):
        sent(k, True, range(PARTS))
    for copy in pending:
        copy.wait_send()
    for store in stores:
        store.wait()


def krylov(sizes, b, eps, screen, x_halo, y_halo, z_halo):
    span_x, span_y, span_z = eps.shape
    tall = span_y + 2 * PAD
    padded = pltpu.VMEM((span_x + 2, 2, tall, LANES), F)
    plain = pltpu.VMEM((span_x, 2, span_y, LANES), F)
    dma = pltpu.SemaphoreType.DMA
    anywhere = pl.BlockSpec(memory_space=pl.ANY)
    most = max(sizes[1], sizes[0] * sizes[2])
    return pl.pallas_call(
        functools.partial(krylov_kernel, sizes),
        out_shape=jax.ShapeDtypeStruct(b.shape, F),
        in_specs=[anywhere] * 6,
        out_specs=anywhere,
        scratch_shapes=[
            padded,
            pltpu.VMEM((span_x + 1, 2, span_y, LANES), F),
            pltpu.VMEM((span_x, 2, tall, LANES), F),
            plain,
            plain,
            plain,
            padded, padded, padded,
            pltpu.VMEM(b.shape, F),
            pltpu.VMEM((6, CHUNK, LANES), F),
            pltpu.VMEM((4, 2, 2, span_x, LANES), F),
            pltpu.VMEM((4, 2, 2, span_x, LANES), F),
            pltpu.VMEM((4, PARTS, span_y, LANES), F),
            pltpu.VMEM((4, 2, PARTS, span_y, LANES), F),
            pltpu.VMEM((PARTS, span_y, LANES), F),
            pltpu.VMEM((2, most, 8, LANES), F),
            dma((8 * PARTS + 4,)),
            dma((4, 2 + 4 * PARTS)),
            dma((4, 2 + 4 * PARTS)),
            dma((2, most)),
            dma((2, most)),
            dma((4,)),
        ],
        compiler_params=pltpu.CompilerParams(
            vmem_limit_bytes=60 << 20, collective_id=0, has_side_effects=True
        ),
        name="krylov",
    )(b, eps, screen, x_halo, y_halo, z_halo)


def per_device(
    atom_charge, atom_fraction, atom_corner, block_count, permittivity, base_potential, ion_access
):
    sizes = tuple(lax.axis_size(axis) for axis in AXES)
    slots = atom_charge.shape[3]
    index, value, live, screen, *halos = deliver(
        sizes,
        atom_charge, atom_fraction, atom_corner, block_count,
        permittivity, base_potential, ion_access,
    )
    sources = spread(index, value, permittivity.shape)
    rows_field = krylov(sizes, sources, permittivity, screen, *halos)
    solution_field, sampled = sample(index, value, rows_field, permittivity.shape)
    returned = give_back(sizes[2], sampled)
    return solution_field, jnp.where(live > 0.0, returned, 0.0).reshape(1, 1, 1, slots)


def solution(mesh):
    in_specs = (
        P("gx", "gy", "gz", None),
        P(None, "gx", "gy", "gz", None),
        P(None, "gx", "gy", "gz", None),
        P("gx", "gy", "gz", None),
        P("gx", "gy", "gz"),
        P("gx", "gy", "gz"),
        P("gx", "gy", "gz"),
    )
    out_specs = (P("gx", "gy", "gz"), P("gx", "gy", "gz", None))
    return jax.shard_map(
        per_device, mesh=mesh, in_specs=in_specs, out_specs=out_specs, check_vma=False
    )
```
